256 devices in a mesh: seq: 32 (over x, y, core), chan: 8 (over z).
Axes of the slice: x: 4, y: 4, z: 8, core: 2. Of those that a mesh axis runs over, the one named last changes fastest.
Arguments:
- query_act: bfloat16 [16384, 1024], P('seq', 'chan'), may hold values from -6 to 6
- key_act: bfloat16 [16384, 1024], P('seq', 'chan'), may hold values from -6 to 6
- value_act: bfloat16 [16384, 1024], P('seq', 'chan'), may hold values from -6 to 6
- out_grad: bfloat16 [16384, 1024], P('seq', 'chan'), may hold values from -6 to 6
- filter_in: float32 [16, 64], replicated, may hold values from -1.5 to 1.5
- filter_mid: float32 [64, 64], replicated, may hold values from -0.75 to 0.75
- filter_out: float32 [64, 1024], P(None, 'chan'), may hold values from -0.75 to 0.75
- decay_rate: float32 [1024], P('chan'), may hold values from 1.5258789e-05 to 0.0333333333
- skip_gain: float32 [1024], P('chan'), may hold values from -4 to 4
Outputs:
- output: bfloat16 [16384, 1024], P('seq', 'chan')
- grad_query: bfloat16 [16384, 1024], P('seq', 'chan')
- grad_key: bfloat16 [16384, 1024], P('seq', 'chan')
- grad_value: bfloat16 [16384, 1024], P('seq', 'chan')
- grad_filter_in: float32 [16, 64], replicated
- grad_filter_mid: float32 [64, 64], replicated
- grad_filter_out: float32 [64, 1024], P(None, 'chan')
- grad_decay: float32 [1024], P('chan')
- grad_skip: float32 [1024], P('chan')
The draws below stay inside these ranges and needn't reach their ends.
All inputs are finite; a program needn't handle non-finite values.
Results may differ from the reference program's by a relative error of at most 0.0014.
Values sent between devices are 32-bit elements; how exact they have to be, the bound alone decides.
No kernel may reach another device: no remote copies, remote signals or barrier semaphores. Data moves between devices by JAX's collectives and lax.ppermute only.
A program may use at most 128 MiB of HBM per device.

```python
import math
import jax
import jax.numpy as jnp
from jax import lax

ORDER = 64
EMB = 16
LENGTH = 16384
CHANNELS = 1024


def draw_decay_rate(key, part):
    key = jax.random.fold_in(key, 7)
    pick_key, slow_key, fast_key = jax.random.split(key, 3)
    share = 0.5
    is_slow = jax.random.uniform(pick_key, (CHANNELS,), dtype=jnp.float32) < share
    slow_rate = jnp.exp(jax.random.uniform(slow_key, (CHANNELS,), dtype=jnp.float32, minval=math.log(0.25), maxval=math.log(2.0))) / LENGTH
    fast_rate = jnp.exp(jax.random.uniform(fast_key, (CHANNELS,), dtype=jnp.float32, minval=math.log(2.0 / LENGTH), maxval=math.log(1.0 / 30.0)))
    return jnp.where(is_slow, slow_rate, fast_rate).astype(jnp.float32)


def block_scale(stream_key, dims, cuts, smallest, largest):
    loudness, own = 1.0, jax.random.fold_in(stream_key, 6)
    for dim, parts in cuts:
        draws = jnp.exp(jax.random.uniform(jax.random.fold_in(own, dim), (parts,), jnp.float32, smallest / len(cuts), largest / len(cuts)))
        loudness = loudness * jnp.repeat(draws, dims[dim] // parts).reshape([-1 if axis == dim else 1 for axis in range(len(dims))])
    return loudness


def normal_values(stream_key, dims, spread, reach, shards=(), held_as=jnp.bfloat16):
    result = spread * jax.random.normal(stream_key, dims, jnp.float32)
    if shards:
        result = result * block_scale(stream_key, dims, shards, -0.22, 0.18)
    return jnp.clip(result, -reach, reach).astype(held_as)


def setup_inputs(seed: int = 0) -> dict:
    key_of = jax.random.split(jax.random.key(seed), 10)
    return {
        "query_act": normal_values(key_of[0], (LENGTH, CHANNELS), 1.0, 6.0, ((0, 32), (1, 8))),
        "key_act": normal_values(key_of[1], (LENGTH, CHANNELS), 1.0, 6.0, ((0, 32), (1, 8))),
        "value_act": normal_values(key_of[2], (LENGTH, CHANNELS), 1.0, 6.0, ((0, 32), (1, 8))),
        "out_grad": normal_values(key_of[3], (LENGTH, CHANNELS), 1.0, 6.0, ((0, 32), (1, 8))),
        "filter_in": normal_values(key_of[4], (EMB, ORDER), EMB ** -0.5, 1.5, (), jnp.float32),
        "filter_mid": normal_values(key_of[5], (ORDER, ORDER), ORDER ** -0.5, 0.75, (), jnp.float32),
        "filter_out": normal_values(key_of[6], (ORDER, CHANNELS), ORDER ** -0.5, 0.75, ((1, 8),), jnp.float32),
        "decay_rate": draw_decay_rate(jax.random.fold_in(key_of[9], 71), 0),
        "skip_gain": normal_values(key_of[8], (CHANNELS,), 1.0, 4.0, ((0, 8),), jnp.float32),
    }


def positional_features(positions, seq_total):
    ramp_col = positions.astype(jnp.float32) / seq_total
    sine_cols = []
    cosine_cols = []
    for level_id in range(7):
        factor = max(1, seq_total // 4 // 4 ** (6 - level_id))
        turns = factor * (positions % (seq_total // factor))
        phase = turns.astype(jnp.float32) * (2.0 * math.pi / seq_total)
        sine_cols.append(jnp.sin(phase))
        cosine_cols.append(jnp.cos(phase))
    return jnp.stack([ramp_col] + sine_cols + cosine_cols + [jnp.ones_like(ramp_col)], axis=1)

def filter_values(filter_in, filter_mid, filter_out, decay_rate, positions, seq_total):
    feature_rows = positional_features(positions, seq_total)
    hidden = jnp.sin(jnp.dot(feature_rows, filter_in, precision=lax.Precision.HIGHEST, preferred_element_type=jnp.float32))
    hidden = jnp.sin(jnp.dot(hidden, filter_mid, precision=lax.Precision.HIGHEST, preferred_element_type=jnp.float32))
    shaped = jnp.dot(hidden, filter_out, precision=lax.Precision.HIGHEST, preferred_element_type=jnp.float32)
    time_col = positions.astype(jnp.float32)[:, None]
    window = jnp.exp(-decay_rate[None, :] * time_col) * jnp.sqrt(decay_rate + 1.0 / seq_total)[None, :]
    return shaped * window

def reference(query_act, key_act, value_act, out_grad, filter_in, filter_mid, filter_out, decay_rate, skip_gain):
    positions = jnp.arange(LENGTH, dtype=jnp.int32)

    def make_filter(w_first, w_second, w_third, rates):
        return filter_values(w_first, w_second, w_third, rates, positions, LENGTH)
    filter_vals, pullback = jax.vjp(make_filter, filter_in, filter_mid, filter_out, decay_rate)
    query_wide = query_act.astype(jnp.float32)
    key_wide = key_act.astype(jnp.float32)
    value_wide = value_act.astype(jnp.float32)
    grad_wide = out_grad.astype(jnp.float32)
    gated = key_wide * value_wide
    incoming = grad_wide * query_wide
    padded_len = 2 * LENGTH
    gated_spec = jnp.fft.rfft(gated, n=padded_len, axis=0)
    incoming_spec = jnp.fft.rfft(incoming, n=padded_len, axis=0)
    filter_spec = jnp.fft.rfft(filter_vals, n=padded_len, axis=0)
    conv_field = jnp.fft.irfft(gated_spec * filter_spec, n=padded_len, axis=0)[:LENGTH]
    back_field = jnp.fft.irfft(jnp.conj(filter_spec) * incoming_spec, n=padded_len, axis=0)[:LENGTH]
    dfilt = jnp.fft.irfft(incoming_spec * jnp.conj(gated_spec), n=padded_len, axis=0)[:LENGTH]
    mixed_field = conv_field + skip_gain[None, :] * gated
    output = (query_wide * mixed_field).astype(jnp.bfloat16)
    grad_query = (grad_wide * mixed_field).astype(jnp.bfloat16)
    dgated = back_field + skip_gain[None, :] * incoming
    grad_key = (dgated * value_wide).astype(jnp.bfloat16)
    grad_value = (dgated * key_wide).astype(jnp.bfloat16)
    grad_first, grad_second, grad_third, grad_rates = pullback(dfilt.astype(filter_vals.dtype))
    grad_skip = lax.optimization_barrier(jnp.sum(incoming * gated, axis=0))
    return (output, grad_query, grad_key, grad_value, grad_first, grad_second, grad_third, grad_rates, grad_skip)
```

```python
import functools
import math

import jax
import jax.numpy as jnp
import ml_dtypes
import numpy as np
from jax import lax
from jax.experimental import pallas as pl
from jax.experimental.pallas import tpu as pltpu
from jax.sharding import PartitionSpec as P

F32 = jnp.float32
BF16 = jnp.bfloat16
LENGTH = 16384
SEQ = 32
ROWS = 512
SIDE = 128
OWN = 4
ORDER = 64
STEP = 2048
PIECE = 256
MIB = 1 << 20


def split_table(table):
    high = table.astype(ml_dtypes.bfloat16)
    low = (table - high.astype(np.float64)).astype(ml_dtypes.bfloat16)
    return high, low


@functools.cache
def time_rows():
    p = np.arange(SIDE)
    return 4 * (p % SEQ) + p // SEQ


@functools.cache
def feature_table():
    t = (time_rows()[:, None] * SIDE + np.arange(SIDE)[None, :]).reshape(-1)
    rows = [t / LENGTH]
    angles = []
    for i in range(7):
        factor = max(1, LENGTH // 4 // 4 ** (6 - i))
        angles.append((factor * t % LENGTH) * (2.0 * math.pi / LENGTH))
    rows += [np.sin(a) for a in angles] + [np.cos(a) for a in angles] + [np.ones(LENGTH)]
    high, low = split_table(np.stack(rows).astype(np.float64))
    return np.concatenate([high, low])


@functools.cache
def transform_tables():
    idx = np.arange(SIDE)
    n1 = time_rows()
    first = np.exp(-2j * np.pi * ((n1[None, :] * idx[:, None] % SIDE) / SIDE + n1[None, :] / (4 * SIDE)))
    twiddle = np.exp(-2j * np.pi * idx[None, :] * (4 * idx[:, None] + 1) / (4 * LENGTH))
    second = np.exp(-2j * np.pi * (idx[:, None] * idx[None, :] % SIDE) / SIDE)
    high, low = split_table(np.concatenate([first.real, first.imag]))
    first_fwd = np.concatenate([high, high, low], axis=1)
    high, low = split_table(np.block([[second.real, second.imag], [-second.imag, second.real]]))
    second_fwd = np.concatenate([high, high, low])
    high, low = split_table(np.block([[second.real, -second.imag], [second.imag, second.real]]))
    second_inv = np.concatenate([high, high, low])
    high, low = split_table(np.concatenate([first.real.T, first.imag.T], axis=1) / LENGTH)
    first_inv = np.concatenate([high, high, low], axis=1)
    twiddle = np.concatenate([twiddle.real, twiddle.imag], axis=1).astype(np.float32)
    return first_fwd, second_fwd, twiddle, second_inv, first_inv


@functools.cache
def turn_polynomials():
    nodes = 0.5 * np.cos(np.pi * (np.arange(400) + 0.5) / 800)
    squares = nodes * nodes

    def fit(values, weight, count):
        basis = np.stack([squares**k for k in range(count)], axis=1)
        return np.linalg.lstsq(basis * weight[:, None], values, rcond=None)[0]

    sine = fit(np.sin(2 * np.pi * nodes), nodes, 6)
    cosine = fit(np.cos(2 * np.pi * nodes), np.ones_like(nodes), 7)
    return [float(c) for c in sine], [float(c) for c in cosine]


def sine_cosine(turns):
    sine, cosine = turn_polynomials()
    part = turns - jnp.round(turns)
    square = part * part
    s = jnp.full_like(square, sine[-1])
    for c in sine[-2::-1]:
        s = s * square + c
    c_out = jnp.full_like(square, cosine[-1])
    for c in cosine[-2::-1]:
        c_out = c_out * square + c
    return s * part, c_out


def halves(x):
    high = x.astype(BF16)
    return high, (x - high.astype(F32)).astype(BF16)


def dot(a, b):
    return jnp.dot(a, b, preferred_element_type=F32)


def dot_nt(a, b, precision=None):
    return lax.dot_general(a, b, (((1,), (1,)), ((), ())), precision=precision, preferred_element_type=F32)


def dot_tn(a, b, precision=None):
    return lax.dot_general(a, b, (((0,), (0,)), ((), ())), precision=precision, preferred_element_type=F32)


def data_left(x, axis):
    high, low = halves(x)
    return jnp.concatenate([high, low, high], axis=axis)


def weight_left(x, axis):
    high, low = halves(x)
    return jnp.concatenate([high, high, low], axis=axis)


def own_channels(place):
    row = lax.broadcasted_iota(jnp.int32, (8, SIDE), 0)
    lane = lax.broadcasted_iota(jnp.int32, (8, SIDE), 1)
    return jnp.where((row < OWN) & (lane == place + SEQ * row), 1.0, 0.0).astype(F32)


def position_grid():
    row = lax.broadcasted_iota(jnp.int32, (SIDE, SIDE), 0)
    lane = lax.broadcasted_iota(jnp.int32, (SIDE, SIDE), 1)
    return (ROWS * (row % SEQ) + SIDE * (row // SEQ) + lane).astype(F32)


def spec(shape, index=None):
    if index is None:
        zeros = (0,) * len(shape)
        return pl.BlockSpec(shape, lambda i: zeros)
    return pl.BlockSpec(shape, index)


def out(shape, dtype=F32):
    return jax.ShapeDtypeStruct(shape, dtype)


def call(kernel, grid, in_specs, out_specs, out_shape, scratch=(), limit=32, flops=1, nbytes=1, interpret=False):
    return pl.pallas_call(
        kernel,
        grid=(grid,),
        in_specs=in_specs,
        out_specs=out_specs,
        out_shape=out_shape,
        scratch_shapes=scratch,
        compiler_params=pltpu.CompilerParams(vmem_limit_bytes=limit * MIB),
        cost_estimate=pl.CostEstimate(flops=flops, bytes_accessed=nbytes, transcendentals=0),
        interpret=interpret,
    )


def send_kernel(query, key, value, grad, sent):
    for h in range(ROWS // SIDE):
        rows = pl.ds(SIDE * h, SIDE)
        gated = key[rows, :].astype(F32) * value[rows, :].astype(F32)
        incoming = grad[rows, :].astype(F32) * query[rows, :].astype(F32)
        for offset, block in ((0, gated.T), (OWN, incoming.T)):
            for c in range(OWN):
                sent[pl.ds(8 * h + offset + c, SEQ, stride=SEQ), :] = block[SEQ * c : SEQ * (c + 1), :]


def receive_kernel(query, key, value, grad, skip, field, output, grad_query, grad_key, grad_value):
    for h in range(ROWS // SIDE):
        rows = pl.ds(SIDE * h, SIDE)
        query_wide = query[rows, :].astype(F32)
        key_wide = key[rows, :].astype(F32)
        value_wide = value[rows, :].astype(F32)
        grad_wide = grad[rows, :].astype(F32)
        conv, back = (
            jnp.concatenate([field[pl.ds(8 * h + offset + c, SEQ, stride=SEQ), :] for c in range(OWN)]).T
            for offset in (0, OWN)
        )
        mixed = conv + skip[...] * (key_wide * value_wide)
        output[rows, :] = (query_wide * mixed).astype(BF16)
        grad_query[rows, :] = (grad_wide * mixed).astype(BF16)
        dgated = back + skip[...] * (grad_wide * query_wide)
        grad_key[rows, :] = (dgated * value_wide).astype(BF16)
        grad_value[rows, :] = (dgated * key_wide).astype(BF16)


def forward_rows(fields, first_fwd, second_fwd, twiddle):
    cos, sin = twiddle[:, :SIDE], twiddle[:, SIDE:]
    turned = []
    for pair in range(0, len(fields), 2):
        stage = dot(first_fwd[...], data_left(jnp.concatenate(fields[pair : pair + 2], axis=1), 0))
        for k in range(2):
            re = stage[:SIDE, SIDE * k : SIDE * (k + 1)]
            im = stage[SIDE:, SIDE * k : SIDE * (k + 1)]
            turned.append(data_left(jnp.concatenate([re * cos - im * sin, re * sin + im * cos], axis=1), 1))
    return dot(jnp.concatenate(turned), second_fwd[...])


def inverse_rows(spectra, first_inv, second_inv, twiddle):
    cos, sin = twiddle[:, :SIDE], twiddle[:, SIDE:]
    stage = dot(jnp.concatenate([data_left(s, 1) for s in spectra]), second_inv[...])
    turned = []
    for k in range(len(spectra)):
        re = stage[SIDE * k : SIDE * (k + 1), :SIDE]
        im = stage[SIDE * k : SIDE * (k + 1), SIDE:]
        turned.append(jnp.concatenate([re * cos + im * sin, im * cos - re * sin]))
    fields = []
    for pair in range(0, len(spectra), 2):
        both = dot(first_inv[...], data_left(jnp.concatenate(turned[pair : pair + 2], axis=1), 0))
        fields += [both[:, :SIDE], both[:, SIDE:]]
    return fields


def filter_kernel(place, features, filter_in, filter_mid, filter_out, decay, first_fwd, second_fwd, twiddle,
                  h1_high, h1_low, cos1, h2_high, h2_low, cos2, spectrum, filt, window, shaped):
    step = pl.program_id(0)
    own = own_channels(place())
    turn = 1.0 / (2.0 * math.pi)
    in_high, in_low = halves(filter_in[...].T * turn)
    weight1 = jnp.concatenate([in_high, in_low, in_high], axis=1)
    weight2 = weight_left(filter_mid[...].T * turn, 1)
    weight3 = weight_left(dot_nt(own, filter_out[...], lax.Precision.HIGHEST), 1)
    pieces = [pl.ds(PIECE * k, PIECE) for k in range(STEP // PIECE)]
    for piece in pieces:
        feature = features[:, piece]
        rows = jnp.concatenate([feature[:16], feature[:16], feature[16:]])
        sine, cosine = sine_cosine(dot(weight1, rows))
        cos1[:, piece] = cosine
        h1_high[:, piece], h1_low[:, piece] = halves(sine)
    for piece in pieces:
        high = h1_high[:, piece]
        sine, cosine = sine_cosine(dot(weight2, jnp.concatenate([high, h1_low[:, piece], high])))
        cos2[:, piece] = cosine
        h2_high[:, piece], h2_low[:, piece] = halves(sine)
    for k, piece in enumerate(pieces):
        high = h2_high[:, piece]
        values = dot(weight3, jnp.concatenate([high, h2_low[:, piece], high]))
        for m in range(PIECE // SIDE):
            row = 8 * (step * (STEP // SIDE) + k * (PIECE // SIDE) + m)
            shaped[pl.ds(pl.multiple_of(row, 8), 8), :] = values[:, SIDE * m : SIDE * (m + 1)]

    @pl.when(step == LENGTH // STEP - 1)
    def _():
        time = position_grid()
        rates = jnp.sum(own * decay[...], axis=1, keepdims=True)
        fields = []
        for c in range(OWN):
            rate = rates[c : c + 1, :]
            window_c = jnp.exp(-rate * time) * jnp.sqrt(rate + 1.0 / LENGTH)
            field = shaped[pl.ds(c, SIDE, stride=8), :] * window_c
            window[pl.ds(SIDE * c, SIDE), :] = window_c
            filt[pl.ds(SIDE * c, SIDE), :] = field
            fields.append(field)
        spectrum[...] = forward_rows(fields, first_fwd, second_fwd, twiddle)


def convolve_kernel(place, field, spectrum, filt, window, decay, first_fwd, second_fwd, twiddle, second_inv, first_inv,
                    sent, dshaped, sums):
    fields = []
    for c in range(OWN):
        for offset in (0, OWN):
            fields.append(
                jnp.concatenate([field[pl.ds(8 * h + offset + c, SEQ, stride=SEQ), :] for h in range(ROWS // SIDE)])
            )
    spectra = forward_rows(fields, first_fwd, second_fwd, twiddle)
    products = []
    for c in range(OWN):
        gated, incoming = (spectra[SIDE * k : SIDE * (k + 1)] for k in (2 * c, 2 * c + 1))
        kernel = spectrum[pl.ds(SIDE * c, SIDE), :]
        gated_re, gated_im = gated[:, :SIDE], gated[:, SIDE:]
        incoming_re, incoming_im = incoming[:, :SIDE], incoming[:, SIDE:]
        kernel_re, kernel_im = kernel[:, :SIDE], kernel[:, SIDE:]
        products.append((
            jnp.concatenate([kernel_re * gated_re - kernel_im * gated_im,
                             kernel_re * gated_im + kernel_im * gated_re], axis=1),
            jnp.concatenate([kernel_re * incoming_re + kernel_im * incoming_im,
                             kernel_re * incoming_im - kernel_im * incoming_re], axis=1),
            jnp.concatenate([gated_re * incoming_re + gated_im * incoming_im,
                             gated_re * incoming_im - gated_im * incoming_re], axis=1),
        ))
    results = inverse_rows([p for c in range(OWN) for p in products[c][:2]] + [products[c][2] for c in range(OWN)],
                           first_inv, second_inv, twiddle)
    time = position_grid()
    rates = jnp.sum(own_channels(place()) * decay[...], axis=1, keepdims=True)
    for c in range(OWN):
        for offset, result in ((0, results[2 * c]), (OWN, results[2 * c + 1])):
            for h in range(ROWS // SIDE):
                sent[pl.ds(8 * h + offset + c, SEQ, stride=SEQ), :] = result[SEQ * h : SEQ * (h + 1), :]
        dfilt = results[2 * OWN + c]
        dshaped[pl.ds(c, SIDE, stride=8), :] = dfilt * window[pl.ds(SIDE * c, SIDE), :]
        dshaped[pl.ds(c + OWN, SIDE, stride=8), :] = jnp.zeros((SIDE, SIDE), F32)
        slope = 0.5 / (rates[c : c + 1, :] + 1.0 / LENGTH) - time
        sums[pl.ds(c, 1), :] = jnp.sum(dfilt * filt[pl.ds(SIDE * c, SIDE), :] * slope, axis=0, keepdims=True)
        sums[pl.ds(c + OWN, 1), :] = jnp.sum(fields[2 * c] * fields[2 * c + 1], axis=0, keepdims=True)


def backward_kernel(place, features, h1_high, h1_low, cos1, h2_high, h2_low, cos2, dshaped, sums, filter_mid, filter_out,
                    grads, grad_mid, grad_in, grad_out, d2_high, d2_low, d1_high, d1_low):
    step = pl.program_id(0)
    own = own_channels(place())
    weight3 = weight_left(dot_nt(filter_out[...], own, lax.Precision.HIGHEST), 1)
    weight2 = weight_left(filter_mid[...], 1)

    @pl.when(step == 0)
    def _():
        grad_mid[...] = jnp.zeros_like(grad_mid)
        grad_in[...] = jnp.zeros_like(grad_in)
        grad_out[...] = jnp.zeros_like(grad_out)

    pieces = [pl.ds(PIECE * k, PIECE) for k in range(STEP // PIECE)]
    shaped_high, shaped_low = halves(jnp.concatenate([dshaped[pl.ds(8 * m, 8), :] for m in range(STEP // SIDE)], axis=1))
    for k, piece in enumerate(pieces):
        part = slice(PIECE * k, PIECE * (k + 1))
        rows = jnp.concatenate([shaped_high[:, part], shaped_low[:, part], shaped_high[:, part]])
        d2_high[:, piece], d2_low[:, piece] = halves(dot(weight3, rows) * cos2[:, piece])
    for piece in pieces:
        high = d2_high[:, piece]
        d1_high[:, piece], d1_low[:, piece] = halves(
            dot(weight2, jnp.concatenate([high, d2_low[:, piece], high])) * cos1[:, piece]
        )
    grad_mid[...] += dot_nt(jnp.concatenate([h1_high[...], h1_low[...]]), jnp.concatenate([d2_high[...], d2_low[...]]))
    grad_in[...] += dot_nt(features[...], jnp.concatenate([d1_high[...], d1_low[...]]))
    grad_out[...] += dot_nt(jnp.concatenate([shaped_high, shaped_low]), jnp.concatenate([h2_high[...], h2_low[...]]))

    @pl.when(step == LENGTH // STEP - 1)
    def _():
        def joined(x, half):
            return x[:half, :ORDER] + (x[:half, ORDER:] + x[half:, :ORDER])

        mid = joined(grad_mid, 64)
        first = joined(grad_in, 16)
        third = joined(grad_out, 8)
        grads[pl.ds(0, 32), :] = jnp.concatenate([mid[:32], mid[32:]], axis=1)
        grads[pl.ds(32, 8), :] = jnp.concatenate([first[:8], first[8:]], axis=1)
        grads[pl.ds(40, 64), :] = dot_tn(third, own, lax.Precision.HIGHEST)
        totals = jnp.sum(sums[...], axis=1, keepdims=True)
        grads[pl.ds(104, 8), :] = jnp.concatenate([
            jnp.sum(own[:OWN] * totals[:OWN], axis=0, keepdims=True),
            jnp.sum(own[:OWN] * totals[OWN:], axis=0, keepdims=True),
            jnp.zeros((6, SIDE), F32),
        ])


def finish_kernel(mine, other, grad_in, grad_mid, grad_out, grad_decay, grad_skip):
    total = mine[...] + other[...]
    grad_mid[pl.ds(0, 32), :] = total[:32, :ORDER]
    grad_mid[pl.ds(32, 32), :] = total[:32, ORDER:]
    grad_in[pl.ds(0, 8), :] = total[32:40, :ORDER]
    grad_in[pl.ds(8, 8), :] = total[32:40, ORDER:]
    grad_out[...] = total[40:104]
    grad_decay[...] = total[104:105]
    grad_skip[...] = total[105:106]


def seq_place():
    return lax.axis_index("seq")


def run_send(query, key, value, grad, **kw):
    block = spec((ROWS, SIDE))
    return call(send_kernel, 1, [block] * 4, spec((1024, SIDE)), out((1024, SIDE)), **kw)(query, key, value, grad)


def run_filter(filter_in, filter_mid, filter_out, decay, place=seq_place, **kw):
    first_fwd, second_fwd, twiddle, _, _ = transform_tables()
    wide = lambda i: (0, i)
    hidden = spec((ORDER, STEP), wide)
    half, full = out((ORDER, LENGTH), BF16), out((ORDER, LENGTH))
    return call(
        functools.partial(filter_kernel, place),
        LENGTH // STEP,
        [spec((32, STEP), wide), spec((16, ORDER)), spec((ORDER, ORDER)), spec((ORDER, SIDE)), spec((1, SIDE)),
         spec((256, 384)), spec((768, 256)), spec((SIDE, 256))],
        [hidden] * 6 + [spec((512, 256)), spec((512, SIDE)), spec((512, SIDE))],
        [half, half, full, half, half, full, out((512, 256)), out((512, SIDE)), out((512, SIDE))],
        scratch=[pltpu.VMEM((1024, SIDE), F32)],
        flops=8 * 10**9, nbytes=20 * MIB, **kw,
    )(feature_table(), filter_in, filter_mid, filter_out, decay, first_fwd, second_fwd, twiddle)


def run_convolve(field, spectrum, filt, window, decay, place=seq_place, **kw):
    first_fwd, second_fwd, twiddle, second_inv, first_inv = transform_tables()
    return call(
        functools.partial(convolve_kernel, place),
        1,
        [spec((1024, SIDE)), spec((512, 256)), spec((512, SIDE)), spec((512, SIDE)), spec((1, SIDE)),
         spec((256, 384)), spec((768, 256)), spec((SIDE, 256)), spec((768, 256)), spec((SIDE, 768))],
        [spec((1024, SIDE)), spec((1024, SIDE)), spec((8, SIDE))],
        [out((1024, SIDE)), out((1024, SIDE)), out((8, SIDE))],
        flops=4 * 10**9, nbytes=4 * MIB, **kw,
    )(field, spectrum, filt, window, decay, first_fwd, second_fwd, twiddle, second_inv, first_inv)


def run_backward(hidden, dshaped, sums, filter_mid, filter_out, place=seq_place, **kw):
    wide = lambda i: (0, i)
    block = spec((ORDER, STEP), wide)
    return call(
        functools.partial(backward_kernel, place),
        LENGTH // STEP,
        [spec((32, STEP), wide)] + [block] * 6 + [spec((STEP // 16, SIDE), lambda i: (i, 0)), spec((8, SIDE)),
         spec((ORDER, ORDER)), spec((ORDER, SIDE))],
        spec((112, SIDE)),
        out((112, SIDE)),
        scratch=[pltpu.VMEM((SIDE, SIDE), F32), pltpu.VMEM((32, SIDE), F32), pltpu.VMEM((16, SIDE), F32)]
        + [pltpu.VMEM((ORDER, STEP), BF16)] * 4,
        flops=8 * 10**9, nbytes=20 * MIB, **kw,
    )(feature_table(), *hidden, dshaped, sums, filter_mid, filter_out)


def run_receive(query, key, value, grad, skip, field, **kw):
    block = spec((ROWS, SIDE))
    return call(receive_kernel, 1, [block] * 4 + [spec((1, SIDE)), spec((1024, SIDE))], [block] * 4,
                [out((ROWS, SIDE), BF16)] * 4, **kw)(query, key, value, grad, skip, field)


def run_finish(mine, other, **kw):
    shapes = [(16, ORDER), (ORDER, ORDER), (ORDER, SIDE), (1, SIDE), (1, SIDE)]
    return call(finish_kernel, 1, [spec((112, SIDE))] * 2, [spec(s) for s in shapes], [out(s) for s in shapes], **kw)(
        mine, other
    )


def exchanged(x, axis, distance):
    return lax.ppermute(x, axis, [(i, i ^ distance) for i in range(lax.axis_size(axis))])


def group_sum(x, axis, distances):
    values = [x] + [exchanged(x, axis, d) for d in distances]
    while len(values) > 1:
        values = [a + b for a, b in zip(values[::2], values[1::2])]
    return values[0]


def body(query, key, value, grad, filter_in, filter_mid, filter_out, decay_rate, skip_gain):
    decay = decay_rate.reshape(1, SIDE)
    skip = skip_gain.reshape(1, SIDE)
    sent = run_send(query, key, value, grad).reshape(SEQ, SEQ, SIDE)
    field = lax.all_to_all(sent, "seq", 0, 0, tiled=True).reshape(1024, SIDE)
    *hidden, spectrum, filt, window = run_filter(filter_in, filter_mid, filter_out, decay)
    sent, dshaped, sums = run_convolve(field, spectrum, filt, window, decay)
    field = lax.all_to_all(sent.reshape(SEQ, SEQ, SIDE), "seq", 0, 0, tiled=True).reshape(1024, SIDE)
    grads = run_backward(hidden, dshaped, sums, filter_mid, filter_out)
    output, grad_query, grad_key, grad_value = run_receive(query, key, value, grad, skip, field)
    shared = group_sum(grads[:40], "chan", range(1, 8))
    grads = jnp.concatenate([shared, grads[40:]])
    grads = group_sum(grads, "seq", (8, 16, 24))
    grads = group_sum(grads, "seq", (2, 4, 6))
    first, second, third, rates, gains = run_finish(grads, exchanged(grads, "seq", 1))
    return (output, grad_query, grad_key, grad_value, first, second, third, rates.reshape(SIDE), gains.reshape(SIDE))


def solution(mesh):
    wide = P("seq", "chan")
    return jax.shard_map(
        body,
        mesh=mesh,
        in_specs=(wide, wide, wide, wide, P(), P(), P(None, "chan"), P("chan"), P("chan")),
        out_specs=(wide, wide, wide, wide, P(), P(), P(None, "chan"), P("chan"), P("chan")),
        check_vma=False,
    )
```

```python
import functools
import math

import jax
import jax.numpy as jnp
import ml_dtypes
import numpy as np
from jax import lax
from jax.experimental import pallas as pl
from jax.experimental.pallas import tpu as pltpu
from jax.sharding import PartitionSpec as P

F32 = jnp.float32
BF16 = jnp.bfloat16
LENGTH = 16384
SEQ = 32
ROWS = 512
SIDE = 128
OWN = 4
ORDER = 64
STEP = 2048
PIECE = 256
HALF = LENGTH // 2
MIB = 1 << 20


def split_table(table):
    high = table.astype(ml_dtypes.bfloat16)
    low = (table - high.astype(np.float64)).astype(ml_dtypes.bfloat16)
    return high, low


@functools.cache
def time_rows():
    p = np.arange(SIDE)
    return 4 * (p % SEQ) + p // SEQ


@functools.cache
def feature_table():
    t = (time_rows()[:, None] * SIDE + np.arange(SIDE)[None, :]).reshape(-1)
    rows = [t / LENGTH]
    angles = []
    for i in range(7):
        factor = max(1, LENGTH // 4 // 4 ** (6 - i))
        angles.append((factor * t % LENGTH) * (2.0 * math.pi / LENGTH))
    rows += [np.sin(a) for a in angles] + [np.cos(a) for a in angles] + [np.ones(LENGTH)]
    high, low = split_table(np.stack(rows).astype(np.float64))
    return np.concatenate([high, low])


@functools.cache
def transform_tables():
    idx = np.arange(SIDE)
    n1 = time_rows()
    first = np.exp(-2j * np.pi * ((n1[None, :] * idx[:, None] % SIDE) / SIDE + n1[None, :] / (4 * SIDE)))
    twiddle = np.exp(-2j * np.pi * idx[None, :] * (4 * idx[:, None] + 1) / (4 * LENGTH))
    second = np.exp(-2j * np.pi * (idx[:, None] * idx[None, :] % SIDE) / SIDE)
    high, low = split_table(np.concatenate([first.real, first.imag]))
    first_fwd = np.concatenate([high, high, low], axis=1)
    high, low = split_table(np.block([[second.real, second.imag], [-second.imag, second.real]]))
    second_fwd = np.concatenate([high, high, low])
    high, low = split_table(np.block([[second.real, -second.imag], [second.imag, second.real]]))
    second_inv = np.concatenate([high, high, low])
    high, low = split_table(np.concatenate([first.real.T, first.imag.T], axis=1) / LENGTH)
    first_inv = np.concatenate([high, high, low], axis=1)
    twiddle = np.concatenate([twiddle.real, twiddle.imag], axis=1).astype(np.float32)
    return first_fwd, second_fwd, twiddle, second_inv, first_inv


@functools.cache
def turn_polynomials():
    nodes = 0.5 * np.cos(np.pi * (np.arange(400) + 0.5) / 800)
    squares = nodes * nodes

    def fit(values, weight, count):
        basis = np.stack([squares**k for k in range(count)], axis=1)
        return np.linalg.lstsq(basis * weight[:, None], values, rcond=None)[0]

    sine = fit(np.sin(2 * np.pi * nodes), nodes, 6)
    cosine = fit(np.cos(2 * np.pi * nodes), np.ones_like(nodes), 7)
    return [float(c) for c in sine], [float(c) for c in cosine]


def sine_cosine(turns):
    sine, cosine = turn_polynomials()
    part = turns - jnp.round(turns)
    square = part * part
    s = jnp.full_like(square, sine[-1])
    for c in sine[-2::-1]:
        s = s * square + c
    c_out = jnp.full_like(square, cosine[-1])
    for c in cosine[-2::-1]:
        c_out = c_out * square + c
    return s * part, c_out


def halves(x):
    high = x.astype(BF16)
    return high, (x - high.astype(F32)).astype(BF16)


def dot(a, b):
    return jnp.dot(a, b, preferred_element_type=F32)


def dot_nt(a, b, precision=None):
    return lax.dot_general(a, b, (((1,), (1,)), ((), ())), precision=precision, preferred_element_type=F32)


def dot_tn(a, b, precision=None):
    return lax.dot_general(a, b, (((0,), (0,)), ((), ())), precision=precision, preferred_element_type=F32)


def data_left(x, axis):
    high, low = halves(x)
    return jnp.concatenate([high, low, high], axis=axis)


def weight_left(x, axis):
    high, low = halves(x)
    return jnp.concatenate([high, high, low], axis=axis)


def own_channels(place):
    row = lax.broadcasted_iota(jnp.int32, (8, SIDE), 0)
    lane = lax.broadcasted_iota(jnp.int32, (8, SIDE), 1)
    other = place + 1 - 2 * (place % 2)
    channel = jnp.where(row < OWN, place + SEQ * row, other + SEQ * (row - OWN))
    return jnp.where(lane == channel, 1.0, 0.0).astype(F32)


def position_grid():
    row = lax.broadcasted_iota(jnp.int32, (SIDE, SIDE), 0)
    lane = lax.broadcasted_iota(jnp.int32, (SIDE, SIDE), 1)
    return (ROWS * (row % SEQ) + SIDE * (row // SEQ) + lane).astype(F32)


def spec(shape, index=None):
    if index is None:
        zeros = (0,) * len(shape)
        return pl.BlockSpec(shape, lambda i: zeros)
    return pl.BlockSpec(shape, index)


def out(shape, dtype=F32):
    return jax.ShapeDtypeStruct(shape, dtype)


def call(kernel, grid, in_specs, out_specs, out_shape, scratch=(), limit=16, flops=1, nbytes=1, interpret=False):
    return pl.pallas_call(
        kernel,
        grid=(grid,),
        in_specs=in_specs,
        out_specs=out_specs,
        out_shape=out_shape,
        scratch_shapes=scratch,
        compiler_params=pltpu.CompilerParams(vmem_limit_bytes=limit * MIB),
        cost_estimate=pl.CostEstimate(flops=flops, bytes_accessed=nbytes, transcendentals=0),
        interpret=interpret,
    )


def send_kernel(query, key, value, grad, sent, held, sems):
    copies = [pltpu.make_async_copy(x, held.at[k], sems.at[k]) for k, x in enumerate((key, value, grad, query))]
    for copy in copies:
        copy.start()
    for offset, first, second in ((0, 0, 1), (OWN, 2, 3)):
        copies[first].wait()
        copies[second].wait()
        for h in range(ROWS // SIDE):
            rows = pl.ds(SIDE * h, SIDE)
            block = (held[first, rows, :].astype(F32) * held[second, rows, :].astype(F32)).T
            for c in range(OWN):
                sent[pl.ds(8 * h + offset + c, SEQ, stride=SEQ), :] = block[SEQ * c : SEQ * (c + 1), :]


def receive_kernel(query, key, value, grad, skip, field, output, grad_query, grad_key, grad_value):
    for h in range(ROWS // SIDE):
        rows = pl.ds(SIDE * h, SIDE)
        query_wide = query[rows, :].astype(F32)
        key_wide = key[rows, :].astype(F32)
        value_wide = value[rows, :].astype(F32)
        grad_wide = grad[rows, :].astype(F32)
        conv, back = (
            jnp.concatenate([field[pl.ds(8 * h + offset + c, SEQ, stride=SEQ), :] for c in range(OWN)]).T
            for offset in (0, OWN)
        )
        mixed = conv + skip[...] * (key_wide * value_wide)
        output[rows, :] = (query_wide * mixed).astype(BF16)
        grad_query[rows, :] = (grad_wide * mixed).astype(BF16)
        dgated = back + skip[...] * (grad_wide * query_wide)
        grad_key[rows, :] = (dgated * value_wide).astype(BF16)
        grad_value[rows, :] = (dgated * key_wide).astype(BF16)


def forward_rows(fields, first_fwd, second_fwd, twiddle):
    cos, sin = twiddle[:, :SIDE], twiddle[:, SIDE:]
    turned = []
    for pair in range(0, len(fields), 2):
        stage = dot(first_fwd[...], data_left(jnp.concatenate(fields[pair : pair + 2], axis=1), 0))
        for k in range(2):
            re = stage[:SIDE, SIDE * k : SIDE * (k + 1)]
            im = stage[SIDE:, SIDE * k : SIDE * (k + 1)]
            turned.append(data_left(jnp.concatenate([re * cos - im * sin, re * sin + im * cos], axis=1), 1))
    return dot(jnp.concatenate(turned), second_fwd[...])


def inverse_rows(spectra, first_inv, second_inv, twiddle):
    cos, sin = twiddle[:, :SIDE], twiddle[:, SIDE:]
    stage = dot(jnp.concatenate([data_left(s, 1) for s in spectra]), second_inv[...])
    turned = []
    for k in range(len(spectra)):
        re = stage[SIDE * k : SIDE * (k + 1), :SIDE]
        im = stage[SIDE * k : SIDE * (k + 1), SIDE:]
        turned.append(jnp.concatenate([re * cos + im * sin, im * cos - re * sin]))
    fields = []
    for pair in range(0, len(spectra), 2):
        both = dot(first_inv[...], data_left(jnp.concatenate(turned[pair : pair + 2], axis=1), 0))
        fields += [both[:, :SIDE], both[:, SIDE:]]
    return fields


def filter_kernel(place, features, filter_in, filter_mid, filter_out,
                  h1_high, h1_low, cos1, h2_high, h2_low, cos2, mine, theirs, shaped):
    step = pl.program_id(0)
    own = own_channels(place())
    turn = 1.0 / (2.0 * math.pi)
    in_high, in_low = halves(filter_in[...].T * turn)
    weight1 = jnp.concatenate([in_high, in_low, in_high], axis=1)
    weight2 = weight_left(filter_mid[...].T * turn, 1)
    weight3 = weight_left(dot_nt(own, filter_out[...], lax.Precision.HIGHEST), 1)
    pieces = [pl.ds(PIECE * k, PIECE) for k in range(STEP // PIECE)]
    for piece in pieces:
        feature = features[:, piece]
        rows = jnp.concatenate([feature[:16], feature[:16], feature[16:]])
        sine, cosine = sine_cosine(dot(weight1, rows))
        cos1[:, piece] = cosine
        h1_high[:, piece], h1_low[:, piece] = halves(sine)
    for piece in pieces:
        high = h1_high[:, piece]
        sine, cosine = sine_cosine(dot(weight2, jnp.concatenate([high, h1_low[:, piece], high])))
        cos2[:, piece] = cosine
        h2_high[:, piece], h2_low[:, piece] = halves(sine)
    for k, piece in enumerate(pieces):
        high = h2_high[:, piece]
        values = dot(weight3, jnp.concatenate([high, h2_low[:, piece], high]))
        for m in range(PIECE // SIDE):
            row = 8 * (step * (STEP // SIDE) + k * (PIECE // SIDE) + m)
            shaped[pl.ds(pl.multiple_of(row, 8), 8), :] = values[:, SIDE * m : SIDE * (m + 1)]

    @pl.when(step == HALF // STEP - 1)
    def _():
        for c in range(OWN):
            mine[pl.ds(64 * c, 64), :] = shaped[pl.ds(c, 64, stride=8), :]
            theirs[pl.ds(64 * c, 64), :] = shaped[pl.ds(c + OWN, 64, stride=8), :]


def spectrum_kernel(place, mine, other, decay, first_fwd, second_fwd, twiddle, spectrum, filt, window):
    me = place()
    time = position_grid()
    rates = jnp.sum(own_channels(me) * decay[...], axis=1, keepdims=True)
    lower = me % 2 == 0
    fields = []
    for c in range(OWN):
        rate = rates[c : c + 1, :]
        window_c = jnp.exp(-rate * time) * jnp.sqrt(rate + 1.0 / LENGTH)
        here, there = mine[pl.ds(64 * c, 64), :], other[pl.ds(64 * c, 64), :]
        field = jnp.concatenate([jnp.where(lower, here, there), jnp.where(lower, there, here)]) * window_c
        window[pl.ds(SIDE * c, SIDE), :] = window_c
        filt[pl.ds(SIDE * c, SIDE), :] = field
        fields.append(field)
    spectrum[...] = forward_rows(fields, first_fwd, second_fwd, twiddle)


def convolve_kernel(place, field, spectrum, filt, window, decay, first_fwd, second_fwd, twiddle, second_inv, first_inv,
                    sent, mine, theirs, sums):
    fields = []
    for c in range(OWN):
        for offset in (0, OWN):
            fields.append(
                jnp.concatenate([field[pl.ds(8 * h + offset + c, SEQ, stride=SEQ), :] for h in range(ROWS // SIDE)])
            )
    spectra = forward_rows(fields, first_fwd, second_fwd, twiddle)
    products = []
    for c in range(OWN):
        gated, incoming = (spectra[SIDE * k : SIDE * (k + 1)] for k in (2 * c, 2 * c + 1))
        kernel = spectrum[pl.ds(SIDE * c, SIDE), :]
        gated_re, gated_im = gated[:, :SIDE], gated[:, SIDE:]
        incoming_re, incoming_im = incoming[:, :SIDE], incoming[:, SIDE:]
        kernel_re, kernel_im = kernel[:, :SIDE], kernel[:, SIDE:]
        products.append((
            jnp.concatenate([kernel_re * gated_re - kernel_im * gated_im,
                             kernel_re * gated_im + kernel_im * gated_re], axis=1),
            jnp.concatenate([kernel_re * incoming_re + kernel_im * incoming_im,
                             kernel_re * incoming_im - kernel_im * incoming_re], axis=1),
            jnp.concatenate([gated_re * incoming_re + gated_im * incoming_im,
                             gated_re * incoming_im - gated_im * incoming_re], axis=1),
        ))
    results = inverse_rows([p for c in range(OWN) for p in products[c][:2]] + [products[c][2] for c in range(OWN)],
                           first_inv, second_inv, twiddle)
    time = position_grid()
    me = place()
    lower = me % 2 == 0
    rates = jnp.sum(own_channels(me) * decay[...], axis=1, keepdims=True)
    zeros = jnp.zeros((64, SIDE), F32)
    for c in range(OWN):
        for offset, result in ((0, results[2 * c]), (OWN, results[2 * c + 1])):
            for h in range(ROWS // SIDE):
                sent[pl.ds(8 * h + offset + c, SEQ, stride=SEQ), :] = result[SEQ * h : SEQ * (h + 1), :]
        dfilt = results[2 * OWN + c]
        dshaped = dfilt * window[pl.ds(SIDE * c, SIDE), :]
        mine[pl.ds(c, 64, stride=8), :] = jnp.where(lower, dshaped[:64], dshaped[64:])
        mine[pl.ds(c + OWN, 64, stride=8), :] = zeros
        theirs[pl.ds(c, 64, stride=8), :] = zeros
        theirs[pl.ds(c + OWN, 64, stride=8), :] = jnp.where(lower, dshaped[64:], dshaped[:64])
        slope = 0.5 / (rates[c : c + 1, :] + 1.0 / LENGTH) - time
        sums[pl.ds(c, 1), :] = jnp.sum(dfilt * filt[pl.ds(SIDE * c, SIDE), :] * slope, axis=0, keepdims=True)
        sums[pl.ds(c + OWN, 1), :] = jnp.sum(fields[2 * c] * fields[2 * c + 1], axis=0, keepdims=True)


def backward_kernel(place, features, h1_high, h1_low, cos1, h2_high, h2_low, cos2, mine, other, sums, filter_mid, filter_out,
                    grads, grad_mid, grad_in, grad_out, d2_high, d2_low, d1_high, d1_low):
    step = pl.program_id(0)
    own = own_channels(place())
    weight3 = weight_left(dot_nt(filter_out[...], own, lax.Precision.HIGHEST), 1)
    weight2 = weight_left(filter_mid[...], 1)

    @pl.when(step == 0)
    def _():
        grad_mid[...] = jnp.zeros_like(grad_mid)
        grad_in[...] = jnp.zeros_like(grad_in)
        grad_out[...] = jnp.zeros_like(grad_out)

    pieces = [pl.ds(PIECE * k, PIECE) for k in range(STEP // PIECE)]
    shaped_high, shaped_low = halves(
        jnp.concatenate([mine[pl.ds(8 * m, 8), :] + other[pl.ds(8 * m, 8), :] for m in range(STEP // SIDE)], axis=1)
    )
    for k, piece in enumerate(pieces):
        part = slice(PIECE * k, PIECE * (k + 1))
        rows = jnp.concatenate([shaped_high[:, part], shaped_low[:, part], shaped_high[:, part]])
        d2_high[:, piece], d2_low[:, piece] = halves(dot(weight3, rows) * cos2[:, piece])
    for piece in pieces:
        high = d2_high[:, piece]
        d1_high[:, piece], d1_low[:, piece] = halves(
            dot(weight2, jnp.concatenate([high, d2_low[:, piece], high])) * cos1[:, piece]
        )
    grad_mid[...] += dot_nt(jnp.concatenate([h1_high[...], h1_low[...]]), jnp.concatenate([d2_high[...], d2_low[...]]))
    grad_in[...] += dot_nt(features[...], jnp.concatenate([d1_high[...], d1_low[...]]))
    grad_out[...] += dot_nt(jnp.concatenate([shaped_high, shaped_low]), jnp.concatenate([h2_high[...], h2_low[...]]))

    @pl.when(step == HALF // STEP - 1)
    def _():
        def joined(x, half):
            return x[:half, :ORDER] + (x[:half, ORDER:] + x[half:, :ORDER])

        mid = joined(grad_mid, 64)
        first = joined(grad_in, 16)
        third = joined(grad_out, 8)
        grads[pl.ds(0, 32), :] = jnp.concatenate([mid[:32], mid[32:]], axis=1)
        grads[pl.ds(32, 8), :] = jnp.concatenate([first[:8], first[8:]], axis=1)
        grads[pl.ds(40, 64), :] = dot_tn(third, own, lax.Precision.HIGHEST)
        totals = jnp.sum(sums[...], axis=1, keepdims=True)
        grads[pl.ds(104, 8), :] = jnp.concatenate([
            jnp.sum(own[:OWN] * totals[:OWN], axis=0, keepdims=True),
            jnp.sum(own[:OWN] * totals[OWN:], axis=0, keepdims=True),
            jnp.zeros((6, SIDE), F32),
        ])


def finish_kernel(mine, other, grad_in, grad_mid, grad_out, grad_decay, grad_skip):
    total = mine[...] + other[...]
    grad_mid[pl.ds(0, 32), :] = total[:32, :ORDER]
    grad_mid[pl.ds(32, 32), :] = total[:32, ORDER:]
    grad_in[pl.ds(0, 8), :] = total[32:40, :ORDER]
    grad_in[pl.ds(8, 8), :] = total[32:40, ORDER:]
    grad_out[...] = total[40:104]
    grad_decay[...] = total[104:105]
    grad_skip[...] = total[105:106]


def seq_place():
    return lax.axis_index("seq")


def run_send(query, key, value, grad, **kw):
    return call(
        send_kernel, 1, [pl.BlockSpec(memory_space=pltpu.HBM)] * 4, spec((1024, SIDE)), out((1024, SIDE)),
        scratch=[pltpu.VMEM((4, ROWS, SIDE), BF16), pltpu.SemaphoreType.DMA((4,))], **kw,
    )(query, key, value, grad)


def run_filter(features, filter_in, filter_mid, filter_out, place=seq_place, **kw):
    wide = lambda i: (0, i)
    hidden = spec((ORDER, STEP), wide)
    half, full = out((ORDER, HALF), BF16), out((ORDER, HALF))
    return call(
        functools.partial(filter_kernel, place),
        HALF // STEP,
        [spec((32, STEP), wide), spec((16, ORDER)), spec((ORDER, ORDER)), spec((ORDER, SIDE))],
        [hidden] * 6 + [spec((256, SIDE))] * 2,
        [half, half, full, half, half, full, out((256, SIDE)), out((256, SIDE))],
        scratch=[pltpu.VMEM((512, SIDE), F32)],
        flops=4 * 10**9, nbytes=10 * MIB, **kw,
    )(features, filter_in, filter_mid, filter_out)


def run_spectrum(mine, other, decay, place=seq_place, **kw):
    first_fwd, second_fwd, twiddle, _, _ = transform_tables()
    return call(
        functools.partial(spectrum_kernel, place),
        1,
        [spec((256, SIDE))] * 2 + [spec((1, SIDE)), spec((256, 384)), spec((768, 256)), spec((SIDE, 256))],
        [spec((512, 256)), spec((512, SIDE)), spec((512, SIDE))],
        [out((512, 256)), out((512, SIDE)), out((512, SIDE))],
        flops=10**9, nbytes=MIB, **kw,
    )(mine, other, decay, first_fwd, second_fwd, twiddle)


def run_convolve(field, spectrum, filt, window, decay, place=seq_place, **kw):
    first_fwd, second_fwd, twiddle, second_inv, first_inv = transform_tables()
    return call(
        functools.partial(convolve_kernel, place),
        1,
        [spec((1024, SIDE)), spec((512, 256)), spec((512, SIDE)), spec((512, SIDE)), spec((1, SIDE)),
         spec((256, 384)), spec((768, 256)), spec((SIDE, 256)), spec((768, 256)), spec((SIDE, 768))],
        [spec((1024, SIDE)), spec((512, SIDE)), spec((512, SIDE)), spec((8, SIDE))],
        [out((1024, SIDE)), out((512, SIDE)), out((512, SIDE)), out((8, SIDE))],
        flops=4 * 10**9, nbytes=4 * MIB, **kw,
    )(field, spectrum, filt, window, decay, first_fwd, second_fwd, twiddle, second_inv, first_inv)


def run_backward(features, hidden, mine, other, sums, filter_mid, filter_out, place=seq_place, **kw):
    wide = lambda i: (0, i)
    block = spec((ORDER, STEP), wide)
    deep = spec((STEP // 16, SIDE), lambda i: (i, 0))
    return call(
        functools.partial(backward_kernel, place),
        HALF // STEP,
        [spec((32, STEP), wide)] + [block] * 6 + [deep, deep, spec((8, SIDE)), spec((ORDER, ORDER)), spec((ORDER, SIDE))],
        spec((112, SIDE)),
        out((112, SIDE)),
        scratch=[pltpu.VMEM((SIDE, SIDE), F32), pltpu.VMEM((32, SIDE), F32), pltpu.VMEM((16, SIDE), F32)]
        + [pltpu.VMEM((ORDER, STEP), BF16)] * 4,
        flops=4 * 10**9, nbytes=10 * MIB, **kw,
    )(features, *hidden, mine, other, sums, filter_mid, filter_out)


def run_receive(query, key, value, grad, skip, field, **kw):
    block = spec((ROWS, SIDE))
    return call(receive_kernel, 1, [block] * 4 + [spec((1, SIDE)), spec((1024, SIDE))], [block] * 4,
                [out((ROWS, SIDE), BF16)] * 4, **kw)(query, key, value, grad, skip, field)


def run_finish(mine, other, **kw):
    shapes = [(16, ORDER), (ORDER, ORDER), (ORDER, SIDE), (1, SIDE), (1, SIDE)]
    return call(finish_kernel, 1, [spec((112, SIDE))] * 2, [spec(s) for s in shapes], [out(s) for s in shapes], **kw)(
        mine, other
    )


def exchanged(x, axis, distance):
    return lax.ppermute(x, axis, [(i, i ^ distance) for i in range(lax.axis_size(axis))])


def group_sum(x, axis, distances):
    values = [x] + [exchanged(x, axis, d) for d in distances]
    while len(values) > 1:
        values = [a + b for a, b in zip(values[::2], values[1::2])]
    return values[0]


def body(query, key, value, grad, filter_in, filter_mid, filter_out, decay_rate, skip_gain):
    decay = decay_rate.reshape(1, SIDE)
    skip = skip_gain.reshape(1, SIDE)
    features = lax.dynamic_slice_in_dim(jnp.asarray(feature_table()), HALF * (lax.axis_index("seq") % 2), HALF, axis=1)
    sent = run_send(query, key, value, grad).reshape(SEQ, SEQ, SIDE)
    field = lax.all_to_all(sent, "seq", 0, 0, tiled=True).reshape(1024, SIDE)
    *hidden, mine, theirs = run_filter(features, filter_in, filter_mid, filter_out)
    spectrum, filt, window = run_spectrum(mine, exchanged(theirs, "seq", 1), decay)
    sent, mine, theirs, sums = run_convolve(field, spectrum, filt, window, decay)
    field = lax.all_to_all(sent.reshape(SEQ, SEQ, SIDE), "seq", 0, 0, tiled=True).reshape(1024, SIDE)
    grads = run_backward(features, hidden, mine, exchanged(theirs, "seq", 1), sums, filter_mid, filter_out)
    output, grad_query, grad_key, grad_value = run_receive(query, key, value, grad, skip, field)
    shared = group_sum(group_sum(grads[:40], "chan", (1,)), "chan", (2, 6, 5))
    grads = jnp.concatenate([shared, grads[40:]])
    grads = group_sum(grads, "seq", (8, 16, 24))
    grads = group_sum(grads, "seq", (2, 4, 6))
    first, second, third, rates, gains = run_finish(grads, exchanged(grads, "seq", 1))
    return (output, grad_query, grad_key, grad_value, first, second, third, rates.reshape(SIDE), gains.reshape(SIDE))


def solution(mesh):
    wide = P("seq", "chan")
    return jax.shard_map(
        body,
        mesh=mesh,
        in_specs=(wide, wide, wide, wide, P(), P(), P(None, "chan"), P("chan"), P("chan")),
        out_specs=(wide, wide, wide, wide, P(), P(), P(None, "chan"), P("chan"), P("chan")),
        check_vma=False,
    )
```

```python
import functools
import math

import jax
import jax.numpy as jnp
import ml_dtypes
import numpy as np
from jax import lax
from jax.experimental import pallas as pl
from jax.experimental.pallas import tpu as pltpu
from jax.sharding import Mesh, PartitionSpec as P

F32 = jnp.float32
BF16 = jnp.bfloat16
LENGTH = 16384
SEQ = 32
ROWS = 512
SIDE = 128
OWN = 4
ORDER = 64
STEP = 2048
PIECE = 256
HALF = LENGTH // 2
MIB = 1 << 20
SEQ_AXES = ("x", "y", "core")


def split_table(table):
    high = table.astype(ml_dtypes.bfloat16)
    low = (table - high.astype(np.float64)).astype(ml_dtypes.bfloat16)
    return high, low


@functools.cache
def time_rows():
    p = np.arange(SIDE)
    return 4 * (p % SEQ) + p // SEQ


@functools.cache
def feature_table():
    t = (time_rows()[:, None] * SIDE + np.arange(SIDE)[None, :]).reshape(-1)
    rows = [t / LENGTH]
    angles = []
    for i in range(7):
        factor = max(1, LENGTH // 4 // 4 ** (6 - i))
        angles.append((factor * t % LENGTH) * (2.0 * math.pi / LENGTH))
    rows += [np.sin(a) for a in angles] + [np.cos(a) for a in angles] + [np.ones(LENGTH)]
    high, low = split_table(np.stack(rows).astype(np.float64))
    return np.concatenate([high, low])


@functools.cache
def transform_tables():
    idx = np.arange(SIDE)
    n1 = time_rows()
    first = np.exp(-2j * np.pi * ((n1[None, :] * idx[:, None] % SIDE) / SIDE + n1[None, :] / (4 * SIDE)))
    twiddle = np.exp(-2j * np.pi * idx[None, :] * (4 * idx[:, None] + 1) / (4 * LENGTH))
    second = np.exp(-2j * np.pi * (idx[:, None] * idx[None, :] % SIDE) / SIDE)
    high, low = split_table(np.concatenate([first.real, first.imag]))
    first_fwd = np.concatenate([high, high, low], axis=1)
    high, low = split_table(np.block([[second.real, second.imag], [-second.imag, second.real]]))
    second_fwd = np.concatenate([high, high, low])
    high, low = split_table(np.block([[second.real, -second.imag], [second.imag, second.real]]))
    second_inv = np.concatenate([high, high, low])
    high, low = split_table(np.concatenate([first.real.T, first.imag.T], axis=1) / LENGTH)
    first_inv = np.concatenate([high, high, low], axis=1)
    twiddle = np.concatenate([twiddle.real, twiddle.imag], axis=1).astype(np.float32)
    return first_fwd, second_fwd, twiddle, second_inv, first_inv


@functools.cache
def turn_polynomials():
    nodes = 0.5 * np.cos(np.pi * (np.arange(400) + 0.5) / 800)
    squares = nodes * nodes

    def fit(values, weight, count):
        basis = np.stack([squares**k for k in range(count)], axis=1)
        return np.linalg.lstsq(basis * weight[:, None], values, rcond=None)[0]

    sine = fit(np.sin(2 * np.pi * nodes), nodes, 6)
    cosine = fit(np.cos(2 * np.pi * nodes), np.ones_like(nodes), 7)
    return [float(c) for c in sine], [float(c) for c in cosine]


def sine_cosine(turns):
    sine, cosine = turn_polynomials()
    part = turns - jnp.round(turns)
    square = part * part
    s = jnp.full_like(square, sine[-1])
    for c in sine[-2::-1]:
        s = s * square + c
    c_out = jnp.full_like(square, cosine[-1])
    for c in cosine[-2::-1]:
        c_out = c_out * square + c
    return s * part, c_out


def halves(x):
    high = x.astype(BF16)
    return high, (x - high.astype(F32)).astype(BF16)


def dot(a, b):
    return jnp.dot(a, b, preferred_element_type=F32)


def dot_nt(a, b, precision=None):
    return lax.dot_general(a, b, (((1,), (1,)), ((), ())), precision=precision, preferred_element_type=F32)


def dot_tn(a, b, precision=None):
    return lax.dot_general(a, b, (((0,), (0,)), ((), ())), precision=precision, preferred_element_type=F32)


def data_left(x, axis):
    high, low = halves(x)
    return jnp.concatenate([high, low, high], axis=axis)


def weight_left(x, axis):
    high, low = halves(x)
    return jnp.concatenate([high, high, low], axis=axis)


def own_channels(place):
    row = lax.broadcasted_iota(jnp.int32, (8, SIDE), 0)
    lane = lax.broadcasted_iota(jnp.int32, (8, SIDE), 1)
    other = place + 1 - 2 * (place % 2)
    channel = jnp.where(row < OWN, place + SEQ * row, other + SEQ * (row - OWN))
    return jnp.where(lane == channel, 1.0, 0.0).astype(F32)


def position_grid():
    row = lax.broadcasted_iota(jnp.int32, (SIDE, SIDE), 0)
    lane = lax.broadcasted_iota(jnp.int32, (SIDE, SIDE), 1)
    return (ROWS * (row % SEQ) + SIDE * (row // SEQ) + lane).astype(F32)


def spec(shape, index=None):
    if index is None:
        zeros = (0,) * len(shape)
        return pl.BlockSpec(shape, lambda i: zeros)
    return pl.BlockSpec(shape, index)


def out(shape, dtype=F32):
    return jax.ShapeDtypeStruct(shape, dtype)


def in_hbm(x):
    return pltpu.with_memory_space_constraint(x, pltpu.HBM)


def call(kernel, grid, in_specs, out_specs, out_shape, scratch=(), limit=16, flops=1, nbytes=1, interpret=False):
    return pl.pallas_call(
        kernel,
        grid=(grid,),
        in_specs=in_specs,
        out_specs=out_specs,
        out_shape=out_shape,
        scratch_shapes=scratch,
        compiler_params=pltpu.CompilerParams(vmem_limit_bytes=limit * MIB),
        cost_estimate=pl.CostEstimate(flops=flops, bytes_accessed=nbytes, transcendentals=0),
        interpret=interpret,
    )


def send_kernel(query, key, value, grad, sent, held, sems):
    copies = [pltpu.make_async_copy(x, held.at[k], sems.at[k]) for k, x in enumerate((key, value, grad, query))]
    for copy in copies:
        copy.start()
    for offset, first, second in ((0, 0, 1), (OWN, 2, 3)):
        copies[first].wait()
        copies[second].wait()
        for h in range(ROWS // SIDE):
            rows = pl.ds(SIDE * h, SIDE)
            block = (held[first, rows, :].astype(F32) * held[second, rows, :].astype(F32)).T
            for c in range(OWN):
                sent[pl.ds(8 * h + offset + c, SEQ, stride=SEQ), :] = block[SEQ * c : SEQ * (c + 1), :]


def receive_kernel(query, key, value, grad, skip, field, output, grad_query, grad_key, grad_value):
    for h in range(ROWS // SIDE):
        rows = pl.ds(SIDE * h, SIDE)
        query_wide = query[rows, :].astype(F32)
        key_wide = key[rows, :].astype(F32)
        value_wide = value[rows, :].astype(F32)
        grad_wide = grad[rows, :].astype(F32)
        conv, back = (
            jnp.concatenate([field[pl.ds(8 * h + offset + c, SEQ, stride=SEQ), :] for c in range(OWN)]).T
            for offset in (0, OWN)
        )
        mixed = conv + skip[...] * (key_wide * value_wide)
        output[rows, :] = (query_wide * mixed).astype(BF16)
        grad_query[rows, :] = (grad_wide * mixed).astype(BF16)
        dgated = back + skip[...] * (grad_wide * query_wide)
        grad_key[rows, :] = (dgated * value_wide).astype(BF16)
        grad_value[rows, :] = (dgated * key_wide).astype(BF16)


def forward_rows(fields, first_fwd, second_fwd, twiddle):
    cos, sin = twiddle[:, :SIDE], twiddle[:, SIDE:]
    turned = []
    for pair in range(0, len(fields), 2):
        stage = dot(first_fwd[...], data_left(jnp.concatenate(fields[pair : pair + 2], axis=1), 0))
        for k in range(2):
            re = stage[:SIDE, SIDE * k : SIDE * (k + 1)]
            im = stage[SIDE:, SIDE * k : SIDE * (k + 1)]
            turned.append(data_left(jnp.concatenate([re * cos - im * sin, re * sin + im * cos], axis=1), 1))
    return dot(jnp.concatenate(turned), second_fwd[...])


def inverse_rows(spectra, first_inv, second_inv, twiddle):
    cos, sin = twiddle[:, :SIDE], twiddle[:, SIDE:]
    stage = dot(jnp.concatenate([data_left(s, 1) for s in spectra]), second_inv[...])
    turned = []
    for k in range(len(spectra)):
        re = stage[SIDE * k : SIDE * (k + 1), :SIDE]
        im = stage[SIDE * k : SIDE * (k + 1), SIDE:]
        turned.append(jnp.concatenate([re * cos + im * sin, im * cos - re * sin]))
    fields = []
    for pair in range(0, len(spectra), 2):
        both = dot(first_inv[...], data_left(jnp.concatenate(turned[pair : pair + 2], axis=1), 0))
        fields += [both[:, :SIDE], both[:, SIDE:]]
    return fields


def filter_kernel(place, features, filter_in, filter_mid, filter_out,
                  h1_high, h1_low, cos1, h2_high, h2_low, cos2, mine, theirs, shaped):
    step = pl.program_id(0)
    own = own_channels(place())
    turn = 1.0 / (2.0 * math.pi)
    in_high, in_low = halves(filter_in[...].T * turn)
    weight1 = jnp.concatenate([in_high, in_low, in_high], axis=1)
    weight2 = weight_left(filter_mid[...].T * turn, 1)
    weight3 = weight_left(dot_nt(own, filter_out[...], lax.Precision.HIGHEST), 1)
    pieces = [pl.ds(PIECE * k, PIECE) for k in range(STEP // PIECE)]
    for piece in pieces:
        feature = features[:, piece]
        rows = jnp.concatenate([feature[:16], feature[:16], feature[16:]])
        sine, cosine = sine_cosine(dot(weight1, rows))
        cos1[:, piece] = cosine
        h1_high[:, piece], h1_low[:, piece] = halves(sine)
    for piece in pieces:
        high = h1_high[:, piece]
        sine, cosine = sine_cosine(dot(weight2, jnp.concatenate([high, h1_low[:, piece], high])))
        cos2[:, piece] = cosine
        h2_high[:, piece], h2_low[:, piece] = halves(sine)
    for k, piece in enumerate(pieces):
        high = h2_high[:, piece]
        values = dot(weight3, jnp.concatenate([high, h2_low[:, piece], high]))
        for m in range(PIECE // SIDE):
            row = 8 * (step * (STEP // SIDE) + k * (PIECE // SIDE) + m)
            shaped[pl.ds(pl.multiple_of(row, 8), 8), :] = values[:, SIDE * m : SIDE * (m + 1)]

    @pl.when(step == HALF // STEP - 1)
    def _():
        for c in range(OWN):
            mine[pl.ds(64 * c, 64), :] = shaped[pl.ds(c, 64, stride=8), :]
            theirs[pl.ds(64 * c, 64), :] = shaped[pl.ds(c + OWN, 64, stride=8), :]


def filter_fields(me, mine, other, decay):
    time = position_grid()
    lower = me % 2 == 0
    rates = jnp.sum(own_channels(me) * decay[...], axis=1, keepdims=True)
    for c in range(OWN):
        rate = rates[c : c + 1, :]
        window = jnp.exp(-rate * time) * jnp.sqrt(rate + 1.0 / LENGTH)
        here, there = mine[pl.ds(64 * c, 64), :], other[pl.ds(64 * c, 64), :]
        yield window, jnp.concatenate([jnp.where(lower, here, there), jnp.where(lower, there, here)]), rate


def spectrum_kernel(place, mine, other, decay, first_fwd, second_fwd, twiddle, spectrum):
    fields = [window * shaped for window, shaped, _ in filter_fields(place(), mine, other, decay)]
    spectrum[...] = forward_rows(fields, first_fwd, second_fwd, twiddle)


def convolve_kernel(place, field, spectrum, shaped_mine, shaped_other, decay, first_fwd, second_fwd, twiddle, second_inv,
                    first_inv, sent, mine, theirs, sums):
    fields = []
    for c in range(OWN):
        for offset in (0, OWN):
            fields.append(
                jnp.concatenate([field[pl.ds(8 * h + offset + c, SEQ, stride=SEQ), :] for h in range(ROWS // SIDE)])
            )
    spectra = forward_rows(fields, first_fwd, second_fwd, twiddle)
    products = []
    for c in range(OWN):
        gated, incoming = (spectra[SIDE * k : SIDE * (k + 1)] for k in (2 * c, 2 * c + 1))
        kernel = spectrum[pl.ds(SIDE * c, SIDE), :]
        gated_re, gated_im = gated[:, :SIDE], gated[:, SIDE:]
        incoming_re, incoming_im = incoming[:, :SIDE], incoming[:, SIDE:]
        kernel_re, kernel_im = kernel[:, :SIDE], kernel[:, SIDE:]
        products.append((
            jnp.concatenate([kernel_re * gated_re - kernel_im * gated_im,
                             kernel_re * gated_im + kernel_im * gated_re], axis=1),
            jnp.concatenate([kernel_re * incoming_re + kernel_im * incoming_im,
                             kernel_re * incoming_im - kernel_im * incoming_re], axis=1),
            jnp.concatenate([gated_re * incoming_re + gated_im * incoming_im,
                             gated_re * incoming_im - gated_im * incoming_re], axis=1),
        ))
    results = inverse_rows([p for c in range(OWN) for p in products[c][:2]] + [products[c][2] for c in range(OWN)],
                           first_inv, second_inv, twiddle)
    time = position_grid()
    me = place()
    lower = me % 2 == 0
    pair = lambda x: (jnp.where(lower, x, 0.0), jnp.where(lower, 0.0, x))
    for c, (window, shaped, rate) in enumerate(filter_fields(me, shaped_mine, shaped_other, decay)):
        for offset, result in ((0, results[2 * c]), (OWN, results[2 * c + 1])):
            for h in range(ROWS // SIDE):
                sent[pl.ds(8 * h + offset + c, SEQ, stride=SEQ), :] = result[SEQ * h : SEQ * (h + 1), :]
        dshaped = results[2 * OWN + c] * window
        slope = 0.5 / (rate + 1.0 / LENGTH) - time
        for part, sum_row, value in (
            (mine, None, jnp.where(lower, dshaped[:64], dshaped[64:])),
            (theirs, None, jnp.where(lower, dshaped[64:], dshaped[:64])),
            (sums, 0, jnp.sum(dshaped * shaped * slope, axis=0, keepdims=True)),
            (sums, 8, jnp.sum(fields[2 * c] * fields[2 * c + 1], axis=0, keepdims=True)),
        ):
            for offset, v in zip((0, OWN), pair(value)):
                rows = pl.ds(c + offset, 64, stride=8) if sum_row is None else pl.ds(sum_row + c + offset, 1)
                part[rows, :] = v


def pair_channels(place):
    row = lax.broadcasted_iota(jnp.int32, (8, SIDE), 0)
    lane = lax.broadcasted_iota(jnp.int32, (8, SIDE), 1)
    return jnp.where(lane == place - place % 2 + row // OWN + SEQ * (row % OWN), 1.0, 0.0).astype(F32)


def backward_kernel(place, features, h1_high, h1_low, cos1, h2_high, h2_low, cos2, mine, other, sums, filter_mid, filter_out,
                    grads, total, d2_high, d2_low, d1_high, d1_low):
    step = pl.program_id(0)
    weight3 = weight_left(dot_nt(filter_out[...], pair_channels(place()), lax.Precision.HIGHEST), 1)
    weight2 = weight_left(filter_mid[...], 1)
    pieces = [pl.ds(PIECE * k, PIECE) for k in range(STEP // PIECE)]
    shaped_high, shaped_low = halves(
        jnp.concatenate([mine[pl.ds(8 * m, 8), :] + other[pl.ds(8 * m, 8), :] for m in range(STEP // SIDE)], axis=1)
    )
    for k, piece in enumerate(pieces):
        part = slice(PIECE * k, PIECE * (k + 1))
        rows = jnp.concatenate([shaped_high[:, part], shaped_low[:, part], shaped_high[:, part]])
        d2_high[:, piece], d2_low[:, piece] = halves(dot(weight3, rows) * cos2[:, piece])
    for piece in pieces:
        high = d2_high[:, piece]
        d1_high[:, piece], d1_low[:, piece] = halves(
            dot(weight2, jnp.concatenate([high, d2_low[:, piece], high])) * cos1[:, piece]
        )
    left = jnp.concatenate([h1_high[...], h1_low[...], h2_high[...], h2_low[...], d1_high[...], d1_low[...]])
    right = jnp.concatenate([d2_high[...], d2_low[...], shaped_high, shaped_low, features[...]])
    product = dot_nt(left, right)

    @pl.when(step == 0)
    def _():
        total[...] = product

    @pl.when(step > 0)
    def _():
        total[...] += product

    @pl.when(step == HALF // STEP - 1)
    def _():
        mid = total[:64, :64] + (total[:64, 64:128] + total[64:128, :64])
        grads[pl.ds(0, 32), :] = jnp.concatenate([mid[:32], mid[32:]], axis=1)
        side = [jnp.concatenate([total[64 * k : 64 * (k + 1), 128:], jnp.zeros((64, 80), F32)], axis=1).T for k in range(2, 6)]
        first = side[2][16:32] + (side[2][32:48] + side[3][16:32])
        third = side[0][:8] + (side[0][8:16] + side[1][:8])
        grads[pl.ds(32, 8), :] = jnp.concatenate([first[:8], first[8:]], axis=1)
        lane = lax.broadcasted_iota(jnp.int32, (8, SIDE), 1)
        rates = jnp.sum(sums[pl.ds(0, 8), :], axis=1, keepdims=True)
        gains = jnp.sum(sums[pl.ds(8, 8), :], axis=1, keepdims=True)
        grads[pl.ds(40, 8), :] = jnp.concatenate([third, jnp.zeros((8, 64), F32)], axis=1) + (
            jnp.where(lane == 64, rates, 0.0) + jnp.where(lane == 65, gains, 0.0)
        )


def finish_kernel(gathered, grad_in, grad_mid, grad_out, grad_decay, grad_skip):
    shared = gathered[pl.ds(0, 40), :]
    for chip in range(1, 16):
        shared = shared + gathered[pl.ds(48 * chip, 40), :]
    grad_mid[pl.ds(0, 32), :] = shared[:32, :ORDER]
    grad_mid[pl.ds(32, 32), :] = shared[:32, ORDER:]
    grad_in[pl.ds(0, 8), :] = shared[32:, :ORDER]
    grad_in[pl.ds(8, 8), :] = shared[32:, ORDER:]
    row = lax.broadcasted_iota(jnp.int32, (SIDE, SIDE), 0)
    lane = lax.broadcasted_iota(jnp.int32, (SIDE, SIDE), 1)
    moved = jnp.where(lane == 2 * (row // 8) + row % 8 // OWN + SEQ * (row % OWN), 1.0, 0.0).astype(F32)
    rows = jnp.concatenate([gathered[pl.ds(48 * chip + 40, 8), :] for chip in range(16)])
    channels = dot_tn(rows, moved, lax.Precision.HIGHEST)
    grad_out[...] = channels[:64]
    grad_decay[...] = channels[64:65]
    grad_skip[...] = channels[65:66]


def seq_place():
    return lax.axis_index(SEQ_AXES)


def run_send(query, key, value, grad, **kw):
    return call(
        send_kernel, 1, [pl.BlockSpec(memory_space=pltpu.HBM)] * 4, spec((1024, SIDE)), out((1024, SIDE)),
        scratch=[pltpu.VMEM((4, ROWS, SIDE), BF16), pltpu.SemaphoreType.DMA((4,))], **kw,
    )(*[in_hbm(x) for x in (query, key, value, grad)])


def run_filter(features, filter_in, filter_mid, filter_out, place=seq_place, **kw):
    wide = lambda i: (0, i)
    hidden = spec((ORDER, STEP), wide)
    half, full = pltpu.HBM((ORDER, HALF), BF16), pltpu.HBM((ORDER, HALF), F32)
    return call(
        functools.partial(filter_kernel, place),
        HALF // STEP,
        [spec((32, STEP), wide), spec((16, ORDER)), spec((ORDER, ORDER)), spec((ORDER, SIDE))],
        [hidden] * 6 + [spec((256, SIDE))] * 2,
        [half, half, full, half, half, full, out((256, SIDE)), out((256, SIDE))],
        scratch=[pltpu.VMEM((512, SIDE), F32)],
        flops=4 * 10**9, nbytes=10 * MIB, **kw,
    )(features, filter_in, filter_mid, filter_out)


def run_spectrum(mine, other, decay, place=seq_place, **kw):
    first_fwd, second_fwd, twiddle, _, _ = transform_tables()
    return call(
        functools.partial(spectrum_kernel, place),
        1,
        [spec((256, SIDE))] * 2 + [spec((1, SIDE)), spec((256, 384)), spec((768, 256)), spec((SIDE, 256))],
        spec((512, 256)),
        out((512, 256)),
        flops=10**9, nbytes=MIB, **kw,
    )(mine, other, decay, first_fwd, second_fwd, twiddle)


def run_convolve(field, spectrum, mine, other, decay, place=seq_place, **kw):
    first_fwd, second_fwd, twiddle, second_inv, first_inv = transform_tables()
    return call(
        functools.partial(convolve_kernel, place),
        1,
        [spec((1024, SIDE)), spec((512, 256)), spec((256, SIDE)), spec((256, SIDE)), spec((1, SIDE)),
         spec((256, 384)), spec((768, 256)), spec((SIDE, 256)), spec((768, 256)), spec((SIDE, 768))],
        [spec((1024, SIDE)), spec((512, SIDE)), spec((512, SIDE)), spec((16, SIDE))],
        [out((1024, SIDE)), out((512, SIDE)), out((512, SIDE)), out((16, SIDE))],
        flops=4 * 10**9, nbytes=4 * MIB, **kw,
    )(field, spectrum, mine, other, decay, first_fwd, second_fwd, twiddle, second_inv, first_inv)


def run_backward(features, hidden, mine, other, sums, filter_mid, filter_out, place=seq_place, **kw):
    wide = lambda i: (0, i)
    block = spec((ORDER, STEP), wide)
    deep = spec((STEP // 16, SIDE), lambda i: (i, 0))
    return call(
        functools.partial(backward_kernel, place),
        HALF // STEP,
        [spec((32, STEP), wide)] + [block] * 6 + [deep, deep, spec((16, SIDE)), spec((ORDER, ORDER)), spec((ORDER, SIDE))],
        spec((48, SIDE)),
        out((48, SIDE)),
        scratch=[pltpu.VMEM((384, 176), F32)] + [pltpu.VMEM((ORDER, STEP), BF16)] * 4,
        flops=4 * 10**9, nbytes=10 * MIB, **kw,
    )(features, *[in_hbm(x) for x in hidden], mine, other, sums, filter_mid, filter_out)


def run_receive(query, key, value, grad, skip, field, **kw):
    block = spec((ROWS, SIDE))
    return call(receive_kernel, 1, [block] * 4 + [spec((1, SIDE)), spec((1024, SIDE))], [block] * 4,
                [out((ROWS, SIDE), BF16)] * 4, **kw)(query, key, value, grad, skip, field)


def run_finish(gathered, **kw):
    shapes = [(16, ORDER), (ORDER, ORDER), (ORDER, SIDE), (1, SIDE), (1, SIDE)]
    return call(finish_kernel, 1, [spec((768, SIDE))], [spec(s) for s in shapes], [out(s) for s in shapes], **kw)(gathered)


def exchanged(x, axis, distance):
    return lax.ppermute(x, axis, [(i, i ^ distance) for i in range(lax.axis_size(axis))])


def group_sum(x, axis, distances):
    values = [x] + [exchanged(x, axis, d) for d in distances]
    while len(values) > 1:
        values = [a + b for a, b in zip(values[::2], values[1::2])]
    return values[0]


def body(query, key, value, grad, filter_in, filter_mid, filter_out, decay_rate, skip_gain):
    decay = decay_rate.reshape(1, SIDE)
    skip = skip_gain.reshape(1, SIDE)
    core = lax.axis_index("core")
    features = lax.dynamic_slice_in_dim(jnp.asarray(feature_table()), HALF * core, HALF, axis=1)
    sent = run_send(query, key, value, grad).reshape(SEQ, SEQ, SIDE)
    field = lax.all_to_all(sent, SEQ_AXES, 0, 0, tiled=True).reshape(1024, SIDE)
    *hidden, mine, theirs = run_filter(features, filter_in, filter_mid, filter_out)
    other = exchanged(theirs, "core", 1)
    spectrum = run_spectrum(mine, other, decay)
    sent, mine, theirs, sums = run_convolve(field, spectrum, mine, other, decay)
    field = lax.all_to_all(sent.reshape(SEQ, SEQ, SIDE), SEQ_AXES, 0, 0, tiled=True).reshape(1024, SIDE)
    grads = run_backward(features, hidden, mine, exchanged(theirs, "core", 1), sums, filter_mid, filter_out)
    grads = group_sum(grads, "core", (1,))
    shared = group_sum(grads[:40], "chan", (1, 2, 3))
    shared, field = lax.optimization_barrier((shared, field))
    shared = group_sum(shared, "chan", (6,))
    grads = jnp.broadcast_to(jnp.concatenate([shared, grads[40:]])[None], (16, 48, SIDE))
    gathered = lax.all_to_all(grads, ("x", "y"), 0, 0, tiled=True).reshape(768, SIDE)
    output, grad_query, grad_key, grad_value = run_receive(query, key, value, grad, skip, field)
    first, second, third, rates, gains = run_finish(gathered)
    return (output, grad_query, grad_key, grad_value, first, second, third, rates.reshape(SIDE), gains.reshape(SIDE))


def solution(mesh):
    parts = Mesh(mesh.devices.reshape(4, 4, 2, 8), SEQ_AXES + ("chan",))
    wide = P(SEQ_AXES, "chan")
    return jax.shard_map(
        body,
        mesh=parts,
        in_specs=(wide, wide, wide, wide, P(), P(), P(None, "chan"), P("chan"), P("chan")),
        out_specs=(wide, wide, wide, wide, P(), P(), P(None, "chan"), P("chan"), P("chan")),
        check_vma=False,
    )
```

```python
import functools
import math

import jax
import jax.numpy as jnp
import ml_dtypes
import numpy as np
from jax import lax
from jax.experimental import pallas as pl
from jax.experimental.pallas import tpu as pltpu
from jax.sharding import Mesh, PartitionSpec as P

F32 = jnp.float32
BF16 = jnp.bfloat16
LENGTH = 16384
SEQ = 32
ROWS = 512
SIDE = 128
OWN = 4
ORDER = 64
STEP = 2048
PIECE = 256
BACK = 4096
HALF = LENGTH // 2
MIB = 1 << 20
SEQ_AXES = ("x", "y", "core")


def split_table(table):
    high = table.astype(ml_dtypes.bfloat16)
    low = (table - high.astype(np.float64)).astype(ml_dtypes.bfloat16)
    return high, low


@functools.cache
def time_rows():
    p = np.arange(SIDE)
    return 4 * (p % SEQ) + p // SEQ


@functools.cache
def feature_table():
    t = (time_rows()[:, None] * SIDE + np.arange(SIDE)[None, :]).reshape(-1)
    rows = [t / LENGTH]
    angles = []
    for i in range(7):
        factor = max(1, LENGTH // 4 // 4 ** (6 - i))
        angles.append((factor * t % LENGTH) * (2.0 * math.pi / LENGTH))
    rows += [np.sin(a) for a in angles] + [np.cos(a) for a in angles] + [np.ones(LENGTH)]
    high, low = split_table(np.stack(rows).astype(np.float64))
    return np.concatenate([high, low])


@functools.cache
def transform_tables():
    idx = np.arange(SIDE)
    n1 = time_rows()
    first = np.exp(-2j * np.pi * ((n1[None, :] * idx[:, None] % SIDE) / SIDE + n1[None, :] / (4 * SIDE)))
    twiddle = np.exp(-2j * np.pi * idx[None, :] * (4 * idx[:, None] + 1) / (4 * LENGTH))
    second = np.exp(-2j * np.pi * (idx[:, None] * idx[None, :] % SIDE) / SIDE)
    high, low = split_table(np.concatenate([first.real, first.imag]))
    first_fwd = np.concatenate([high, high, low], axis=1)
    high, low = split_table(np.block([[second.real, second.imag], [-second.imag, second.real]]))
    second_fwd = np.concatenate([high, high, low])
    high, low = split_table(np.block([[second.real, -second.imag], [second.imag, second.real]]))
    second_inv = np.concatenate([high, high, low])
    high, low = split_table(np.concatenate([first.real.T, first.imag.T], axis=1) / LENGTH)
    first_inv = np.concatenate([high, high, low], axis=1)
    twiddle = np.concatenate([twiddle.real, twiddle.imag], axis=1).astype(np.float32)
    return first_fwd, second_fwd, twiddle, second_inv, first_inv


@functools.cache
def turn_polynomials():
    nodes = 0.5 * np.cos(np.pi * (np.arange(400) + 0.5) / 800)
    squares = nodes * nodes

    def fit(values, weight, count):
        basis = np.stack([squares**k for k in range(count)], axis=1)
        return np.linalg.lstsq(basis * weight[:, None], values, rcond=None)[0]

    sine = fit(np.sin(2 * np.pi * nodes), nodes, 6)
    cosine = fit(np.cos(2 * np.pi * nodes), np.ones_like(nodes), 7)
    return [float(c) for c in sine], [float(c) for c in cosine]


def sine_cosine(turns):
    sine, cosine = turn_polynomials()
    part = turns - jnp.round(turns)
    square = part * part
    s = jnp.full_like(square, sine[-1])
    for c in sine[-2::-1]:
        s = s * square + c
    c_out = jnp.full_like(square, cosine[-1])
    for c in cosine[-2::-1]:
        c_out = c_out * square + c
    return s * part, c_out


def halves(x):
    high = x.astype(BF16)
    return high, (x - high.astype(F32)).astype(BF16)


def dot(a, b):
    return jnp.dot(a, b, preferred_element_type=F32)


def dot_nt(a, b, precision=None):
    return lax.dot_general(a, b, (((1,), (1,)), ((), ())), precision=precision, preferred_element_type=F32)


def dot_tn(a, b, precision=None):
    return lax.dot_general(a, b, (((0,), (0,)), ((), ())), precision=precision, preferred_element_type=F32)


def data_left(x, axis):
    high, low = halves(x)
    return jnp.concatenate([high, low, high], axis=axis)


def weight_left(x, axis):
    high, low = halves(x)
    return jnp.concatenate([high, high, low], axis=axis)


def picked(filter_out, channels):
    return dot_nt(jnp.concatenate(halves(filter_out[...])), channels.astype(BF16))


def own_channels(place):
    row = lax.broadcasted_iota(jnp.int32, (8, SIDE), 0)
    lane = lax.broadcasted_iota(jnp.int32, (8, SIDE), 1)
    other = place + 1 - 2 * (place % 2)
    channel = jnp.where(row < OWN, place + SEQ * row, other + SEQ * (row - OWN))
    return jnp.where(lane == channel, 1.0, 0.0).astype(F32)


def position_grid():
    row = lax.broadcasted_iota(jnp.int32, (SIDE, SIDE), 0)
    lane = lax.broadcasted_iota(jnp.int32, (SIDE, SIDE), 1)
    return (ROWS * (row % SEQ) + SIDE * (row // SEQ) + lane).astype(F32)


def spec(shape, index=None):
    if index is None:
        zeros = (0,) * len(shape)
        return pl.BlockSpec(shape, lambda i: zeros)
    return pl.BlockSpec(shape, index)


def out(shape, dtype=F32):
    return jax.ShapeDtypeStruct(shape, dtype)


def in_hbm(x):
    return pltpu.with_memory_space_constraint(x, pltpu.HBM)


def call(kernel, grid, in_specs, out_specs, out_shape, scratch=(), limit=16, flops=1, nbytes=1, interpret=False):
    return pl.pallas_call(
        kernel,
        grid=(grid,),
        in_specs=in_specs,
        out_specs=out_specs,
        out_shape=out_shape,
        scratch_shapes=scratch,
        compiler_params=pltpu.CompilerParams(vmem_limit_bytes=limit * MIB),
        cost_estimate=pl.CostEstimate(flops=flops, bytes_accessed=nbytes, transcendentals=0),
        interpret=interpret,
    )


def send_kernel(query, key, value, grad, sent, held, sems):
    copies = [pltpu.make_async_copy(x, held.at[k], sems.at[k]) for k, x in enumerate((key, value, grad, query))]
    for copy in copies:
        copy.start()
    for offset, first, second in ((0, 0, 1), (OWN, 2, 3)):
        copies[first].wait()
        copies[second].wait()
        for h in range(ROWS // SIDE):
            rows = pl.ds(SIDE * h, SIDE)
            block = (held[first, rows, :].astype(F32) * held[second, rows, :].astype(F32)).T
            for c in range(OWN):
                sent[pl.ds(8 * h + offset + c, SEQ, stride=SEQ), :] = block[SEQ * c : SEQ * (c + 1), :]


def receive_kernel(query, key, value, grad, skip, field, output, grad_query, grad_key, grad_value):
    for h in range(ROWS // SIDE):
        rows = pl.ds(SIDE * h, SIDE)
        query_wide = query[rows, :].astype(F32)
        key_wide = key[rows, :].astype(F32)
        value_wide = value[rows, :].astype(F32)
        grad_wide = grad[rows, :].astype(F32)
        conv, back = (
            jnp.concatenate([field[pl.ds(8 * h + offset + c, SEQ, stride=SEQ), :] for c in range(OWN)]).T
            for offset in (0, OWN)
        )
        mixed = conv + skip[...] * (key_wide * value_wide)
        output[rows, :] = (query_wide * mixed).astype(BF16)
        grad_query[rows, :] = (grad_wide * mixed).astype(BF16)
        dgated = back + skip[...] * (grad_wide * query_wide)
        grad_key[rows, :] = (dgated * value_wide).astype(BF16)
        grad_value[rows, :] = (dgated * key_wide).astype(BF16)


def forward_rows(fields, first_fwd, second_fwd, twiddle):
    cos, sin = twiddle[:, :SIDE], twiddle[:, SIDE:]
    turned = []
    for pair in range(0, len(fields), 2):
        stage = dot(first_fwd[...], data_left(jnp.concatenate(fields[pair : pair + 2], axis=1), 0))
        for k in range(2):
            re = stage[:SIDE, SIDE * k : SIDE * (k + 1)]
            im = stage[SIDE:, SIDE * k : SIDE * (k + 1)]
            turned.append(data_left(jnp.concatenate([re * cos - im * sin, re * sin + im * cos], axis=1), 1))
    return dot(jnp.concatenate(turned), second_fwd[...])


def inverse_rows(spectra, first_inv, second_inv, twiddle):
    cos, sin = twiddle[:, :SIDE], twiddle[:, SIDE:]
    stage = dot(jnp.concatenate([data_left(s, 1) for s in spectra]), second_inv[...])
    turned = []
    for k in range(len(spectra)):
        re = stage[SIDE * k : SIDE * (k + 1), :SIDE]
        im = stage[SIDE * k : SIDE * (k + 1), SIDE:]
        turned.append(jnp.concatenate([re * cos + im * sin, im * cos - re * sin]))
    fields = []
    for pair in range(0, len(spectra), 2):
        both = dot(first_inv[...], data_left(jnp.concatenate(turned[pair : pair + 2], axis=1), 0))
        fields += [both[:, :SIDE], both[:, SIDE:]]
    return fields


def filter_kernel(place, features, filter_in, filter_mid, filter_out,
                  h1_high, h1_low, cos1, h2_high, h2_low, cos2, mine, theirs, shaped):
    step = pl.program_id(0)
    own = own_channels(place())
    turn = 1.0 / (2.0 * math.pi)
    in_high, in_low = halves(filter_in[...].T * turn)
    weight1 = jnp.concatenate([in_high, in_low, in_high], axis=1)
    weight2 = weight_left(filter_mid[...].T * turn, 1)
    weight3 = picked(filter_out, own).T.astype(BF16)
    weight3 = jnp.concatenate([weight3[:, :64], weight3[:, :64], weight3[:, 64:]], axis=1)
    pieces = [pl.ds(PIECE * k, PIECE) for k in range(STEP // PIECE)]
    for piece in pieces:
        feature = features[:, piece]
        rows = jnp.concatenate([feature[:16], feature[:16], feature[16:]])
        sine, cosine = sine_cosine(dot(weight1, rows))
        cos1[:, piece] = cosine
        h1_high[:, piece], h1_low[:, piece] = halves(sine)
    for piece in pieces:
        high = h1_high[:, piece]
        sine, cosine = sine_cosine(dot(weight2, jnp.concatenate([high, h1_low[:, piece], high])))
        cos2[:, piece] = cosine
        h2_high[:, piece], h2_low[:, piece] = halves(sine)
    for k, piece in enumerate(pieces):
        high = h2_high[:, piece]
        values = dot(weight3, jnp.concatenate([high, h2_low[:, piece], high]))
        for m in range(PIECE // SIDE):
            row = 8 * (step * (STEP // SIDE) + k * (PIECE // SIDE) + m)
            shaped[pl.ds(pl.multiple_of(row, 8), 8), :] = values[:, SIDE * m : SIDE * (m + 1)]

    @pl.when(step == HALF // STEP - 1)
    def _():
        for c in range(OWN):
            mine[pl.ds(64 * c, 64), :] = shaped[pl.ds(c, 64, stride=8), :]
            theirs[pl.ds(64 * c, 64), :] = shaped[pl.ds(c + OWN, 64, stride=8), :]


def filter_fields(me, mine, other, decay):
    time = position_grid()
    lower = me % 2 == 0
    rates = jnp.sum(own_channels(me) * decay[...], axis=1, keepdims=True)
    for c in range(OWN):
        rate = rates[c : c + 1, :]
        window = jnp.exp(-rate * time) * jnp.sqrt(rate + 1.0 / LENGTH)
        here, there = mine[pl.ds(64 * c, 64), :], other[pl.ds(64 * c, 64), :]
        yield window, jnp.concatenate([jnp.where(lower, here, there), jnp.where(lower, there, here)]), rate


def spectrum_kernel(place, mine, other, decay, first_fwd, second_fwd, twiddle, spectrum):
    fields = [window * shaped for window, shaped, _ in filter_fields(place(), mine, other, decay)]
    spectrum[...] = forward_rows(fields, first_fwd, second_fwd, twiddle)


def convolve_kernel(place, field, spectrum, shaped_mine, shaped_other, decay, first_fwd, second_fwd, twiddle, second_inv,
                    first_inv, sent, mine, theirs, sums):
    fields = []
    for c in range(OWN):
        for offset in (0, OWN):
            fields.append(
                jnp.concatenate([field[pl.ds(8 * h + offset + c, SEQ, stride=SEQ), :] for h in range(ROWS // SIDE)])
            )
    spectra = forward_rows(fields, first_fwd, second_fwd, twiddle)
    products = []
    for c in range(OWN):
        gated, incoming = (spectra[SIDE * k : SIDE * (k + 1)] for k in (2 * c, 2 * c + 1))
        kernel = spectrum[pl.ds(SIDE * c, SIDE), :]
        gated_re, gated_im = gated[:, :SIDE], gated[:, SIDE:]
        incoming_re, incoming_im = incoming[:, :SIDE], incoming[:, SIDE:]
        kernel_re, kernel_im = kernel[:, :SIDE], kernel[:, SIDE:]
        products.append((
            jnp.concatenate([kernel_re * gated_re - kernel_im * gated_im,
                             kernel_re * gated_im + kernel_im * gated_re], axis=1),
            jnp.concatenate([kernel_re * incoming_re + kernel_im * incoming_im,
                             kernel_re * incoming_im - kernel_im * incoming_re], axis=1),
            jnp.concatenate([gated_re * incoming_re + gated_im * incoming_im,
                             gated_re * incoming_im - gated_im * incoming_re], axis=1),
        ))
    results = inverse_rows([p for c in range(OWN) for p in products[c][:2]] + [products[c][2] for c in range(OWN)],
                           first_inv, second_inv, twiddle)
    time = position_grid()
    me = place()
    lower = me % 2 == 0
    pair = lambda x: (jnp.where(lower, x, 0.0), jnp.where(lower, 0.0, x))
    for c, (window, shaped, rate) in enumerate(filter_fields(me, shaped_mine, shaped_other, decay)):
        for offset, result in ((0, results[2 * c]), (OWN, results[2 * c + 1])):
            for h in range(ROWS // SIDE):
                sent[pl.ds(8 * h + offset + c, SEQ, stride=SEQ), :] = result[SEQ * h : SEQ * (h + 1), :]
        dshaped = results[2 * OWN + c] * window
        slope = 0.5 / (rate + 1.0 / LENGTH) - time
        for part, sum_row, value in (
            (mine, None, jnp.where(lower, dshaped[:64], dshaped[64:])),
            (theirs, None, jnp.where(lower, dshaped[64:], dshaped[:64])),
            (sums, 0, jnp.sum(dshaped * shaped * slope, axis=0, keepdims=True)),
            (sums, 8, jnp.sum(fields[2 * c] * fields[2 * c + 1], axis=0, keepdims=True)),
        ):
            for offset, v in zip((0, OWN), pair(value)):
                rows = pl.ds(c + offset, 64, stride=8) if sum_row is None else pl.ds(sum_row + c + offset, 1)
                part[rows, :] = v


def pair_channels(place):
    row = lax.broadcasted_iota(jnp.int32, (8, SIDE), 0)
    lane = lax.broadcasted_iota(jnp.int32, (8, SIDE), 1)
    return jnp.where(lane == place - place % 2 + row // OWN + SEQ * (row % OWN), 1.0, 0.0).astype(F32)


def backward_kernel(place, features, h1_high, h1_low, cos1, h2_high, h2_low, cos2, mine, other, sums, filter_mid, filter_out,
                    grads, total, d2_high, d2_low, d1_high, d1_low):
    step = pl.program_id(0)
    weight3 = picked(filter_out, pair_channels(place())).astype(BF16)
    weight3 = jnp.concatenate([weight3[:64], weight3[:64], weight3[64:]], axis=1)
    weight2 = weight_left(filter_mid[...], 1)
    pieces = [pl.ds(PIECE * k, PIECE) for k in range(BACK // PIECE)]
    shaped_high, shaped_low = halves(
        jnp.concatenate([mine[pl.ds(8 * m, 8), :] + other[pl.ds(8 * m, 8), :] for m in range(BACK // SIDE)], axis=1)
    )
    for k, piece in enumerate(pieces):
        part = slice(PIECE * k, PIECE * (k + 1))
        rows = jnp.concatenate([shaped_high[:, part], shaped_low[:, part], shaped_high[:, part]])
        d2_high[:, piece], d2_low[:, piece] = halves(dot(weight3, rows) * cos2[:, piece])
    for piece in pieces:
        high = d2_high[:, piece]
        d1_high[:, piece], d1_low[:, piece] = halves(
            dot(weight2, jnp.concatenate([high, d2_low[:, piece], high])) * cos1[:, piece]
        )
    left = jnp.concatenate([h1_high[...], h1_low[...], h2_high[...], h2_low[...], d1_high[...], d1_low[...]])
    right = jnp.concatenate([d2_high[...], d2_low[...], shaped_high, shaped_low, features[...]])
    product = dot_nt(left, right)

    @pl.when(step == 0)
    def _():
        total[...] = product

    @pl.when(step > 0)
    def _():
        total[...] += product

    @pl.when(step == HALF // BACK - 1)
    def _():
        mid = total[:64, :64] + (total[:64, 64:128] + total[64:128, :64])
        grads[pl.ds(0, 32), :] = jnp.concatenate([mid[:32], mid[32:]], axis=1)
        side = [jnp.concatenate([total[64 * k : 64 * (k + 1), 128:], jnp.zeros((64, 80), F32)], axis=1).T for k in range(2, 6)]
        first = side[2][16:32] + (side[2][32:48] + side[3][16:32])
        third = side[0][:8] + (side[0][8:16] + side[1][:8])
        grads[pl.ds(32, 8), :] = jnp.concatenate([first[:8], first[8:]], axis=1)
        lane = lax.broadcasted_iota(jnp.int32, (8, SIDE), 1)
        rates = jnp.sum(sums[pl.ds(0, 8), :], axis=1, keepdims=True)
        gains = jnp.sum(sums[pl.ds(8, 8), :], axis=1, keepdims=True)
        grads[pl.ds(40, 8), :] = jnp.concatenate([third, jnp.zeros((8, 64), F32)], axis=1) + (
            jnp.where(lane == 64, rates, 0.0) + jnp.where(lane == 65, gains, 0.0)
        )


def finish_kernel(gathered, grad_in, grad_mid, grad_out, grad_decay, grad_skip):
    shared = gathered[pl.ds(0, 40), :]
    for chip in range(1, 16):
        shared = shared + gathered[pl.ds(48 * chip, 40), :]
    grad_mid[pl.ds(0, 32), :] = shared[:32, :ORDER]
    grad_mid[pl.ds(32, 32), :] = shared[:32, ORDER:]
    grad_in[pl.ds(0, 8), :] = shared[32:, :ORDER]
    grad_in[pl.ds(8, 8), :] = shared[32:, ORDER:]
    row = lax.broadcasted_iota(jnp.int32, (SIDE, SIDE), 0)
    lane = lax.broadcasted_iota(jnp.int32, (SIDE, SIDE), 1)
    moved = jnp.where(lane == 2 * (row // 8) + row % 8 // OWN + SEQ * (row % OWN), 1.0, 0.0).astype(F32)
    rows = jnp.concatenate([gathered[pl.ds(48 * chip + 40, 8), :] for chip in range(16)])
    channels = dot_tn(rows, moved, lax.Precision.HIGHEST)
    grad_out[...] = channels[:64]
    grad_decay[...] = channels[64:65]
    grad_skip[...] = channels[65:66]


def seq_place():
    return lax.axis_index(SEQ_AXES)


def run_send(query, key, value, grad, **kw):
    return call(
        send_kernel, 1, [pl.BlockSpec(memory_space=pltpu.HBM)] * 4, spec((1024, SIDE)), out((1024, SIDE)),
        scratch=[pltpu.VMEM((4, ROWS, SIDE), BF16), pltpu.SemaphoreType.DMA((4,))], **kw,
    )(*[in_hbm(x) for x in (query, key, value, grad)])


def run_filter(features, filter_in, filter_mid, filter_out, place=seq_place, **kw):
    wide = lambda i: (0, i)
    hidden = spec((ORDER, STEP), wide)
    half, full = pltpu.HBM((ORDER, HALF), BF16), pltpu.HBM((ORDER, HALF), F32)
    return call(
        functools.partial(filter_kernel, place),
        HALF // STEP,
        [spec((32, STEP), wide), spec((16, ORDER)), spec((ORDER, ORDER)), spec((ORDER, SIDE))],
        [hidden] * 6 + [spec((256, SIDE))] * 2,
        [half, half, full, half, half, full, out((256, SIDE)), out((256, SIDE))],
        scratch=[pltpu.VMEM((512, SIDE), F32)],
        flops=4 * 10**9, nbytes=10 * MIB, **kw,
    )(features, filter_in, filter_mid, filter_out)


def run_spectrum(mine, other, decay, place=seq_place, **kw):
    first_fwd, second_fwd, twiddle, _, _ = transform_tables()
    return call(
        functools.partial(spectrum_kernel, place),
        1,
        [spec((256, SIDE))] * 2 + [spec((1, SIDE)), spec((256, 384)), spec((768, 256)), spec((SIDE, 256))],
        spec((512, 256)),
        out((512, 256)),
        flops=10**9, nbytes=MIB, **kw,
    )(mine, other, decay, first_fwd, second_fwd, twiddle)


def run_convolve(field, spectrum, mine, other, decay, place=seq_place, **kw):
    first_fwd, second_fwd, twiddle, second_inv, first_inv = transform_tables()
    return call(
        functools.partial(convolve_kernel, place),
        1,
        [spec((1024, SIDE)), spec((512, 256)), spec((256, SIDE)), spec((256, SIDE)), spec((1, SIDE)),
         spec((256, 384)), spec((768, 256)), spec((SIDE, 256)), spec((768, 256)), spec((SIDE, 768))],
        [spec((1024, SIDE)), spec((512, SIDE)), spec((512, SIDE)), spec((16, SIDE))],
        [out((1024, SIDE)), pltpu.HBM((512, SIDE), F32), out((512, SIDE)), pltpu.HBM((16, SIDE), F32)],
        flops=4 * 10**9, nbytes=4 * MIB, **kw,
    )(field, spectrum, mine, other, decay, first_fwd, second_fwd, twiddle, second_inv, first_inv)


def run_backward(features, hidden, mine, other, sums, filter_mid, filter_out, place=seq_place, **kw):
    wide = lambda i: (0, i)
    block = spec((ORDER, BACK), wide)
    deep = spec((BACK // 16, SIDE), lambda i: (i, 0))
    return call(
        functools.partial(backward_kernel, place),
        HALF // BACK,
        [spec((32, BACK), wide)] + [block] * 6 + [deep, deep, spec((16, SIDE)), spec((ORDER, ORDER)), spec((ORDER, SIDE))],
        spec((48, SIDE)),
        out((48, SIDE)),
        scratch=[pltpu.VMEM((384, 176), F32)] + [pltpu.VMEM((ORDER, BACK), BF16)] * 4,
        flops=4 * 10**9, nbytes=10 * MIB, **kw,
    )(features, *[in_hbm(x) for x in hidden], in_hbm(mine), other, in_hbm(sums), in_hbm(filter_mid), in_hbm(filter_out))


def run_receive(query, key, value, grad, skip, field, **kw):
    block = spec((ROWS, SIDE))
    return call(receive_kernel, 1, [block] * 4 + [spec((1, SIDE)), spec((1024, SIDE))], [block] * 4,
                [out((ROWS, SIDE), BF16)] * 4, **kw)(query, key, value, grad, skip, field)


def run_finish(gathered, **kw):
    shapes = [(16, ORDER), (ORDER, ORDER), (ORDER, SIDE), (1, SIDE), (1, SIDE)]
    return call(finish_kernel, 1, [spec((768, SIDE))], [spec(s) for s in shapes], [out(s) for s in shapes], **kw)(gathered)


def exchanged(x, axis, distance):
    return lax.ppermute(x, axis, [(i, i ^ distance) for i in range(lax.axis_size(axis))])


def group_sum(x, axis, distances):
    values = [x] + [exchanged(x, axis, d) for d in distances]
    while len(values) > 1:
        values = [a + b for a, b in zip(values[::2], values[1::2])]
    return values[0]


def body(query, key, value, grad, filter_in, filter_mid, filter_out, decay_rate, skip_gain):
    decay = decay_rate.reshape(1, SIDE)
    skip = skip_gain.reshape(1, SIDE)
    core = lax.axis_index("core")
    features = lax.dynamic_slice_in_dim(jnp.asarray(feature_table()), HALF * core, HALF, axis=1)
    sent = run_send(query, key, value, grad).reshape(SEQ, SEQ, SIDE)
    field = lax.all_to_all(sent, SEQ_AXES, 0, 0, tiled=True).reshape(1024, SIDE)
    *hidden, mine, theirs = run_filter(features, filter_in, filter_mid, filter_out)
    other = exchanged(theirs, "core", 1)
    spectrum = run_spectrum(mine, other, decay)
    sent, mine, theirs, sums = run_convolve(field, spectrum, mine, other, decay)
    field = lax.all_to_all(sent.reshape(SEQ, SEQ, SIDE), SEQ_AXES, 0, 0, tiled=True).reshape(1024, SIDE)
    grads = run_backward(features, hidden, mine, exchanged(theirs, "core", 1), sums, filter_mid, filter_out)
    grads = group_sum(grads, "core", (1,))
    shared = group_sum(grads[:40], "chan", (1, 2, 3))
    shared, field = lax.optimization_barrier((shared, field))
    shared = group_sum(shared, "chan", (6,))
    grads = jnp.broadcast_to(jnp.concatenate([shared, grads[40:]])[None], (16, 48, SIDE))
    gathered = lax.all_to_all(grads, ("x", "y"), 0, 0, tiled=True).reshape(768, SIDE)
    output, grad_query, grad_key, grad_value = run_receive(query, key, value, grad, skip, field)
    first, second, third, rates, gains = run_finish(gathered)
    return (output, grad_query, grad_key, grad_value, first, second, third, rates.reshape(SIDE), gains.reshape(SIDE))


def solution(mesh):
    parts = Mesh(mesh.devices.reshape(4, 4, 2, 8), SEQ_AXES + ("chan",))
    wide = P(SEQ_AXES, "chan")
    return jax.shard_map(
        body,
        mesh=parts,
        in_specs=(wide, wide, wide, wide, P(), P(), P(None, "chan"), P("chan"), P("chan")),
        out_specs=(wide, wide, wide, wide, P(), P(), P(None, "chan"), P("chan"), P("chan")),
        check_vma=False,
    )
```

```python
import functools
import math

import jax
import jax.numpy as jnp
import ml_dtypes
import numpy as np
from jax import lax
from jax.experimental import pallas as pl
from jax.experimental.pallas import tpu as pltpu
from jax.sharding import Mesh, PartitionSpec as P

F32 = jnp.float32
BF16 = jnp.bfloat16
LENGTH = 16384
SEQ = 32
ROWS = 512
SIDE = 128
OWN = 4
ORDER = 64
STEP = 2048
PIECE = 256
BACK = 4096
HALF = LENGTH // 2
MIB = 1 << 20
SEQ_AXES = ("x", "y", "core")


def split_table(table):
    high = table.astype(ml_dtypes.bfloat16)
    low = (table - high.astype(np.float64)).astype(ml_dtypes.bfloat16)
    return high, low


@functools.cache
def time_rows():
    p = np.arange(SIDE)
    return 4 * (p % SEQ) + p // SEQ


@functools.cache
def feature_table():
    t = (time_rows()[:, None] * SIDE + np.arange(SIDE)[None, :]).reshape(-1)
    rows = [t / LENGTH]
    angles = []
    for i in range(7):
        factor = max(1, LENGTH // 4 // 4 ** (6 - i))
        angles.append((factor * t % LENGTH) * (2.0 * math.pi / LENGTH))
    rows += [np.sin(a) for a in angles] + [np.cos(a) for a in angles] + [np.ones(LENGTH)]
    high, low = split_table(np.stack(rows).astype(np.float64))
    return np.concatenate([high, low])


@functools.cache
def transform_tables():
    idx = np.arange(SIDE)
    n1 = time_rows()
    first = np.exp(-2j * np.pi * ((n1[None, :] * idx[:, None] % SIDE) / SIDE + n1[None, :] / (4 * SIDE)))
    twiddle = np.exp(-2j * np.pi * idx[None, :] * (4 * idx[:, None] + 1) / (4 * LENGTH))
    second = np.exp(-2j * np.pi * (idx[:, None] * idx[None, :] % SIDE) / SIDE)
    high, low = split_table(np.concatenate([first.real, first.imag]))
    first_fwd = np.concatenate([high, high, low], axis=1)
    high, low = split_table(np.block([[second.real, second.imag], [-second.imag, second.real]]))
    second_fwd = np.concatenate([high, high, low])
    high, low = split_table(np.block([[second.real, -second.imag], [second.imag, second.real]]))
    second_inv = np.concatenate([high, high, low])
    high, low = split_table(np.concatenate([first.real.T, first.imag.T], axis=1) / LENGTH)
    first_inv = np.concatenate([high, high, low], axis=1)
    twiddle = np.concatenate([twiddle.real, twiddle.imag], axis=1).astype(np.float32)
    return first_fwd, second_fwd, twiddle, second_inv, first_inv


@functools.cache
def turn_polynomials():
    nodes = 0.5 * np.cos(np.pi * (np.arange(400) + 0.5) / 800)
    squares = nodes * nodes

    def fit(values, weight, count):
        basis = np.stack([squares**k for k in range(count)], axis=1)
        return np.linalg.lstsq(basis * weight[:, None], values, rcond=None)[0]

    sine = fit(np.sin(2 * np.pi * nodes), nodes, 6)
    cosine = fit(np.cos(2 * np.pi * nodes), np.ones_like(nodes), 6)
    return [float(c) for c in sine], [float(c) for c in cosine]


def sine_cosine(turns):
    sine, cosine = turn_polynomials()
    part = turns - jnp.round(turns)
    square = part * part
    s = jnp.full_like(square, sine[-1])
    for c in sine[-2::-1]:
        s = s * square + c
    c_out = jnp.full_like(square, cosine[-1])
    for c in cosine[-2::-1]:
        c_out = c_out * square + c
    return s * part, c_out


def halves(x):
    high = x.astype(BF16)
    return high, (x - high.astype(F32)).astype(BF16)


def dot(a, b):
    return jnp.dot(a, b, preferred_element_type=F32)


def dot_nt(a, b, precision=None):
    return lax.dot_general(a, b, (((1,), (1,)), ((), ())), precision=precision, preferred_element_type=F32)


def dot_tn(a, b, precision=None):
    return lax.dot_general(a, b, (((0,), (0,)), ((), ())), precision=precision, preferred_element_type=F32)


def data_left(x, axis):
    high, low = halves(x)
    return jnp.concatenate([high, low, high], axis=axis)


def weight_left(x, axis):
    high, low = halves(x)
    return jnp.concatenate([high, high, low], axis=axis)


def picked(filter_out, channels):
    return dot_nt(jnp.concatenate(halves(filter_out[...])), channels.astype(BF16))


def own_channels(place):
    row = lax.broadcasted_iota(jnp.int32, (8, SIDE), 0)
    lane = lax.broadcasted_iota(jnp.int32, (8, SIDE), 1)
    other = place + 1 - 2 * (place % 2)
    channel = jnp.where(row < OWN, place + SEQ * row, other + SEQ * (row - OWN))
    return jnp.where(lane == channel, 1.0, 0.0).astype(F32)


def position_grid():
    row = lax.broadcasted_iota(jnp.int32, (SIDE, SIDE), 0)
    lane = lax.broadcasted_iota(jnp.int32, (SIDE, SIDE), 1)
    return (ROWS * (row % SEQ) + SIDE * (row // SEQ) + lane).astype(F32)


def spec(shape, index=None):
    if index is None:
        zeros = (0,) * len(shape)
        return pl.BlockSpec(shape, lambda i: zeros)
    return pl.BlockSpec(shape, index)


def out(shape, dtype=F32):
    return jax.ShapeDtypeStruct(shape, dtype)


def in_hbm(x):
    return pltpu.with_memory_space_constraint(x, pltpu.HBM)


def call(kernel, grid, in_specs, out_specs, out_shape, scratch=(), limit=16, flops=1, nbytes=1, interpret=False):
    return pl.pallas_call(
        kernel,
        grid=(grid,),
        in_specs=in_specs,
        out_specs=out_specs,
        out_shape=out_shape,
        scratch_shapes=scratch,
        compiler_params=pltpu.CompilerParams(vmem_limit_bytes=limit * MIB),
        cost_estimate=pl.CostEstimate(flops=flops, bytes_accessed=nbytes, transcendentals=0),
        interpret=interpret,
    )


def send_kernel(query, key, value, grad, sent, held, sems):
    copies = [pltpu.make_async_copy(x, held.at[k], sems.at[k]) for k, x in enumerate((key, value, grad, query))]
    for copy in copies:
        copy.start()
    for offset, first, second in ((0, 0, 1), (OWN, 2, 3)):
        copies[first].wait()
        copies[second].wait()
        for h in range(ROWS // SIDE):
            rows = pl.ds(SIDE * h, SIDE)
            block = (held[first, rows, :].astype(F32) * held[second, rows, :].astype(F32)).T
            for c in range(OWN):
                sent[pl.ds(8 * h + offset + c, SEQ, stride=SEQ), :] = block[SEQ * c : SEQ * (c + 1), :]


def receive_kernel(query, key, value, grad, skip, field, output, grad_query, grad_key, grad_value):
    for h in range(ROWS // SIDE):
        rows = pl.ds(SIDE * h, SIDE)
        query_wide = query[rows, :].astype(F32)
        key_wide = key[rows, :].astype(F32)
        value_wide = value[rows, :].astype(F32)
        grad_wide = grad[rows, :].astype(F32)
        conv, back = (
            jnp.concatenate([field[pl.ds(8 * h + offset + c, SEQ, stride=SEQ), :] for c in range(OWN)]).T
            for offset in (0, OWN)
        )
        mixed = conv + skip[...] * (key_wide * value_wide)
        output[rows, :] = (query_wide * mixed).astype(BF16)
        grad_query[rows, :] = (grad_wide * mixed).astype(BF16)
        dgated = back + skip[...] * (grad_wide * query_wide)
        grad_key[rows, :] = (dgated * value_wide).astype(BF16)
        grad_value[rows, :] = (dgated * key_wide).astype(BF16)


def forward_rows(fields, first_fwd, second_fwd, twiddle):
    cos, sin = twiddle[:, :SIDE], twiddle[:, SIDE:]
    turned = []
    for pair in range(0, len(fields), 2):
        stage = dot(first_fwd[...], data_left(jnp.concatenate(fields[pair : pair + 2], axis=1), 0))
        for k in range(2):
            re = stage[:SIDE, SIDE * k : SIDE * (k + 1)]
            im = stage[SIDE:, SIDE * k : SIDE * (k + 1)]
            turned.append(data_left(jnp.concatenate([re * cos - im * sin, re * sin + im * cos], axis=1), 1))
    return dot(jnp.concatenate(turned), second_fwd[...])


def inverse_rows(spectra, first_inv, second_inv, twiddle):
    cos, sin = twiddle[:, :SIDE], twiddle[:, SIDE:]
    stage = dot(jnp.concatenate([data_left(s, 1) for s in spectra]), second_inv[...])
    turned = []
    for k in range(len(spectra)):
        re = stage[SIDE * k : SIDE * (k + 1), :SIDE]
        im = stage[SIDE * k : SIDE * (k + 1), SIDE:]
        turned.append(jnp.concatenate([re * cos + im * sin, im * cos - re * sin]))
    fields = []
    for pair in range(0, len(spectra), 2):
        both = dot(first_inv[...], data_left(jnp.concatenate(turned[pair : pair + 2], axis=1), 0))
        fields += [both[:, :SIDE], both[:, SIDE:]]
    return fields


def filter_kernel(place, features, filter_in, filter_mid, filter_out,
                  hidden, cosines, mine, theirs, shaped):
    step = pl.program_id(0)
    own = own_channels(place())
    turn = 1.0 / (2.0 * math.pi)
    in_high, in_low = halves(filter_in[...].T * turn)
    weight1 = jnp.concatenate([in_high, in_low, in_high], axis=1)
    weight2 = weight_left(filter_mid[...].T * turn, 1)
    weight3 = picked(filter_out, own).T.astype(BF16)
    weight3 = jnp.concatenate([weight3[:, :64], weight3[:, :64], weight3[:, 64:]], axis=1)
    pieces = [pl.ds(PIECE * k, PIECE) for k in range(STEP // PIECE)]
    for piece in pieces:
        feature = features[:, piece]
        rows = jnp.concatenate([feature[:16], feature[:16], feature[16:]])
        sine, cosine = sine_cosine(dot(weight1, rows))
        cosines[pl.ds(0, 64), piece] = cosine
        hidden[pl.ds(0, 128), piece] = jnp.concatenate(halves(sine))
    for piece in pieces:
        rows = hidden[pl.ds(0, 128), piece]
        sine, cosine = sine_cosine(dot(weight2, jnp.concatenate([rows, rows[:64]])))
        cosines[pl.ds(64, 64), piece] = cosine
        hidden[pl.ds(128, 128), piece] = jnp.concatenate(halves(sine))
    for k, piece in enumerate(pieces):
        rows = hidden[pl.ds(128, 128), piece]
        values = dot(weight3, jnp.concatenate([rows, rows[:64]]))
        for m in range(PIECE // SIDE):
            row = 8 * (step * (STEP // SIDE) + k * (PIECE // SIDE) + m)
            shaped[pl.ds(pl.multiple_of(row, 8), 8), :] = values[:, SIDE * m : SIDE * (m + 1)]

    @pl.when(step == HALF // STEP - 1)
    def _():
        for c in range(OWN):
            mine[pl.ds(64 * c, 64), :] = shaped[pl.ds(c, 64, stride=8), :]
            theirs[pl.ds(64 * c, 64), :] = shaped[pl.ds(c + OWN, 64, stride=8), :]


def filter_fields(me, mine, other, decay):
    time = position_grid()
    lower = me % 2 == 0
    rates = jnp.sum(own_channels(me) * decay[...], axis=1, keepdims=True)
    for c in range(OWN):
        rate = rates[c : c + 1, :]
        window = jnp.exp(-rate * time) * jnp.sqrt(rate + 1.0 / LENGTH)
        here, there = mine[pl.ds(64 * c, 64), :], other[pl.ds(64 * c, 64), :]
        yield window, jnp.concatenate([jnp.where(lower, here, there), jnp.where(lower, there, here)]), rate


def spectrum_kernel(place, mine, other, decay, first_fwd, second_fwd, twiddle, spectrum):
    fields = [window * shaped for window, shaped, _ in filter_fields(place(), mine, other, decay)]
    spectrum[...] = forward_rows(fields, first_fwd, second_fwd, twiddle)


def correlate_kernel(place, field, shaped_mine, shaped_other, decay, first_fwd, second_fwd, twiddle, second_inv, first_inv,
                     spectra, mine, theirs, sums):
    fields = []
    for c in range(OWN):
        for offset in (0, OWN):
            fields.append(
                jnp.concatenate([field[pl.ds(8 * h + offset + c, SEQ, stride=SEQ), :] for h in range(ROWS // SIDE)])
            )
    spectra[...] = forward_rows(fields, first_fwd, second_fwd, twiddle)
    products = []
    for c in range(OWN):
        gated, incoming = (spectra[pl.ds(SIDE * k, SIDE), :] for k in (2 * c, 2 * c + 1))
        gated_re, gated_im = gated[:, :SIDE], gated[:, SIDE:]
        incoming_re, incoming_im = incoming[:, :SIDE], incoming[:, SIDE:]
        products.append(jnp.concatenate([gated_re * incoming_re + gated_im * incoming_im,
                                         gated_re * incoming_im - gated_im * incoming_re], axis=1))
    results = inverse_rows(products, first_inv, second_inv, twiddle)
    time = position_grid()
    me = place()
    lower = me % 2 == 0
    pair = lambda x: (jnp.where(lower, x, 0.0), jnp.where(lower, 0.0, x))
    for c, (window, shaped, rate) in enumerate(filter_fields(me, shaped_mine, shaped_other, decay)):
        dshaped = results[c] * window
        slope = 0.5 / (rate + 1.0 / LENGTH) - time
        for part, sum_row, value in (
            (mine, None, jnp.where(lower, dshaped[:64], dshaped[64:])),
            (theirs, None, jnp.where(lower, dshaped[64:], dshaped[:64])),
            (sums, 0, jnp.sum(dshaped * shaped * slope, axis=0, keepdims=True)),
            (sums, 8, jnp.sum(fields[2 * c] * fields[2 * c + 1], axis=0, keepdims=True)),
        ):
            for offset, v in zip((0, OWN), pair(value)):
                rows = pl.ds(c + offset, 64, stride=8) if sum_row is None else pl.ds(sum_row + c + offset, 1)
                part[rows, :] = v


def convolve_kernel(spectra, spectrum, twiddle, second_inv, first_inv, sent):
    products = []
    for c in range(OWN):
        gated, incoming = (spectra[pl.ds(SIDE * k, SIDE), :] for k in (2 * c, 2 * c + 1))
        kernel = spectrum[pl.ds(SIDE * c, SIDE), :]
        gated_re, gated_im = gated[:, :SIDE], gated[:, SIDE:]
        incoming_re, incoming_im = incoming[:, :SIDE], incoming[:, SIDE:]
        kernel_re, kernel_im = kernel[:, :SIDE], kernel[:, SIDE:]
        products += [
            jnp.concatenate([kernel_re * gated_re - kernel_im * gated_im,
                             kernel_re * gated_im + kernel_im * gated_re], axis=1),
            jnp.concatenate([kernel_re * incoming_re + kernel_im * incoming_im,
                             kernel_re * incoming_im - kernel_im * incoming_re], axis=1),
        ]
    results = inverse_rows(products, first_inv, second_inv, twiddle)
    for c in range(OWN):
        for offset, result in ((0, results[2 * c]), (OWN, results[2 * c + 1])):
            for h in range(ROWS // SIDE):
                sent[pl.ds(8 * h + offset + c, SEQ, stride=SEQ), :] = result[SEQ * h : SEQ * (h + 1), :]


def pair_channels(place):
    row = lax.broadcasted_iota(jnp.int32, (8, SIDE), 0)
    lane = lax.broadcasted_iota(jnp.int32, (8, SIDE), 1)
    return jnp.where(lane == place - place % 2 + row // OWN + SEQ * (row % OWN), 1.0, 0.0).astype(F32)


def backward_kernel(place, features, hidden, cosines, mine, other, sums, filter_mid, filter_out, grads, total, d2, d1):
    step = pl.program_id(0)
    weight3 = picked(filter_out, pair_channels(place())).astype(BF16)
    weight3 = jnp.concatenate([weight3[:64], weight3[:64], weight3[64:]], axis=1)
    weight2 = weight_left(filter_mid[...], 1)
    pieces = [pl.ds(PIECE * k, PIECE) for k in range(BACK // PIECE)]
    shaped_high, shaped_low = halves(
        jnp.concatenate([mine[pl.ds(8 * m, 8), :] + other[pl.ds(8 * m, 8), :] for m in range(BACK // SIDE)], axis=1)
    )
    for k, piece in enumerate(pieces):
        part = slice(PIECE * k, PIECE * (k + 1))
        rows = jnp.concatenate([shaped_high[:, part], shaped_low[:, part], shaped_high[:, part]])
        d2[:, piece] = jnp.concatenate(halves(dot(weight3, rows) * cosines[pl.ds(64, 64), piece]))
    for piece in pieces:
        rows = d2[:, piece]
        d1[:, piece] = jnp.concatenate(
            halves(dot(weight2, jnp.concatenate([rows, rows[:64]])) * cosines[pl.ds(0, 64), piece])
        )
    left = jnp.concatenate([hidden[...], d1[...]])
    right = jnp.concatenate([d2[...], shaped_high, shaped_low, features[...]])
    product = dot_nt(left, right)

    @pl.when(step == 0)
    def _():
        total[...] = product

    @pl.when(step > 0)
    def _():
        total[...] += product

    @pl.when(step == HALF // BACK - 1)
    def _():
        mid = total[:64, :64] + (total[:64, 64:128] + total[64:128, :64])
        grads[pl.ds(0, 32), :] = jnp.concatenate([mid[:32], mid[32:]], axis=1)
        side = [jnp.concatenate([total[64 * k : 64 * (k + 1), 128:], jnp.zeros((64, 80), F32)], axis=1).T for k in range(2, 6)]
        first = side[2][16:32] + (side[2][32:48] + side[3][16:32])
        third = side[0][:8] + (side[0][8:16] + side[1][:8])
        grads[pl.ds(32, 8), :] = jnp.concatenate([first[:8], first[8:]], axis=1)
        channels = pair_channels(place())
        rates = jnp.sum(sums[pl.ds(0, 8), :], axis=1, keepdims=True)
        gains = jnp.sum(sums[pl.ds(8, 8), :], axis=1, keepdims=True)
        grads[pl.ds(40, 64), :] = dot_tn(third, channels, lax.Precision.HIGHEST)
        grads[pl.ds(104, 8), :] = jnp.concatenate([
            jnp.sum(channels * rates, axis=0, keepdims=True),
            jnp.sum(channels * gains, axis=0, keepdims=True),
            jnp.zeros((6, SIDE), F32),
        ])


def finish_kernel(total, grad_in, grad_mid, grad_out, grad_decay, grad_skip):
    grad_mid[pl.ds(0, 32), :] = total[:32, :ORDER]
    grad_mid[pl.ds(32, 32), :] = total[:32, ORDER:]
    grad_in[pl.ds(0, 8), :] = total[32:40, :ORDER]
    grad_in[pl.ds(8, 8), :] = total[32:40, ORDER:]
    grad_out[...] = total[40:104]
    grad_decay[...] = total[104:105]
    grad_skip[...] = total[105:106]


def seq_place():
    return lax.axis_index(SEQ_AXES)


def run_send(query, key, value, grad, **kw):
    return call(
        send_kernel, 1, [pl.BlockSpec(memory_space=pltpu.HBM)] * 4, spec((1024, SIDE)), out((1024, SIDE)),
        scratch=[pltpu.VMEM((4, ROWS, SIDE), BF16), pltpu.SemaphoreType.DMA((4,))], **kw,
    )(*[in_hbm(x) for x in (query, key, value, grad)])


def run_filter(features, filter_in, filter_mid, filter_out, place=seq_place, **kw):
    wide = lambda i: (0, i)
    return call(
        functools.partial(filter_kernel, place),
        HALF // STEP,
        [spec((32, STEP), wide), spec((16, ORDER)), spec((ORDER, ORDER)), spec((ORDER, SIDE))],
        [spec((256, STEP), wide), spec((SIDE, STEP), wide)] + [spec((256, SIDE))] * 2,
        [pltpu.HBM((256, HALF), BF16), pltpu.HBM((SIDE, HALF), F32), out((256, SIDE)), out((256, SIDE))],
        scratch=[pltpu.VMEM((512, SIDE), F32)],
        flops=4 * 10**9, nbytes=10 * MIB, **kw,
    )(features, in_hbm(filter_in), in_hbm(filter_mid), in_hbm(filter_out))


def run_spectrum(mine, other, decay, place=seq_place, **kw):
    first_fwd, second_fwd, twiddle, _, _ = transform_tables()
    return call(
        functools.partial(spectrum_kernel, place),
        1,
        [spec((256, SIDE))] * 2 + [spec((1, SIDE)), spec((256, 384)), spec((768, 256)), spec((SIDE, 256))],
        spec((512, 256)),
        out((512, 256)),
        flops=10**9, nbytes=MIB, **kw,
    )(mine, other, decay, first_fwd, second_fwd, twiddle)


def run_correlate(field, mine, other, decay, place=seq_place, **kw):
    first_fwd, second_fwd, twiddle, second_inv, first_inv = transform_tables()
    return call(
        functools.partial(correlate_kernel, place),
        1,
        [spec((1024, SIDE)), spec((256, SIDE)), spec((256, SIDE)), spec((1, SIDE)),
         spec((256, 384)), spec((768, 256)), spec((SIDE, 256)), spec((768, 256)), spec((SIDE, 768))],
        [spec((1024, 256)), spec((512, SIDE)), spec((512, SIDE)), spec((16, SIDE))],
        [out((1024, 256)), out((512, SIDE)), out((512, SIDE)), out((16, SIDE))],
        flops=2 * 10**9, nbytes=4 * MIB, **kw,
    )(field, mine, other, decay, first_fwd, second_fwd, twiddle, second_inv, first_inv)


def run_convolve(spectra, spectrum, **kw):
    _, _, twiddle, second_inv, first_inv = transform_tables()
    return call(
        convolve_kernel,
        1,
        [spec((1024, 256)), spec((512, 256)), spec((SIDE, 256)), spec((768, 256)), spec((SIDE, 768))],
        spec((1024, SIDE)),
        out((1024, SIDE)),
        flops=2 * 10**9, nbytes=3 * MIB, **kw,
    )(spectra, spectrum, twiddle, second_inv, first_inv)


def run_backward(features, hidden, mine, other, sums, filter_mid, filter_out, place=seq_place, **kw):
    wide = lambda i: (0, i)
    deep = spec((BACK // 16, SIDE), lambda i: (i, 0))
    return call(
        functools.partial(backward_kernel, place),
        HALF // BACK,
        [spec((32, BACK), wide), spec((256, BACK), wide), spec((SIDE, BACK), wide), deep, deep, spec((16, SIDE)), spec((ORDER, ORDER)), spec((ORDER, SIDE))],
        spec((112, SIDE)),
        out((112, SIDE)),
        scratch=[pltpu.VMEM((384, 176), F32)] + [pltpu.VMEM((SIDE, BACK), BF16)] * 2,
        flops=4 * 10**9, nbytes=10 * MIB, **kw,
    )(features, *hidden, mine, other, sums, in_hbm(filter_mid), in_hbm(filter_out))


def run_receive(query, key, value, grad, skip, field, **kw):
    block = spec((ROWS, SIDE))
    return call(receive_kernel, 1, [block] * 4 + [spec((1, SIDE)), spec((1024, SIDE))], [block] * 4,
                [out((ROWS, SIDE), BF16)] * 4, **kw)(query, key, value, grad, skip, field)


def run_finish(total, **kw):
    shapes = [(16, ORDER), (ORDER, ORDER), (ORDER, SIDE), (1, SIDE), (1, SIDE)]
    return call(finish_kernel, 1, [spec((112, SIDE))], [spec(s) for s in shapes], [out(s) for s in shapes], **kw)(
        total
    )


def exchanged(x, axis, distance):
    return lax.ppermute(x, axis, [(i, i ^ distance) for i in range(lax.axis_size(axis))])


def group_sum(x, axis, distances):
    values = [x] + [exchanged(x, axis, d) for d in distances]
    while len(values) > 1:
        values = [a + b for a, b in zip(values[::2], values[1::2])]
    return values[0]


def body(query, key, value, grad, filter_in, filter_mid, filter_out, decay_rate, skip_gain):
    decay = decay_rate.reshape(1, SIDE)
    skip = skip_gain.reshape(1, SIDE)
    core = lax.axis_index("core")
    features = lax.dynamic_slice_in_dim(jnp.asarray(feature_table()), HALF * core, HALF, axis=1)
    sent = run_send(query, key, value, grad).reshape(SEQ, SEQ, SIDE)
    field = lax.all_to_all(sent, SEQ_AXES, 0, 0, tiled=True).reshape(1024, SIDE)
    *hidden, mine, theirs = run_filter(features, filter_in, filter_mid, filter_out)
    other = exchanged(theirs, "core", 1)
    spectrum = run_spectrum(mine, other, decay)
    spectra, mine, theirs, sums = run_correlate(field, mine, other, decay)
    mine, spectrum = lax.optimization_barrier((mine, spectrum))
    grads = run_backward(features, hidden, mine, exchanged(theirs, "core", 1), sums, filter_mid, filter_out)
    grads, spectra = lax.optimization_barrier((grads, spectra))
    sent = run_convolve(spectra, spectrum)
    field = lax.all_to_all(sent.reshape(SEQ, SEQ, SIDE), SEQ_AXES, 0, 0, tiled=True).reshape(1024, SIDE)
    grads = group_sum(grads, "core", (1,))
    shared = group_sum(grads[:40], "chan", (1, 2, 3))
    shared, sent = lax.optimization_barrier((shared, sent))
    shared = group_sum(shared, "chan", (6,))
    grads = jnp.concatenate([shared, grads[40:]])
    grads = group_sum(grads, "x", (1, 2, 3))
    grads, field = lax.optimization_barrier((grads, field))
    grads = group_sum(grads, "y", (1, 2, 3))
    output, grad_query, grad_key, grad_value = run_receive(query, key, value, grad, skip, field)
    grads, output = lax.optimization_barrier((grads, output))
    first, second, third, rates, gains = run_finish(grads)
    return (output, grad_query, grad_key, grad_value, first, second, third, rates.reshape(SIDE), gains.reshape(SIDE))


def solution(mesh):
    parts = Mesh(mesh.devices.reshape(4, 4, 2, 8), SEQ_AXES + ("chan",))
    wide = P(SEQ_AXES, "chan")
    return jax.shard_map(
        body,
        mesh=parts,
        in_specs=(wide, wide, wide, wide, P(), P(), P(None, "chan"), P("chan"), P("chan")),
        out_specs=(wide, wide, wide, wide, P(), P(), P(None, "chan"), P("chan"), P("chan")),
        check_vma=False,
    )
```

```python
import functools
import math

import jax
import jax.numpy as jnp
import ml_dtypes
import numpy as np
from jax import lax
from jax.experimental import pallas as pl
from jax.experimental.pallas import tpu as pltpu
from jax.sharding import Mesh, PartitionSpec as P

F32 = jnp.float32
BF16 = jnp.bfloat16
LENGTH = 16384
SEQ = 32
ROWS = 512
SIDE = 128
OWN = 4
ORDER = 64
STEP = 2048
PIECE = 256
HALF = LENGTH // 2
MIB = 1 << 20
SEQ_AXES = ("x", "y", "core")


def split_table(table):
    high = table.astype(ml_dtypes.bfloat16)
    low = (table - high.astype(np.float64)).astype(ml_dtypes.bfloat16)
    return high, low


@functools.cache
def time_rows():
    p = np.arange(SIDE)
    return 4 * (p % SEQ) + p // SEQ


@functools.cache
def feature_table():
    t = (time_rows()[:, None] * SIDE + np.arange(SIDE)[None, :]).reshape(-1)
    rows = [t / LENGTH]
    angles = []
    for i in range(7):
        factor = max(1, LENGTH // 4 // 4 ** (6 - i))
        angles.append((factor * t % LENGTH) * (2.0 * math.pi / LENGTH))
    rows += [np.sin(a) for a in angles] + [np.cos(a) for a in angles] + [np.ones(LENGTH)]
    high, low = split_table(np.stack(rows).astype(np.float64))
    return np.concatenate([high, low])


@functools.cache
def transform_tables():
    idx = np.arange(SIDE)
    n1 = time_rows()
    first = np.exp(-2j * np.pi * ((n1[None, :] * idx[:, None] % SIDE) / SIDE + n1[None, :] / (4 * SIDE)))
    twiddle = np.exp(-2j * np.pi * idx[None, :] * (4 * idx[:, None] + 1) / (4 * LENGTH))
    second = np.exp(-2j * np.pi * (idx[:, None] * idx[None, :] % SIDE) / SIDE)
    high, low = split_table(np.concatenate([first.real, first.imag]))
    first_fwd = np.concatenate([high, high, low], axis=1)
    high, low = split_table(np.block([[second.real, second.imag], [-second.imag, second.real]]))
    second_fwd = np.concatenate([high, high, low])
    high, low = split_table(np.block([[second.real, -second.imag], [second.imag, second.real]]))
    second_inv = np.concatenate([high, high, low])
    high, low = split_table(np.concatenate([first.real.T, first.imag.T], axis=1) / LENGTH)
    first_inv = np.concatenate([high, high, low], axis=1)
    twiddle = np.concatenate([twiddle.real, twiddle.imag], axis=1).astype(np.float32)
    return first_fwd, second_fwd, twiddle, second_inv, first_inv


@functools.cache
def turn_polynomials():
    nodes = 0.5 * np.cos(np.pi * (np.arange(400) + 0.5) / 800)
    squares = nodes * nodes

    def fit(values, weight, count):
        basis = np.stack([squares**k for k in range(count)], axis=1)
        return np.linalg.lstsq(basis * weight[:, None], values, rcond=None)[0]

    sine = fit(np.sin(2 * np.pi * nodes), nodes, 6)
    cosine = fit(np.cos(2 * np.pi * nodes), np.ones_like(nodes), 6)
    return [float(c) for c in sine], [float(c) for c in cosine]


def sine_cosine(turns):
    sine, cosine = turn_polynomials()
    part = turns - jnp.round(turns)
    square = part * part
    s = jnp.full_like(square, sine[-1])
    for c in sine[-2::-1]:
        s = s * square + c
    c_out = jnp.full_like(square, cosine[-1])
    for c in cosine[-2::-1]:
        c_out = c_out * square + c
    return s * part, c_out


def halves(x):
    high = x.astype(BF16)
    return high, (x - high.astype(F32)).astype(BF16)


def dot(a, b):
    return jnp.dot(a, b, preferred_element_type=F32)


def dot_nt(a, b, precision=None):
    return lax.dot_general(a, b, (((1,), (1,)), ((), ())), precision=precision, preferred_element_type=F32)


def dot_tn(a, b, precision=None):
    return lax.dot_general(a, b, (((0,), (0,)), ((), ())), precision=precision, preferred_element_type=F32)


def data_left(x, axis):
    high, low = halves(x)
    return jnp.concatenate([high, low, high], axis=axis)


def weight_left(x, axis):
    high, low = halves(x)
    return jnp.concatenate([high, high, low], axis=axis)


def picked(filter_out, channels):
    return dot_nt(jnp.concatenate(halves(filter_out[...])), channels.astype(BF16))


def own_channels(place):
    row = lax.broadcasted_iota(jnp.int32, (8, SIDE), 0)
    lane = lax.broadcasted_iota(jnp.int32, (8, SIDE), 1)
    other = place + 1 - 2 * (place % 2)
    channel = jnp.where(row < OWN, place + SEQ * row, other + SEQ * (row - OWN))
    return jnp.where(lane == channel, 1.0, 0.0).astype(F32)


def position_grid():
    row = lax.broadcasted_iota(jnp.int32, (SIDE, SIDE), 0)
    lane = lax.broadcasted_iota(jnp.int32, (SIDE, SIDE), 1)
    return (ROWS * (row % SEQ) + SIDE * (row // SEQ) + lane).astype(F32)


def spec(shape, index=None):
    if index is None:
        zeros = (0,) * len(shape)
        return pl.BlockSpec(shape, lambda i: zeros)
    return pl.BlockSpec(shape, index)


def out(shape, dtype=F32):
    return jax.ShapeDtypeStruct(shape, dtype)


def in_hbm(x):
    return pltpu.with_memory_space_constraint(x, pltpu.HBM)


def call(kernel, grid, in_specs, out_specs, out_shape, scratch=(), limit=16, flops=1, nbytes=1, interpret=False):
    return pl.pallas_call(
        kernel,
        grid=(grid,),
        in_specs=in_specs,
        out_specs=out_specs,
        out_shape=out_shape,
        scratch_shapes=scratch,
        compiler_params=pltpu.CompilerParams(vmem_limit_bytes=limit * MIB),
        cost_estimate=pl.CostEstimate(flops=flops, bytes_accessed=nbytes, transcendentals=0),
        interpret=interpret,
    )


def send_kernel(place, query, key, value, grad, table, sent, features, held, half_held, sems):
    half = pl.ds(pl.multiple_of(HALF * (place() % 2), HALF), HALF)
    features_in = pltpu.make_async_copy(table.at[:, half], half_held, sems.at[4])
    features_out = pltpu.make_async_copy(half_held, features, sems.at[5])
    copies = [pltpu.make_async_copy(x, held.at[k], sems.at[k]) for k, x in enumerate((key, value, grad, query))]
    for copy in copies:
        copy.start()
    features_in.start()
    for offset, first, second in ((0, 0, 1), (OWN, 2, 3)):
        if offset:
            features_in.wait()
            features_out.start()
        copies[first].wait()
        copies[second].wait()
        for h in range(ROWS // SIDE):
            rows = pl.ds(SIDE * h, SIDE)
            block = (held[first, rows, :].astype(F32) * held[second, rows, :].astype(F32)).T
            for c in range(OWN):
                sent[pl.ds(8 * h + offset + c, SEQ, stride=SEQ), :] = block[SEQ * c : SEQ * (c + 1), :]
    features_out.wait()


def receive_kernel(query, key, value, grad, skip, field, output, grad_query, grad_key, grad_value):
    for h in range(ROWS // SIDE):
        rows = pl.ds(SIDE * h, SIDE)
        query_wide = query[rows, :].astype(F32)
        key_wide = key[rows, :].astype(F32)
        value_wide = value[rows, :].astype(F32)
        grad_wide = grad[rows, :].astype(F32)
        conv, back = (
            jnp.concatenate([field[pl.ds(8 * h + offset + c, SEQ, stride=SEQ), :] for c in range(OWN)]).T
            for offset in (0, OWN)
        )
        mixed = conv + skip[...] * (key_wide * value_wide)
        output[rows, :] = (query_wide * mixed).astype(BF16)
        grad_query[rows, :] = (grad_wide * mixed).astype(BF16)
        dgated = back + skip[...] * (grad_wide * query_wide)
        grad_key[rows, :] = (dgated * value_wide).astype(BF16)
        grad_value[rows, :] = (dgated * key_wide).astype(BF16)


def forward_rows(fields, first_fwd, second_fwd, twiddle):
    cos, sin = twiddle[:, :SIDE], twiddle[:, SIDE:]
    turned = []
    for pair in range(0, len(fields), 2):
        stage = dot(first_fwd[...], data_left(jnp.concatenate(fields[pair : pair + 2], axis=1), 0))
        for k in range(2):
            re = stage[:SIDE, SIDE * k : SIDE * (k + 1)]
            im = stage[SIDE:, SIDE * k : SIDE * (k + 1)]
            turned.append(data_left(jnp.concatenate([re * cos - im * sin, re * sin + im * cos], axis=1), 1))
    return dot(jnp.concatenate(turned), second_fwd[...])


def inverse_rows(spectra, first_inv, second_inv, twiddle):
    cos, sin = twiddle[:, :SIDE], twiddle[:, SIDE:]
    stage = dot(jnp.concatenate([data_left(s, 1) for s in spectra]), second_inv[...])
    turned = []
    for k in range(len(spectra)):
        re = stage[SIDE * k : SIDE * (k + 1), :SIDE]
        im = stage[SIDE * k : SIDE * (k + 1), SIDE:]
        turned.append(jnp.concatenate([re * cos + im * sin, im * cos - re * sin]))
    fields = []
    for pair in range(0, len(spectra), 2):
        both = dot(first_inv[...], data_left(jnp.concatenate(turned[pair : pair + 2], axis=1), 0))
        fields += [both[:, :SIDE], both[:, SIDE:]]
    return fields


def filter_kernel(place, features, filter_in, filter_mid, filter_out,
                  hidden, cosines, mine, theirs, shaped):
    step = pl.program_id(0)
    own = own_channels(place())
    turn = 1.0 / (2.0 * math.pi)
    in_high, in_low = halves(filter_in[...].T * turn)
    weight1 = jnp.concatenate([in_high, in_low, in_high], axis=1)
    weight2 = weight_left(filter_mid[...].T * turn, 1)
    weight3 = picked(filter_out, own).T.astype(BF16)
    weight3 = jnp.concatenate([weight3[:, :64], weight3[:, :64], weight3[:, 64:]], axis=1)
    pieces = [pl.ds(PIECE * k, PIECE) for k in range(STEP // PIECE)]
    for piece in pieces:
        feature = features[:, piece]
        rows = jnp.concatenate([feature[:16], feature[:16], feature[16:]])
        sine, cosine = sine_cosine(dot(weight1, rows))
        cosines[pl.ds(0, 64), piece] = cosine
        hidden[pl.ds(0, 128), piece] = jnp.concatenate(halves(sine))
    for piece in pieces:
        rows = hidden[pl.ds(0, 128), piece]
        sine, cosine = sine_cosine(dot(weight2, jnp.concatenate([rows, rows[:64]])))
        cosines[pl.ds(64, 64), piece] = cosine
        hidden[pl.ds(128, 128), piece] = jnp.concatenate(halves(sine))
    for k, piece in enumerate(pieces):
        rows = hidden[pl.ds(128, 128), piece]
        values = dot(weight3, jnp.concatenate([rows, rows[:64]]))
        for m in range(PIECE // SIDE):
            row = 8 * (step * (STEP // SIDE) + k * (PIECE // SIDE) + m)
            shaped[pl.ds(pl.multiple_of(row, 8), 8), :] = values[:, SIDE * m : SIDE * (m + 1)]

    @pl.when(step == HALF // STEP - 1)
    def _():
        for c in range(OWN):
            mine[pl.ds(64 * c, 64), :] = shaped[pl.ds(c, 64, stride=8), :]
            theirs[pl.ds(64 * c, 64), :] = shaped[pl.ds(c + OWN, 64, stride=8), :]


def filter_fields(me, mine, other, decay):
    time = position_grid()
    lower = me % 2 == 0
    rates = jnp.sum(own_channels(me) * decay[...], axis=1, keepdims=True)
    for c in range(OWN):
        rate = rates[c : c + 1, :]
        window = jnp.exp(-rate * time) * jnp.sqrt(rate + 1.0 / LENGTH)
        here, there = mine[pl.ds(64 * c, 64), :], other[pl.ds(64 * c, 64), :]
        yield window, jnp.concatenate([jnp.where(lower, here, there), jnp.where(lower, there, here)]), rate


def spectrum_kernel(place, mine, other, decay, first_fwd, second_fwd, twiddle, spectrum):
    fields = [window * shaped for window, shaped, _ in filter_fields(place(), mine, other, decay)]
    spectrum[...] = forward_rows(fields, first_fwd, second_fwd, twiddle)


def correlate_kernel(place, field, shaped_mine, shaped_other, decay, first_fwd, second_fwd, twiddle, second_inv, first_inv,
                     spectra, mine, theirs, sums):
    fields = []
    for c in range(OWN):
        for offset in (0, OWN):
            fields.append(
                jnp.concatenate([field[pl.ds(8 * h + offset + c, SEQ, stride=SEQ), :] for h in range(ROWS // SIDE)])
            )
    spectra[...] = forward_rows(fields, first_fwd, second_fwd, twiddle)
    products = []
    for c in range(OWN):
        gated, incoming = (spectra[pl.ds(SIDE * k, SIDE), :] for k in (2 * c, 2 * c + 1))
        gated_re, gated_im = gated[:, :SIDE], gated[:, SIDE:]
        incoming_re, incoming_im = incoming[:, :SIDE], incoming[:, SIDE:]
        products.append(jnp.concatenate([gated_re * incoming_re + gated_im * incoming_im,
                                         gated_re * incoming_im - gated_im * incoming_re], axis=1))
    results = inverse_rows(products, first_inv, second_inv, twiddle)
    time = position_grid()
    me = place()
    lower = me % 2 == 0
    pair = lambda x: (jnp.where(lower, x, 0.0), jnp.where(lower, 0.0, x))
    for c, (window, shaped, rate) in enumerate(filter_fields(me, shaped_mine, shaped_other, decay)):
        dshaped = results[c] * window
        slope = 0.5 / (rate + 1.0 / LENGTH) - time
        for part, sum_row, value in (
            (mine, None, jnp.where(lower, dshaped[:64], dshaped[64:])),
            (theirs, None, jnp.where(lower, dshaped[64:], dshaped[:64])),
            (sums, 0, jnp.sum(dshaped * shaped * slope, axis=0, keepdims=True)),
            (sums, 8, jnp.sum(fields[2 * c] * fields[2 * c + 1], axis=0, keepdims=True)),
        ):
            for offset, v in zip((0, OWN), pair(value)):
                rows = pl.ds(c + offset, 64, stride=8) if sum_row is None else pl.ds(sum_row + c + offset, 1)
                part[rows, :] = v


def convolve_kernel(spectra, spectrum, twiddle, second_inv, first_inv, sent):
    products = []
    for c in range(OWN):
        gated, incoming = (spectra[pl.ds(SIDE * k, SIDE), :] for k in (2 * c, 2 * c + 1))
        kernel = spectrum[pl.ds(SIDE * c, SIDE), :]
        gated_re, gated_im = gated[:, :SIDE], gated[:, SIDE:]
        incoming_re, incoming_im = incoming[:, :SIDE], incoming[:, SIDE:]
        kernel_re, kernel_im = kernel[:, :SIDE], kernel[:, SIDE:]
        products += [
            jnp.concatenate([kernel_re * gated_re - kernel_im * gated_im,
                             kernel_re * gated_im + kernel_im * gated_re], axis=1),
            jnp.concatenate([kernel_re * incoming_re + kernel_im * incoming_im,
                             kernel_re * incoming_im - kernel_im * incoming_re], axis=1),
        ]
    results = inverse_rows(products, first_inv, second_inv, twiddle)
    for c in range(OWN):
        for offset, result in ((0, results[2 * c]), (OWN, results[2 * c + 1])):
            for h in range(ROWS // SIDE):
                sent[pl.ds(8 * h + offset + c, SEQ, stride=SEQ), :] = result[SEQ * h : SEQ * (h + 1), :]


def pair_channels(place):
    row = lax.broadcasted_iota(jnp.int32, (8, SIDE), 0)
    lane = lax.broadcasted_iota(jnp.int32, (8, SIDE), 1)
    return jnp.where(lane == place - place % 2 + row // OWN + SEQ * (row % OWN), 1.0, 0.0).astype(F32)


def backward_kernel(place, features, hidden, cosines, mine, other, sums, filter_mid, filter_out, grads, d2, d1, shaped):
    weight3 = picked(filter_out, pair_channels(place())).astype(BF16)
    weight3 = jnp.concatenate([weight3[:64], weight3[:64], weight3[64:]], axis=1)
    weight2 = weight_left(filter_mid[...], 1)
    pieces = range(0, HALF, PIECE)
    for start in pieces:
        piece = pl.ds(start, PIECE)
        tiles = range(start // SIDE, (start + PIECE) // SIDE)
        both = jnp.concatenate(
            halves(jnp.concatenate([mine[pl.ds(8 * m, 8), :] + other[pl.ds(8 * m, 8), :] for m in tiles], axis=1))
        )
        shaped[:, piece] = both
        rows = jnp.concatenate([both, both[:8]])
        d2[:, piece] = jnp.concatenate(halves(dot(weight3, rows) * cosines[pl.ds(64, 64), piece]))
    for start in pieces:
        piece = pl.ds(start, PIECE)
        rows = d2[:, piece]
        d1[:, piece] = jnp.concatenate(
            halves(dot(weight2, jnp.concatenate([rows, rows[:64]])) * cosines[pl.ds(0, 64), piece])
        )
    left = jnp.concatenate([hidden[...], d1[...]])
    right = jnp.concatenate([d2[...], shaped[...], features[...]])
    total = dot_nt(left, right)
    mid = total[:64, :64] + (total[:64, 64:128] + total[64:128, :64])
    grads[pl.ds(0, 32), :] = jnp.concatenate([mid[:32], mid[32:]], axis=1)
    side = [jnp.concatenate([total[64 * k : 64 * (k + 1), 128:], jnp.zeros((64, 80), F32)], axis=1).T for k in range(2, 6)]
    first = side[2][16:32] + (side[2][32:48] + side[3][16:32])
    third = side[0][:8] + (side[0][8:16] + side[1][:8])
    grads[pl.ds(32, 8), :] = jnp.concatenate([first[:8], first[8:]], axis=1)
    channels = pair_channels(place())
    rates = jnp.sum(sums[pl.ds(0, 8), :], axis=1, keepdims=True)
    gains = jnp.sum(sums[pl.ds(8, 8), :], axis=1, keepdims=True)
    grads[pl.ds(40, 64), :] = dot_tn(third, channels, lax.Precision.HIGHEST)
    grads[pl.ds(104, 8), :] = jnp.concatenate([
        jnp.sum(channels * rates, axis=0, keepdims=True),
        jnp.sum(channels * gains, axis=0, keepdims=True),
        jnp.zeros((6, SIDE), F32),
    ])


def finish_kernel(total, grad_in, grad_mid, grad_out, grad_decay, grad_skip):
    grad_mid[pl.ds(0, 32), :] = total[:32, :ORDER]
    grad_mid[pl.ds(32, 32), :] = total[:32, ORDER:]
    grad_in[pl.ds(0, 8), :] = total[32:40, :ORDER]
    grad_in[pl.ds(8, 8), :] = total[32:40, ORDER:]
    grad_out[...] = total[40:104]
    grad_decay[...] = total[104:105]
    grad_skip[...] = total[105:106]


def seq_place():
    return lax.axis_index(SEQ_AXES)


def run_send(query, key, value, grad, place=seq_place, **kw):
    whole = pl.BlockSpec(memory_space=pl.ANY)
    return call(
        functools.partial(send_kernel, place), 1, [whole] * 5, [spec((1024, SIDE)), whole],
        [out((1024, SIDE)), pltpu.HBM((32, HALF), BF16)],
        scratch=[pltpu.VMEM((4, ROWS, SIDE), BF16), pltpu.VMEM((32, HALF), BF16), pltpu.SemaphoreType.DMA((6,))], **kw,
    )(*[in_hbm(x) for x in (query, key, value, grad, jnp.asarray(feature_table()))])


def run_filter(features, filter_in, filter_mid, filter_out, place=seq_place, **kw):
    wide = lambda i: (0, i)
    return call(
        functools.partial(filter_kernel, place),
        HALF // STEP,
        [spec((32, STEP), wide), spec((16, ORDER)), spec((ORDER, ORDER)), spec((ORDER, SIDE))],
        [spec((256, STEP), wide), spec((SIDE, STEP), wide)] + [spec((256, SIDE))] * 2,
        [pltpu.HBM((256, HALF), BF16), pltpu.HBM((SIDE, HALF), F32), out((256, SIDE)), out((256, SIDE))],
        scratch=[pltpu.VMEM((512, SIDE), F32)],
        flops=4 * 10**9, nbytes=10 * MIB, **kw,
    )(in_hbm(features), in_hbm(filter_in), in_hbm(filter_mid), in_hbm(filter_out))


def run_spectrum(mine, other, decay, place=seq_place, **kw):
    first_fwd, second_fwd, twiddle, _, _ = transform_tables()
    return call(
        functools.partial(spectrum_kernel, place),
        1,
        [spec((256, SIDE))] * 2 + [spec((1, SIDE)), spec((256, 384)), spec((768, 256)), spec((SIDE, 256))],
        spec((512, 256)),
        out((512, 256)),
        flops=10**9, nbytes=MIB, **kw,
    )(mine, other, decay, first_fwd, second_fwd, twiddle)


def run_correlate(field, mine, other, decay, place=seq_place, **kw):
    first_fwd, second_fwd, twiddle, second_inv, first_inv = transform_tables()
    return call(
        functools.partial(correlate_kernel, place),
        1,
        [spec((1024, SIDE)), spec((256, SIDE)), spec((256, SIDE)), spec((1, SIDE)),
         spec((256, 384)), spec((768, 256)), spec((SIDE, 256)), spec((768, 256)), spec((SIDE, 768))],
        [spec((1024, 256)), spec((512, SIDE)), spec((512, SIDE)), spec((16, SIDE))],
        [out((1024, 256)), out((512, SIDE)), out((512, SIDE)), out((16, SIDE))],
        flops=2 * 10**9, nbytes=4 * MIB, **kw,
    )(field, mine, other, decay, first_fwd, second_fwd, twiddle, second_inv, first_inv)


def run_convolve(spectra, spectrum, **kw):
    _, _, twiddle, second_inv, first_inv = transform_tables()
    return call(
        convolve_kernel,
        1,
        [spec((1024, 256)), spec((512, 256)), spec((SIDE, 256)), spec((768, 256)), spec((SIDE, 768))],
        spec((1024, SIDE)),
        out((1024, SIDE)),
        flops=2 * 10**9, nbytes=3 * MIB, **kw,
    )(spectra, spectrum, twiddle, second_inv, first_inv)


def run_backward(features, hidden, mine, other, sums, filter_mid, filter_out, place=seq_place, **kw):
    held = pl.BlockSpec(memory_space=pltpu.VMEM)
    return call(
        functools.partial(backward_kernel, place),
        1,
        [held] * 6 + [spec((ORDER, ORDER)), spec((ORDER, SIDE))],
        spec((112, SIDE)),
        out((112, SIDE)),
        scratch=[pltpu.VMEM((SIDE, HALF), BF16)] * 2 + [pltpu.VMEM((16, HALF), BF16)],
        flops=4 * 10**9, nbytes=10 * MIB, **kw,
    )(features, *hidden, mine, other, sums, in_hbm(filter_mid), in_hbm(filter_out))


def run_receive(query, key, value, grad, skip, field, **kw):
    block = spec((ROWS, SIDE))
    return call(receive_kernel, 1, [block] * 4 + [spec((1, SIDE)), spec((1024, SIDE))], [block] * 4,
                [out((ROWS, SIDE), BF16)] * 4, **kw)(query, key, value, grad, skip, field)


def run_finish(total, **kw):
    shapes = [(16, ORDER), (ORDER, ORDER), (ORDER, SIDE), (1, SIDE), (1, SIDE)]
    return call(finish_kernel, 1, [spec((112, SIDE))], [spec(s) for s in shapes], [out(s) for s in shapes], **kw)(
        total
    )


def exchanged(x, axis, distance):
    return lax.ppermute(x, axis, [(i, i ^ distance) for i in range(lax.axis_size(axis))])


def group_sum(x, axis, distances):
    values = [x] + [exchanged(x, axis, d) for d in distances]
    while len(values) > 1:
        values = [a + b for a, b in zip(values[::2], values[1::2])]
    return values[0]


def body(query, key, value, grad, filter_in, filter_mid, filter_out, decay_rate, skip_gain):
    decay = decay_rate.reshape(1, SIDE)
    skip = skip_gain.reshape(1, SIDE)
    sent, features = run_send(query, key, value, grad)
    field = lax.all_to_all(sent.reshape(SEQ, SEQ, SIDE), SEQ_AXES, 0, 0, tiled=True).reshape(1024, SIDE)
    *hidden, mine, theirs = run_filter(features, filter_in, filter_mid, filter_out)
    other = exchanged(theirs, "core", 1)
    spectrum = run_spectrum(mine, other, decay)
    spectra, mine, theirs, sums = run_correlate(field, mine, other, decay)
    mine, spectrum = lax.optimization_barrier((mine, spectrum))
    grads = run_backward(features, hidden, mine, exchanged(theirs, "core", 1), sums, filter_mid, filter_out)
    grads, spectra = lax.optimization_barrier((grads, spectra))
    sent = run_convolve(spectra, spectrum)
    field = lax.all_to_all(sent.reshape(SEQ, SEQ, SIDE), SEQ_AXES, 0, 0, tiled=True).reshape(1024, SIDE)
    grads = group_sum(grads, "core", (1,))
    shared = group_sum(grads[:40], "chan", (1, 2, 3))
    shared, sent = lax.optimization_barrier((shared, sent))
    shared = group_sum(shared, "chan", (6,))
    grads = jnp.concatenate([shared, grads[40:]])
    grads = group_sum(grads, "x", (1, 2, 3))
    grads, field = lax.optimization_barrier((grads, field))
    grads = group_sum(grads, "y", (1, 2, 3))
    output, grad_query, grad_key, grad_value = run_receive(query, key, value, grad, skip, field)
    grads, output = lax.optimization_barrier((grads, output))
    first, second, third, rates, gains = run_finish(grads)
    return (output, grad_query, grad_key, grad_value, first, second, third, rates.reshape(SIDE), gains.reshape(SIDE))


def solution(mesh):
    parts = Mesh(mesh.devices.reshape(4, 4, 2, 8), SEQ_AXES + ("chan",))
    wide = P(SEQ_AXES, "chan")
    return jax.shard_map(
        body,
        mesh=parts,
        in_specs=(wide, wide, wide, wide, P(), P(), P(None, "chan"), P("chan"), P("chan")),
        out_specs=(wide, wide, wide, wide, P(), P(), P(None, "chan"), P("chan"), P("chan")),
        check_vma=False,
    )
```

```python
import functools
import math

import jax
import jax.numpy as jnp
import ml_dtypes
import numpy as np
from jax import lax
from jax.experimental import pallas as pl
from jax.experimental.pallas import tpu as pltpu
from jax.sharding import Mesh, PartitionSpec as P

F32 = jnp.float32
BF16 = jnp.bfloat16
LENGTH = 16384
SEQ = 32
ROWS = 512
SIDE = 128
OWN = 4
ORDER = 64
STEP = 2048
PIECE = 256
HALF = LENGTH // 2
MIB = 1 << 20
SEQ_AXES = ("x", "y", "core")


def split_table(table):
    high = table.astype(ml_dtypes.bfloat16)
    low = (table - high.astype(np.float64)).astype(ml_dtypes.bfloat16)
    return high, low


@functools.cache
def time_rows():
    p = np.arange(SIDE)
    return 4 * (p % SEQ) + p // SEQ


@functools.cache
def feature_table():
    t = (time_rows()[:, None] * SIDE + np.arange(SIDE)[None, :]).reshape(-1)
    rows = [t / LENGTH]
    angles = []
    for i in range(7):
        factor = max(1, LENGTH // 4 // 4 ** (6 - i))
        angles.append((factor * t % LENGTH) * (2.0 * math.pi / LENGTH))
    rows += [np.sin(a) for a in angles] + [np.cos(a) for a in angles] + [np.ones(LENGTH)]
    high, low = split_table(np.stack(rows).astype(np.float64))
    return np.concatenate([high, low])


@functools.cache
def transform_tables():
    idx = np.arange(SIDE)
    n1 = time_rows()
    first = np.exp(-2j * np.pi * ((n1[None, :] * idx[:, None] % SIDE) / SIDE + n1[None, :] / (4 * SIDE)))
    twiddle = np.exp(-2j * np.pi * idx[None, :] * (4 * idx[:, None] + 1) / (4 * LENGTH))
    second = np.exp(-2j * np.pi * (idx[:, None] * idx[None, :] % SIDE) / SIDE)
    high, low = split_table(np.concatenate([first.real, first.imag]))
    first_fwd = np.concatenate([high, high, low], axis=1)
    high, low = split_table(np.block([[second.real, second.imag], [-second.imag, second.real]]))
    second_fwd = np.concatenate([high, high, low])
    high, low = split_table(np.block([[second.real, -second.imag], [second.imag, second.real]]))
    second_inv = np.concatenate([high, high, low])
    high, low = split_table(np.concatenate([first.real.T, first.imag.T], axis=1) / LENGTH)
    first_inv = np.concatenate([high, high, low], axis=1)
    twiddle = np.concatenate([twiddle.real, twiddle.imag], axis=1).astype(np.float32)
    return first_fwd, second_fwd, twiddle, second_inv, first_inv


@functools.cache
def turn_polynomials():
    nodes = 0.5 * np.cos(np.pi * (np.arange(400) + 0.5) / 800)
    squares = nodes * nodes

    def fit(values, weight, count):
        basis = np.stack([squares**k for k in range(count)], axis=1)
        return np.linalg.lstsq(basis * weight[:, None], values, rcond=None)[0]

    sine = fit(np.sin(2 * np.pi * nodes), nodes, 6)
    cosine = fit(np.cos(2 * np.pi * nodes), np.ones_like(nodes), 6)
    return [float(c) for c in sine], [float(c) for c in cosine]


def sine_cosine(turns):
    sine, cosine = turn_polynomials()
    part = turns - jnp.round(turns)
    square = part * part
    s = jnp.full_like(square, sine[-1])
    for c in sine[-2::-1]:
        s = s * square + c
    c_out = jnp.full_like(square, cosine[-1])
    for c in cosine[-2::-1]:
        c_out = c_out * square + c
    return s * part, c_out


def halves(x):
    high = x.astype(BF16)
    return high, (x - high.astype(F32)).astype(BF16)


def dot(a, b):
    return jnp.dot(a, b, preferred_element_type=F32)


def dot_nt(a, b, precision=None):
    return lax.dot_general(a, b, (((1,), (1,)), ((), ())), precision=precision, preferred_element_type=F32)


def dot_tn(a, b, precision=None):
    return lax.dot_general(a, b, (((0,), (0,)), ((), ())), precision=precision, preferred_element_type=F32)


def data_left(x, axis):
    high, low = halves(x)
    return jnp.concatenate([high, low, high], axis=axis)


def weight_left(x, axis):
    high, low = halves(x)
    return jnp.concatenate([high, high, low], axis=axis)


def picked(filter_out, channels):
    return dot_nt(jnp.concatenate(halves(filter_out[...])), channels.astype(BF16))


def own_channels(place):
    row = lax.broadcasted_iota(jnp.int32, (8, SIDE), 0)
    lane = lax.broadcasted_iota(jnp.int32, (8, SIDE), 1)
    other = place + 1 - 2 * (place % 2)
    channel = jnp.where(row < OWN, place + SEQ * row, other + SEQ * (row - OWN))
    return jnp.where(lane == channel, 1.0, 0.0).astype(F32)


def position_grid():
    row = lax.broadcasted_iota(jnp.int32, (SIDE, SIDE), 0)
    lane = lax.broadcasted_iota(jnp.int32, (SIDE, SIDE), 1)
    return (ROWS * (row % SEQ) + SIDE * (row // SEQ) + lane).astype(F32)


def spec(shape, index=None):
    if index is None:
        zeros = (0,) * len(shape)
        return pl.BlockSpec(shape, lambda i: zeros)
    return pl.BlockSpec(shape, index)


def out(shape, dtype=F32):
    return jax.ShapeDtypeStruct(shape, dtype)


def in_hbm(x):
    return pltpu.with_memory_space_constraint(x, pltpu.HBM)


def call(kernel, grid, in_specs, out_specs, out_shape, scratch=(), limit=16, flops=1, nbytes=1, interpret=False):
    return pl.pallas_call(
        kernel,
        grid=(grid,),
        in_specs=in_specs,
        out_specs=out_specs,
        out_shape=out_shape,
        scratch_shapes=scratch,
        compiler_params=pltpu.CompilerParams(vmem_limit_bytes=limit * MIB),
        cost_estimate=pl.CostEstimate(flops=flops, bytes_accessed=nbytes, transcendentals=0),
        interpret=interpret,
    )


def send_kernel(place, query, key, value, grad, table, sent, features, held, half_held, sems):
    half = pl.ds(pl.multiple_of(HALF * (place() % 2), HALF), HALF)
    features_in = pltpu.make_async_copy(table.at[:, half], half_held, sems.at[4])
    features_out = pltpu.make_async_copy(half_held, features, sems.at[5])
    copies = [pltpu.make_async_copy(x, held.at[k], sems.at[k]) for k, x in enumerate((key, value, grad, query))]
    for copy in copies:
        copy.start()
    features_in.start()
    for offset, first, second in ((0, 0, 1), (OWN, 2, 3)):
        if offset:
            features_in.wait()
            features_out.start()
        copies[first].wait()
        copies[second].wait()
        for h in range(ROWS // SIDE):
            rows = pl.ds(SIDE * h, SIDE)
            block = (held[first, rows, :].astype(F32) * held[second, rows, :].astype(F32)).T
            for c in range(OWN):
                sent[pl.ds(8 * h + offset + c, SEQ, stride=SEQ), :] = block[SEQ * c : SEQ * (c + 1), :]
    features_out.wait()


def receive_kernel(query, key, value, grad, skip, field, output, grad_query, grad_key, grad_value):
    for h in range(ROWS // SIDE):
        rows = pl.ds(SIDE * h, SIDE)
        query_wide = query[rows, :].astype(F32)
        key_wide = key[rows, :].astype(F32)
        value_wide = value[rows, :].astype(F32)
        grad_wide = grad[rows, :].astype(F32)
        conv, back = (
            jnp.concatenate([field[pl.ds(8 * h + offset + c, SEQ, stride=SEQ), :] for c in range(OWN)]).T
            for offset in (0, OWN)
        )
        mixed = conv + skip[...] * (key_wide * value_wide)
        output[rows, :] = (query_wide * mixed).astype(BF16)
        grad_query[rows, :] = (grad_wide * mixed).astype(BF16)
        dgated = back + skip[...] * (grad_wide * query_wide)
        grad_key[rows, :] = (dgated * value_wide).astype(BF16)
        grad_value[rows, :] = (dgated * key_wide).astype(BF16)


def forward_rows(fields, first_fwd, second_fwd, twiddle):
    cos, sin = twiddle[:, :SIDE], twiddle[:, SIDE:]
    turned = []
    for pair in range(0, len(fields), 2):
        stage = dot(first_fwd[...], data_left(jnp.concatenate(fields[pair : pair + 2], axis=1), 0))
        for k in range(2):
            re = stage[:SIDE, SIDE * k : SIDE * (k + 1)]
            im = stage[SIDE:, SIDE * k : SIDE * (k + 1)]
            turned.append(data_left(jnp.concatenate([re * cos - im * sin, re * sin + im * cos], axis=1), 1))
    return dot(jnp.concatenate(turned), second_fwd[...])


def inverse_rows(spectra, first_inv, second_inv, twiddle):
    cos, sin = twiddle[:, :SIDE], twiddle[:, SIDE:]
    stage = dot(jnp.concatenate([data_left(s, 1) for s in spectra]), second_inv[...])
    turned = []
    for k in range(len(spectra)):
        re = stage[SIDE * k : SIDE * (k + 1), :SIDE]
        im = stage[SIDE * k : SIDE * (k + 1), SIDE:]
        turned.append(jnp.concatenate([re * cos + im * sin, im * cos - re * sin]))
    fields = []
    for pair in range(0, len(spectra), 2):
        both = dot(first_inv[...], data_left(jnp.concatenate(turned[pair : pair + 2], axis=1), 0))
        fields += [both[:, :SIDE], both[:, SIDE:]]
    return fields


def filter_kernel(place, features, filter_in, filter_mid, filter_out,
                  hidden, cosines, mine, theirs, shaped):
    step = pl.program_id(0)
    own = own_channels(place())
    turn = 1.0 / (2.0 * math.pi)
    in_high, in_low = halves(filter_in[...].T * turn)
    weight1 = jnp.concatenate([in_high, in_low, in_high], axis=1)
    weight2 = weight_left(filter_mid[...].T * turn, 1)
    weight3 = picked(filter_out, own).T.astype(BF16)
    weight3 = jnp.concatenate([weight3[:, :64], weight3[:, :64], weight3[:, 64:]], axis=1)
    pieces = [pl.ds(PIECE * k, PIECE) for k in range(STEP // PIECE)]
    for piece in pieces:
        feature = features[:, piece]
        rows = jnp.concatenate([feature[:16], feature[:16], feature[16:]])
        sine, cosine = sine_cosine(dot(weight1, rows))
        cosines[pl.ds(0, 64), piece] = cosine
        hidden[pl.ds(0, 128), piece] = jnp.concatenate(halves(sine))
    for piece in pieces:
        rows = hidden[pl.ds(0, 128), piece]
        sine, cosine = sine_cosine(dot(weight2, jnp.concatenate([rows, rows[:64]])))
        cosines[pl.ds(64, 64), piece] = cosine
        hidden[pl.ds(128, 128), piece] = jnp.concatenate(halves(sine))
    for k, piece in enumerate(pieces):
        rows = hidden[pl.ds(128, 128), piece]
        values = dot(weight3, jnp.concatenate([rows, rows[:64]]))
        for m in range(PIECE // SIDE):
            row = 8 * (step * (STEP // SIDE) + k * (PIECE // SIDE) + m)
            shaped[pl.ds(pl.multiple_of(row, 8), 8), :] = values[:, SIDE * m : SIDE * (m + 1)]

    @pl.when(step == HALF // STEP - 1)
    def _():
        for c in range(OWN):
            mine[pl.ds(64 * c, 64), :] = shaped[pl.ds(c, 64, stride=8), :]
            theirs[pl.ds(64 * c, 64), :] = shaped[pl.ds(c + OWN, 64, stride=8), :]


def filter_fields(me, mine, other, decay):
    time = position_grid()
    lower = me % 2 == 0
    rates = jnp.sum(own_channels(me) * decay[...], axis=1, keepdims=True)
    for c in range(OWN):
        rate = rates[c : c + 1, :]
        window = jnp.exp(-rate * time) * jnp.sqrt(rate + 1.0 / LENGTH)
        here, there = mine[pl.ds(64 * c, 64), :], other[pl.ds(64 * c, 64), :]
        yield window, jnp.concatenate([jnp.where(lower, here, there), jnp.where(lower, there, here)]), rate


def spectrum_kernel(place, mine, other, decay, first_fwd, second_fwd, twiddle, spectrum):
    fields = [window * shaped for window, shaped, _ in filter_fields(place(), mine, other, decay)]
    spectrum[...] = forward_rows(fields, first_fwd, second_fwd, twiddle)


def correlate_kernel(place, field, shaped_mine, shaped_other, decay, first_fwd, second_fwd, twiddle, second_inv, first_inv,
                     spectra, mine, theirs, sums):
    fields = []
    for c in range(OWN):
        for offset in (0, OWN):
            fields.append(
                jnp.concatenate([field[pl.ds(8 * h + offset + c, SEQ, stride=SEQ), :] for h in range(ROWS // SIDE)])
            )
    spectra[...] = forward_rows(fields, first_fwd, second_fwd, twiddle)
    products = []
    for c in range(OWN):
        gated, incoming = (spectra[pl.ds(SIDE * k, SIDE), :] for k in (2 * c, 2 * c + 1))
        gated_re, gated_im = gated[:, :SIDE], gated[:, SIDE:]
        incoming_re, incoming_im = incoming[:, :SIDE], incoming[:, SIDE:]
        products.append(jnp.concatenate([gated_re * incoming_re + gated_im * incoming_im,
                                         gated_re * incoming_im - gated_im * incoming_re], axis=1))
    results = inverse_rows(products, first_inv, second_inv, twiddle)
    time = position_grid()
    me = place()
    lower = me % 2 == 0
    pair = lambda x: (jnp.where(lower, x, 0.0), jnp.where(lower, 0.0, x))
    for c, (window, shaped, rate) in enumerate(filter_fields(me, shaped_mine, shaped_other, decay)):
        dshaped = results[c] * window
        slope = 0.5 / (rate + 1.0 / LENGTH) - time
        for part, sum_row, value in (
            (mine, None, jnp.where(lower, dshaped[:64], dshaped[64:])),
            (theirs, None, jnp.where(lower, dshaped[64:], dshaped[:64])),
            (sums, 0, jnp.sum(dshaped * shaped * slope, axis=0, keepdims=True)),
            (sums, 8, jnp.sum(fields[2 * c] * fields[2 * c + 1], axis=0, keepdims=True)),
        ):
            for offset, v in zip((0, OWN), pair(value)):
                rows = pl.ds(c + offset, 64, stride=8) if sum_row is None else pl.ds(sum_row + c + offset, 1)
                part[rows, :] = v


def convolve_kernel(spectra, spectrum, twiddle, second_inv, first_inv, sent):
    products = []
    for c in range(OWN):
        gated, incoming = (spectra[pl.ds(SIDE * k, SIDE), :] for k in (2 * c, 2 * c + 1))
        kernel = spectrum[pl.ds(SIDE * c, SIDE), :]
        gated_re, gated_im = gated[:, :SIDE], gated[:, SIDE:]
        incoming_re, incoming_im = incoming[:, :SIDE], incoming[:, SIDE:]
        kernel_re, kernel_im = kernel[:, :SIDE], kernel[:, SIDE:]
        products += [
            jnp.concatenate([kernel_re * gated_re - kernel_im * gated_im,
                             kernel_re * gated_im + kernel_im * gated_re], axis=1),
            jnp.concatenate([kernel_re * incoming_re + kernel_im * incoming_im,
                             kernel_re * incoming_im - kernel_im * incoming_re], axis=1),
        ]
    results = inverse_rows(products, first_inv, second_inv, twiddle)
    for c in range(OWN):
        for offset, result in ((0, results[2 * c]), (OWN, results[2 * c + 1])):
            for h in range(ROWS // SIDE):
                sent[pl.ds(8 * h + offset + c, SEQ, stride=SEQ), :] = result[SEQ * h : SEQ * (h + 1), :]


def pair_channels(place):
    row = lax.broadcasted_iota(jnp.int32, (8, SIDE), 0)
    lane = lax.broadcasted_iota(jnp.int32, (8, SIDE), 1)
    return jnp.where(lane == place - place % 2 + row // OWN + SEQ * (row % OWN), 1.0, 0.0).astype(F32)


def backward_kernel(place, features, hidden, cosines, mine, other, sums, filter_mid, filter_out, grads, d2, d1, shaped):
    weight3 = picked(filter_out, pair_channels(place())).astype(BF16)
    weight3 = jnp.concatenate([weight3[:64], weight3[:64], weight3[64:]], axis=1)
    weight2 = weight_left(filter_mid[...], 1)
    pieces = range(0, HALF, PIECE)
    for start in pieces:
        piece = pl.ds(start, PIECE)
        tiles = range(start // SIDE, (start + PIECE) // SIDE)
        both = jnp.concatenate(
            halves(jnp.concatenate([mine[pl.ds(8 * m, 8), :] + other[pl.ds(8 * m, 8), :] for m in tiles], axis=1))
        )
        shaped[:, piece] = both
        rows = jnp.concatenate([both, both[:8]])
        d2[:, piece] = jnp.concatenate(halves(dot(weight3, rows) * cosines[pl.ds(64, 64), piece]))
    for start in pieces:
        piece = pl.ds(start, PIECE)
        rows = d2[:, piece]
        d1[:, piece] = jnp.concatenate(
            halves(dot(weight2, jnp.concatenate([rows, rows[:64]])) * cosines[pl.ds(0, 64), piece])
        )
    left = jnp.concatenate([hidden[...], d1[...]])
    right = jnp.concatenate([d2[...], shaped[...], features[...]])
    total = dot_nt(left, right)
    mid = total[:64, :64] + (total[:64, 64:128] + total[64:128, :64])
    grads[pl.ds(0, 32), :] = jnp.concatenate([mid[:32], mid[32:]], axis=1)
    side = [jnp.concatenate([total[64 * k : 64 * (k + 1), 128:], jnp.zeros((64, 80), F32)], axis=1).T for k in range(2, 6)]
    first = side[2][16:32] + (side[2][32:48] + side[3][16:32])
    third = side[0][:8] + (side[0][8:16] + side[1][:8])
    grads[pl.ds(32, 8), :] = jnp.concatenate([first[:8], first[8:]], axis=1)
    channels = pair_channels(place())
    rates = jnp.sum(sums[pl.ds(0, 8), :], axis=1, keepdims=True)
    gains = jnp.sum(sums[pl.ds(8, 8), :], axis=1, keepdims=True)
    grads[pl.ds(40, 64), :] = dot_tn(third, channels, lax.Precision.HIGHEST)
    grads[pl.ds(104, 8), :] = jnp.concatenate([
        jnp.sum(channels * rates, axis=0, keepdims=True),
        jnp.sum(channels * gains, axis=0, keepdims=True),
        jnp.zeros((6, SIDE), F32),
    ])


def finish_kernel(total, grad_in, grad_mid, grad_out, grad_decay, grad_skip):
    grad_mid[pl.ds(0, 32), :] = total[:32, :ORDER]
    grad_mid[pl.ds(32, 32), :] = total[:32, ORDER:]
    grad_in[pl.ds(0, 8), :] = total[32:40, :ORDER]
    grad_in[pl.ds(8, 8), :] = total[32:40, ORDER:]
    grad_out[...] = total[40:104]
    grad_decay[...] = total[104:105]
    grad_skip[...] = total[105:106]


def seq_place():
    return lax.axis_index(SEQ_AXES)


def run_send(query, key, value, grad, place=seq_place, **kw):
    whole = pl.BlockSpec(memory_space=pl.ANY)
    return call(
        functools.partial(send_kernel, place), 1, [whole] * 5, [spec((1024, SIDE)), whole],
        [out((1024, SIDE)), pltpu.HBM((32, HALF), BF16)],
        scratch=[pltpu.VMEM((4, ROWS, SIDE), BF16), pltpu.VMEM((32, HALF), BF16), pltpu.SemaphoreType.DMA((6,))], **kw,
    )(*[in_hbm(x) for x in (query, key, value, grad, jnp.asarray(feature_table()))])


def run_filter(features, filter_in, filter_mid, filter_out, place=seq_place, **kw):
    wide = lambda i: (0, i)
    return call(
        functools.partial(filter_kernel, place),
        HALF // STEP,
        [spec((32, STEP), wide), spec((16, ORDER)), spec((ORDER, ORDER)), spec((ORDER, SIDE))],
        [spec((256, STEP), wide), spec((SIDE, STEP), wide)] + [spec((256, SIDE))] * 2,
        [pltpu.HBM((256, HALF), BF16), pltpu.HBM((SIDE, HALF), F32), out((256, SIDE)), out((256, SIDE))],
        scratch=[pltpu.VMEM((512, SIDE), F32)],
        flops=4 * 10**9, nbytes=10 * MIB, **kw,
    )(in_hbm(features), in_hbm(filter_in), in_hbm(filter_mid), in_hbm(filter_out))


def run_spectrum(mine, other, decay, place=seq_place, **kw):
    first_fwd, second_fwd, twiddle, _, _ = transform_tables()
    return call(
        functools.partial(spectrum_kernel, place),
        1,
        [spec((256, SIDE))] * 2 + [spec((1, SIDE)), spec((256, 384)), spec((768, 256)), spec((SIDE, 256))],
        spec((512, 256)),
        out((512, 256)),
        flops=10**9, nbytes=MIB, **kw,
    )(mine, other, decay, first_fwd, second_fwd, twiddle)


def run_correlate(field, mine, other, decay, place=seq_place, **kw):
    first_fwd, second_fwd, twiddle, second_inv, first_inv = transform_tables()
    return call(
        functools.partial(correlate_kernel, place),
        1,
        [spec((1024, SIDE)), spec((256, SIDE)), spec((256, SIDE)), spec((1, SIDE)),
         spec((256, 384)), spec((768, 256)), spec((SIDE, 256)), spec((768, 256)), spec((SIDE, 768))],
        [spec((1024, 256)), spec((512, SIDE)), spec((512, SIDE)), spec((16, SIDE))],
        [out((1024, 256)), out((512, SIDE)), out((512, SIDE)), out((16, SIDE))],
        flops=2 * 10**9, nbytes=4 * MIB, **kw,
    )(field, mine, other, decay, first_fwd, second_fwd, twiddle, second_inv, first_inv)


def run_convolve(spectra, spectrum, **kw):
    _, _, twiddle, second_inv, first_inv = transform_tables()
    return call(
        convolve_kernel,
        1,
        [spec((1024, 256)), spec((512, 256)), spec((SIDE, 256)), spec((768, 256)), spec((SIDE, 768))],
        spec((1024, SIDE)),
        out((1024, SIDE)),
        flops=2 * 10**9, nbytes=3 * MIB, **kw,
    )(spectra, spectrum, twiddle, second_inv, first_inv)


def run_backward(features, hidden, mine, other, sums, filter_mid, filter_out, place=seq_place, **kw):
    held = pl.BlockSpec(memory_space=pltpu.VMEM)
    return call(
        functools.partial(backward_kernel, place),
        1,
        [held] * 6 + [spec((ORDER, ORDER)), spec((ORDER, SIDE))],
        spec((112, SIDE)),
        out((112, SIDE)),
        scratch=[pltpu.VMEM((SIDE, HALF), BF16)] * 2 + [pltpu.VMEM((16, HALF), BF16)],
        flops=4 * 10**9, nbytes=10 * MIB, **kw,
    )(features, *hidden, mine, other, sums, in_hbm(filter_mid), in_hbm(filter_out))


def run_receive(query, key, value, grad, skip, field, **kw):
    block = spec((ROWS, SIDE))
    return call(receive_kernel, 1, [block] * 4 + [spec((1, SIDE)), spec((1024, SIDE))], [block] * 4,
                [out((ROWS, SIDE), BF16)] * 4, **kw)(query, key, value, grad, skip, field)


def run_finish(total, **kw):
    shapes = [(16, ORDER), (ORDER, ORDER), (ORDER, SIDE), (1, SIDE), (1, SIDE)]
    return call(finish_kernel, 1, [spec((112, SIDE))], [spec(s) for s in shapes], [out(s) for s in shapes], **kw)(
        total
    )


def exchanged(x, axis, distance):
    return lax.ppermute(x, axis, [(i, i ^ distance) for i in range(lax.axis_size(axis))])


def group_sum(x, axis, distances):
    values = [x] + [exchanged(x, axis, d) for d in distances]
    while len(values) > 1:
        values = [a + b for a, b in zip(values[::2], values[1::2])]
    return values[0]


def body(query, key, value, grad, filter_in, filter_mid, filter_out, decay_rate, skip_gain):
    decay = decay_rate.reshape(1, SIDE)
    skip = skip_gain.reshape(1, SIDE)
    sent, features = run_send(query, key, value, grad)
    field = lax.all_to_all(sent.reshape(SEQ, SEQ, SIDE), SEQ_AXES, 0, 0, tiled=True).reshape(1024, SIDE)
    *hidden, mine, theirs = run_filter(features, filter_in, filter_mid, filter_out)
    other = exchanged(theirs, "core", 1)
    spectrum = run_spectrum(mine, other, decay)
    spectra, mine, theirs, sums = run_correlate(field, mine, other, decay)
    mine, spectrum = lax.optimization_barrier((mine, spectrum))
    grads = run_backward(features, hidden, mine, exchanged(theirs, "core", 1), sums, filter_mid, filter_out)
    grads, spectra = lax.optimization_barrier((grads, spectra))
    sent = run_convolve(spectra, spectrum)
    other = exchanged(grads, "core", 1)
    other, sent = lax.optimization_barrier((other, sent))
    grads = grads + other
    field = lax.all_to_all(sent.reshape(SEQ, SEQ, SIDE), SEQ_AXES, 0, 0, tiled=True).reshape(1024, SIDE)
    shared = group_sum(grads[:40], "chan", (1, 2, 3))
    shared = group_sum(shared, "chan", (6,))
    grads = jnp.concatenate([shared, grads[40:]])
    grads = group_sum(grads, "x", (1, 2, 3))
    grads, field = lax.optimization_barrier((grads, field))
    grads = group_sum(grads, "y", (1, 2, 3))
    output, grad_query, grad_key, grad_value = run_receive(query, key, value, grad, skip, field)
    grads, output = lax.optimization_barrier((grads, output))
    first, second, third, rates, gains = run_finish(grads)
    return (output, grad_query, grad_key, grad_value, first, second, third, rates.reshape(SIDE), gains.reshape(SIDE))


def solution(mesh):
    parts = Mesh(mesh.devices.reshape(4, 4, 2, 8), SEQ_AXES + ("chan",))
    wide = P(SEQ_AXES, "chan")
    return jax.shard_map(
        body,
        mesh=parts,
        in_specs=(wide, wide, wide, wide, P(), P(), P(None, "chan"), P("chan"), P("chan")),
        out_specs=(wide, wide, wide, wide, P(), P(), P(None, "chan"), P("chan"), P("chan")),
        check_vma=False,
    )
```

```python
import functools
import math

import jax
import jax.numpy as jnp
import ml_dtypes
import numpy as np
from jax import lax
from jax.experimental import pallas as pl
from jax.experimental.pallas import tpu as pltpu
from jax.sharding import Mesh, PartitionSpec as P

F32 = jnp.float32
BF16 = jnp.bfloat16
LENGTH = 16384
SEQ = 32
ROWS = 512
SIDE = 128
OWN = 4
ORDER = 64
STEP = 2048
PIECE = 256
HALF = LENGTH // 2
MIB = 1 << 20
SEQ_AXES = ("x", "y", "core")


def split_table(table):
    high = table.astype(ml_dtypes.bfloat16)
    low = (table - high.astype(np.float64)).astype(ml_dtypes.bfloat16)
    return high, low


@functools.cache
def time_rows():
    p = np.arange(SIDE)
    return 4 * (p % SEQ) + p // SEQ


@functools.cache
def feature_table():
    t = (time_rows()[:, None] * SIDE + np.arange(SIDE)[None, :]).reshape(-1)
    rows = [t / LENGTH]
    angles = []
    for i in range(7):
        factor = max(1, LENGTH // 4 // 4 ** (6 - i))
        angles.append((factor * t % LENGTH) * (2.0 * math.pi / LENGTH))
    rows += [np.sin(a) for a in angles] + [np.cos(a) for a in angles] + [np.ones(LENGTH)]
    high, low = split_table(np.stack(rows).astype(np.float64))
    return np.concatenate([high, low])


@functools.cache
def transform_tables():
    idx = np.arange(SIDE)
    n1 = time_rows()
    first = np.exp(-2j * np.pi * ((n1[None, :] * idx[:, None] % SIDE) / SIDE + n1[None, :] / (4 * SIDE)))
    twiddle = np.exp(-2j * np.pi * idx[None, :] * (4 * idx[:, None] + 1) / (4 * LENGTH))
    second = np.exp(-2j * np.pi * (idx[:, None] * idx[None, :] % SIDE) / SIDE)
    high, low = split_table(np.concatenate([first.real, first.imag]))
    first_fwd = np.concatenate([high, high, low], axis=1)
    high, low = split_table(np.block([[second.real, second.imag], [-second.imag, second.real]]))
    second_fwd = np.concatenate([high, high, low])
    high, low = split_table(np.block([[second.real, -second.imag], [second.imag, second.real]]))
    second_inv = np.concatenate([high, high, low])
    high, low = split_table(np.concatenate([first.real.T, first.imag.T], axis=1) / LENGTH)
    first_inv = np.concatenate([high, high, low], axis=1)
    twiddle = np.concatenate([twiddle.real, twiddle.imag], axis=1).astype(np.float32)
    return first_fwd, second_fwd, twiddle, second_inv, first_inv


@functools.cache
def turn_polynomials():
    nodes = 0.5 * np.cos(np.pi * (np.arange(400) + 0.5) / 800)
    squares = nodes * nodes

    def fit(values, weight, count):
        basis = np.stack([squares**k for k in range(count)], axis=1)
        return np.linalg.lstsq(basis * weight[:, None], values, rcond=None)[0]

    sine = fit(np.sin(2 * np.pi * nodes), nodes, 6)
    cosine = fit(np.cos(2 * np.pi * nodes), np.ones_like(nodes), 6)
    return [float(c) for c in sine], [float(c) for c in cosine]


def sine_cosine(turns):
    sine, cosine = turn_polynomials()
    part = turns - jnp.round(turns)
    square = part * part
    s = jnp.full_like(square, sine[-1])
    for c in sine[-2::-1]:
        s = s * square + c
    c_out = jnp.full_like(square, cosine[-1])
    for c in cosine[-2::-1]:
        c_out = c_out * square + c
    return s * part, c_out


def halves(x):
    high = x.astype(BF16)
    return high, (x - high.astype(F32)).astype(BF16)


def dot(a, b):
    return jnp.dot(a, b, preferred_element_type=F32)


def dot_nt(a, b, precision=None):
    return lax.dot_general(a, b, (((1,), (1,)), ((), ())), precision=precision, preferred_element_type=F32)


def dot_tn(a, b, precision=None):
    return lax.dot_general(a, b, (((0,), (0,)), ((), ())), precision=precision, preferred_element_type=F32)


def data_left(x, axis):
    high, low = halves(x)
    return jnp.concatenate([high, low, high], axis=axis)


def weight_left(x, axis):
    high, low = halves(x)
    return jnp.concatenate([high, high, low], axis=axis)


def picked(filter_out, channels):
    return dot_nt(jnp.concatenate(halves(filter_out[...])), channels.astype(BF16))


def own_channels(place):
    row = lax.broadcasted_iota(jnp.int32, (8, SIDE), 0)
    lane = lax.broadcasted_iota(jnp.int32, (8, SIDE), 1)
    other = place + 1 - 2 * (place % 2)
    channel = jnp.where(row < OWN, place + SEQ * row, other + SEQ * (row - OWN))
    return jnp.where(lane == channel, 1.0, 0.0).astype(F32)


def position_grid():
    row = lax.broadcasted_iota(jnp.int32, (SIDE, SIDE), 0)
    lane = lax.broadcasted_iota(jnp.int32, (SIDE, SIDE), 1)
    return (ROWS * (row % SEQ) + SIDE * (row // SEQ) + lane).astype(F32)


def spec(shape, index=None):
    if index is None:
        zeros = (0,) * len(shape)
        return pl.BlockSpec(shape, lambda i: zeros)
    return pl.BlockSpec(shape, index)


def out(shape, dtype=F32):
    return jax.ShapeDtypeStruct(shape, dtype)


def in_hbm(x):
    return pltpu.with_memory_space_constraint(x, pltpu.HBM)


def call(kernel, grid, in_specs, out_specs, out_shape, scratch=(), limit=16, flops=1, nbytes=1, interpret=False):
    return pl.pallas_call(
        kernel,
        grid=(grid,),
        in_specs=in_specs,
        out_specs=out_specs,
        out_shape=out_shape,
        scratch_shapes=scratch,
        compiler_params=pltpu.CompilerParams(vmem_limit_bytes=limit * MIB),
        cost_estimate=pl.CostEstimate(flops=flops, bytes_accessed=nbytes, transcendentals=0),
        interpret=interpret,
    )


def send_kernel(query, key, value, grad, sent, held, sems):
    copies = [pltpu.make_async_copy(x, held.at[k], sems.at[k]) for k, x in enumerate((key, value, grad, query))]
    for copy in copies:
        copy.start()
    for offset, first, second in ((0, 0, 1), (OWN, 2, 3)):
        copies[first].wait()
        copies[second].wait()
        for h in range(ROWS // SIDE):
            rows = pl.ds(SIDE * h, SIDE)
            block = (held[first, rows, :].astype(F32) * held[second, rows, :].astype(F32)).T
            for c in range(OWN):
                sent[pl.ds(8 * h + offset + c, SEQ, stride=SEQ), :] = block[SEQ * c : SEQ * (c + 1), :]


def receive_kernel(query, key, value, grad, skip, field, output, grad_query, grad_key, grad_value):
    for h in range(ROWS // SIDE):
        rows = pl.ds(SIDE * h, SIDE)
        query_wide = query[rows, :].astype(F32)
        key_wide = key[rows, :].astype(F32)
        value_wide = value[rows, :].astype(F32)
        grad_wide = grad[rows, :].astype(F32)
        conv, back = (
            jnp.concatenate([field[pl.ds(8 * h + offset + c, SEQ, stride=SEQ), :] for c in range(OWN)]).T
            for offset in (0, OWN)
        )
        mixed = conv + skip[...] * (key_wide * value_wide)
        output[rows, :] = (query_wide * mixed).astype(BF16)
        grad_query[rows, :] = (grad_wide * mixed).astype(BF16)
        dgated = back + skip[...] * (grad_wide * query_wide)
        grad_key[rows, :] = (dgated * value_wide).astype(BF16)
        grad_value[rows, :] = (dgated * key_wide).astype(BF16)


def forward_rows(fields, first_fwd, second_fwd, twiddle):
    cos, sin = twiddle[:, :SIDE], twiddle[:, SIDE:]
    turned = []
    for pair in range(0, len(fields), 2):
        stage = dot(first_fwd[...], data_left(jnp.concatenate(fields[pair : pair + 2], axis=1), 0))
        for k in range(2):
            re = stage[:SIDE, SIDE * k : SIDE * (k + 1)]
            im = stage[SIDE:, SIDE * k : SIDE * (k + 1)]
            turned.append(data_left(jnp.concatenate([re * cos - im * sin, re * sin + im * cos], axis=1), 1))
    return dot(jnp.concatenate(turned), second_fwd[...])


def inverse_rows(spectra, first_inv, second_inv, twiddle):
    cos, sin = twiddle[:, :SIDE], twiddle[:, SIDE:]
    stage = dot(jnp.concatenate([data_left(s, 1) for s in spectra]), second_inv[...])
    turned = []
    for k in range(len(spectra)):
        re = stage[SIDE * k : SIDE * (k + 1), :SIDE]
        im = stage[SIDE * k : SIDE * (k + 1), SIDE:]
        turned.append(jnp.concatenate([re * cos + im * sin, im * cos - re * sin]))
    fields = []
    for pair in range(0, len(spectra), 2):
        both = dot(first_inv[...], data_left(jnp.concatenate(turned[pair : pair + 2], axis=1), 0))
        fields += [both[:, :SIDE], both[:, SIDE:]]
    return fields


def filter_kernel(place, features, filter_in, filter_mid, filter_out,
                  hidden, cosines, mine, theirs, shaped):
    step = pl.program_id(0)
    own = own_channels(place())
    turn = 1.0 / (2.0 * math.pi)
    in_high, in_low = halves(filter_in[...].T * turn)
    weight1 = jnp.concatenate([in_high, in_low, in_high], axis=1)
    weight2 = weight_left(filter_mid[...].T * turn, 1)
    weight3 = picked(filter_out, own).T.astype(BF16)
    weight3 = jnp.concatenate([weight3[:, :64], weight3[:, :64], weight3[:, 64:]], axis=1)
    pieces = [pl.ds(PIECE * k, PIECE) for k in range(STEP // PIECE)]
    for piece in pieces:
        feature = features[:, piece]
        rows = jnp.concatenate([feature[:16], feature[:16], feature[16:]])
        sine, cosine = sine_cosine(dot(weight1, rows))
        cosines[pl.ds(0, 64), piece] = cosine
        hidden[pl.ds(0, 128), piece] = jnp.concatenate(halves(sine))
    for piece in pieces:
        rows = hidden[pl.ds(0, 128), piece]
        sine, cosine = sine_cosine(dot(weight2, jnp.concatenate([rows, rows[:64]])))
        cosines[pl.ds(64, 64), piece] = cosine
        hidden[pl.ds(128, 128), piece] = jnp.concatenate(halves(sine))
    for k, piece in enumerate(pieces):
        rows = hidden[pl.ds(128, 128), piece]
        values = dot(weight3, jnp.concatenate([rows, rows[:64]]))
        for m in range(PIECE // SIDE):
            row = 8 * (step * (STEP // SIDE) + k * (PIECE // SIDE) + m)
            shaped[pl.ds(pl.multiple_of(row, 8), 8), :] = values[:, SIDE * m : SIDE * (m + 1)]

    @pl.when(step == HALF // STEP - 1)
    def _():
        for c in range(OWN):
            mine[pl.ds(64 * c, 64), :] = shaped[pl.ds(c, 64, stride=8), :]
            theirs[pl.ds(64 * c, 64), :] = shaped[pl.ds(c + OWN, 64, stride=8), :]


def filter_fields(me, mine, other, decay):
    time = position_grid()
    lower = me % 2 == 0
    rates = jnp.sum(own_channels(me) * decay[...], axis=1, keepdims=True)
    for c in range(OWN):
        rate = rates[c : c + 1, :]
        window = jnp.exp(-rate * time) * jnp.sqrt(rate + 1.0 / LENGTH)
        here, there = mine[pl.ds(64 * c, 64), :], other[pl.ds(64 * c, 64), :]
        yield window, jnp.concatenate([jnp.where(lower, here, there), jnp.where(lower, there, here)]), rate


def spectrum_kernel(place, mine, other, decay, first_fwd, second_fwd, twiddle, spectrum):
    fields = [window * shaped for window, shaped, _ in filter_fields(place(), mine, other, decay)]
    spectrum[...] = forward_rows(fields, first_fwd, second_fwd, twiddle)


def correlate_kernel(place, field, shaped_mine, shaped_other, decay, first_fwd, second_fwd, twiddle, second_inv, first_inv,
                     spectra, mine, theirs, sums):
    fields = []
    for c in range(OWN):
        for offset in (0, OWN):
            fields.append(
                jnp.concatenate([field[pl.ds(8 * h + offset + c, SEQ, stride=SEQ), :] for h in range(ROWS // SIDE)])
            )
    spectra[...] = forward_rows(fields, first_fwd, second_fwd, twiddle)
    products = []
    for c in range(OWN):
        gated, incoming = (spectra[pl.ds(SIDE * k, SIDE), :] for k in (2 * c, 2 * c + 1))
        gated_re, gated_im = gated[:, :SIDE], gated[:, SIDE:]
        incoming_re, incoming_im = incoming[:, :SIDE], incoming[:, SIDE:]
        products.append(jnp.concatenate([gated_re * incoming_re + gated_im * incoming_im,
                                         gated_re * incoming_im - gated_im * incoming_re], axis=1))
    results = inverse_rows(products, first_inv, second_inv, twiddle)
    time = position_grid()
    me = place()
    lower = me % 2 == 0
    pair = lambda x: (jnp.where(lower, x, 0.0), jnp.where(lower, 0.0, x))
    for c, (window, shaped, rate) in enumerate(filter_fields(me, shaped_mine, shaped_other, decay)):
        dshaped = results[c] * window
        slope = 0.5 / (rate + 1.0 / LENGTH) - time
        for part, sum_row, value in (
            (mine, None, jnp.where(lower, dshaped[:64], dshaped[64:])),
            (theirs, None, jnp.where(lower, dshaped[64:], dshaped[:64])),
            (sums, 0, jnp.sum(dshaped * shaped * slope, axis=0, keepdims=True)),
            (sums, 8, jnp.sum(fields[2 * c] * fields[2 * c + 1], axis=0, keepdims=True)),
        ):
            for offset, v in zip((0, OWN), pair(value)):
                rows = pl.ds(c + offset, 64, stride=8) if sum_row is None else pl.ds(sum_row + c + offset, 1)
                part[rows, :] = v


def convolve_kernel(spectra, spectrum, twiddle, second_inv, first_inv, sent):
    products = []
    for c in range(OWN):
        gated, incoming = (spectra[pl.ds(SIDE * k, SIDE), :] for k in (2 * c, 2 * c + 1))
        kernel = spectrum[pl.ds(SIDE * c, SIDE), :]
        gated_re, gated_im = gated[:, :SIDE], gated[:, SIDE:]
        incoming_re, incoming_im = incoming[:, :SIDE], incoming[:, SIDE:]
        kernel_re, kernel_im = kernel[:, :SIDE], kernel[:, SIDE:]
        products += [
            jnp.concatenate([kernel_re * gated_re - kernel_im * gated_im,
                             kernel_re * gated_im + kernel_im * gated_re], axis=1),
            jnp.concatenate([kernel_re * incoming_re + kernel_im * incoming_im,
                             kernel_re * incoming_im - kernel_im * incoming_re], axis=1),
        ]
    results = inverse_rows(products, first_inv, second_inv, twiddle)
    for c in range(OWN):
        for offset, result in ((0, results[2 * c]), (OWN, results[2 * c + 1])):
            for h in range(ROWS // SIDE):
                sent[pl.ds(8 * h + offset + c, SEQ, stride=SEQ), :] = result[SEQ * h : SEQ * (h + 1), :]


def pair_channels(place):
    row = lax.broadcasted_iota(jnp.int32, (8, SIDE), 0)
    lane = lax.broadcasted_iota(jnp.int32, (8, SIDE), 1)
    return jnp.where(lane == place - place % 2 + row // OWN + SEQ * (row % OWN), 1.0, 0.0).astype(F32)


def backward_kernel(place, table, hidden, cosines, mine, other, sums, filter_mid, filter_out, grads, d2, d1, shaped,
                    features, sem):
    half = pl.ds(pl.multiple_of(HALF * (place() % 2), HALF), HALF)
    features_copy = pltpu.make_async_copy(table.at[:, half], features, sem)
    features_copy.start()
    weight3 = picked(filter_out, pair_channels(place())).astype(BF16)
    weight3 = jnp.concatenate([weight3[:64], weight3[:64], weight3[64:]], axis=1)
    weight2 = weight_left(filter_mid[...], 1)
    pieces = range(0, HALF, PIECE)
    for start in pieces:
        piece = pl.ds(start, PIECE)
        tiles = range(start // SIDE, (start + PIECE) // SIDE)
        both = jnp.concatenate(
            halves(jnp.concatenate([mine[pl.ds(8 * m, 8), :] + other[pl.ds(8 * m, 8), :] for m in tiles], axis=1))
        )
        shaped[:, piece] = both
        rows = jnp.concatenate([both, both[:8]])
        d2[:, piece] = jnp.concatenate(halves(dot(weight3, rows) * cosines[pl.ds(64, 64), piece]))
    for start in pieces:
        piece = pl.ds(start, PIECE)
        rows = d2[:, piece]
        d1[:, piece] = jnp.concatenate(
            halves(dot(weight2, jnp.concatenate([rows, rows[:64]])) * cosines[pl.ds(0, 64), piece])
        )
    features_copy.wait()
    left = jnp.concatenate([hidden[...], d1[...]])
    right = jnp.concatenate([d2[...], shaped[...], features[...]])
    total = dot_nt(left, right)
    mid = total[:64, :64] + (total[:64, 64:128] + total[64:128, :64])
    grads[pl.ds(0, 32), :] = jnp.concatenate([mid[:32], mid[32:]], axis=1)
    side = [jnp.concatenate([total[64 * k : 64 * (k + 1), 128:], jnp.zeros((64, 80), F32)], axis=1).T for k in range(2, 6)]
    first = side[2][16:32] + (side[2][32:48] + side[3][16:32])
    third = side[0][:8] + (side[0][8:16] + side[1][:8])
    grads[pl.ds(32, 8), :] = jnp.concatenate([first[:8], first[8:]], axis=1)
    channels = pair_channels(place())
    rates = jnp.sum(sums[pl.ds(0, 8), :], axis=1, keepdims=True)
    gains = jnp.sum(sums[pl.ds(8, 8), :], axis=1, keepdims=True)
    grads[pl.ds(40, 64), :] = dot_tn(third, channels, lax.Precision.HIGHEST)
    grads[pl.ds(104, 8), :] = jnp.concatenate([
        jnp.sum(channels * rates, axis=0, keepdims=True),
        jnp.sum(channels * gains, axis=0, keepdims=True),
        jnp.zeros((6, SIDE), F32),
    ])


def finish_kernel(total, grad_in, grad_mid, grad_out, grad_decay, grad_skip):
    grad_mid[pl.ds(0, 32), :] = total[:32, :ORDER]
    grad_mid[pl.ds(32, 32), :] = total[:32, ORDER:]
    grad_in[pl.ds(0, 8), :] = total[32:40, :ORDER]
    grad_in[pl.ds(8, 8), :] = total[32:40, ORDER:]
    grad_out[...] = total[40:104]
    grad_decay[...] = total[104:105]
    grad_skip[...] = total[105:106]


def seq_place():
    return lax.axis_index(SEQ_AXES)


def run_send(query, key, value, grad, **kw):
    return call(
        send_kernel, 1, [pl.BlockSpec(memory_space=pltpu.HBM)] * 4, spec((1024, SIDE)), out((1024, SIDE)),
        scratch=[pltpu.VMEM((4, ROWS, SIDE), BF16), pltpu.SemaphoreType.DMA((4,))], **kw,
    )(*[in_hbm(x) for x in (query, key, value, grad)])


def run_filter(features, filter_in, filter_mid, filter_out, place=seq_place, **kw):
    wide = lambda i: (0, i)
    return call(
        functools.partial(filter_kernel, place),
        HALF // STEP,
        [spec((32, STEP), lambda i: (0, i + HALF // STEP * (place() % 2))), spec((16, ORDER)), spec((ORDER, ORDER)), spec((ORDER, SIDE))],
        [spec((256, STEP), wide), spec((SIDE, STEP), wide)] + [spec((256, SIDE))] * 2,
        [pltpu.HBM((256, HALF), BF16), pltpu.HBM((SIDE, HALF), F32), out((256, SIDE)), out((256, SIDE))],
        scratch=[pltpu.VMEM((512, SIDE), F32)],
        flops=4 * 10**9, nbytes=10 * MIB, **kw,
    )(in_hbm(features), in_hbm(filter_in), in_hbm(filter_mid), in_hbm(filter_out))


def run_spectrum(mine, other, decay, place=seq_place, **kw):
    first_fwd, second_fwd, twiddle, _, _ = transform_tables()
    return call(
        functools.partial(spectrum_kernel, place),
        1,
        [spec((256, SIDE))] * 2 + [spec((1, SIDE)), spec((256, 384)), spec((768, 256)), spec((SIDE, 256))],
        spec((512, 256)),
        out((512, 256)),
        flops=10**9, nbytes=MIB, **kw,
    )(mine, other, decay, first_fwd, second_fwd, twiddle)


def run_correlate(field, mine, other, decay, place=seq_place, **kw):
    first_fwd, second_fwd, twiddle, second_inv, first_inv = transform_tables()
    return call(
        functools.partial(correlate_kernel, place),
        1,
        [spec((1024, SIDE)), spec((256, SIDE)), spec((256, SIDE)), spec((1, SIDE)),
         spec((256, 384)), spec((768, 256)), spec((SIDE, 256)), spec((768, 256)), spec((SIDE, 768))],
        [spec((1024, 256)), spec((512, SIDE)), spec((512, SIDE)), spec((16, SIDE))],
        [out((1024, 256)), out((512, SIDE)), out((512, SIDE)), out((16, SIDE))],
        flops=2 * 10**9, nbytes=4 * MIB, **kw,
    )(field, mine, other, decay, first_fwd, second_fwd, twiddle, second_inv, first_inv)


def run_convolve(spectra, spectrum, **kw):
    _, _, twiddle, second_inv, first_inv = transform_tables()
    return call(
        convolve_kernel,
        1,
        [spec((1024, 256)), spec((512, 256)), spec((SIDE, 256)), spec((768, 256)), spec((SIDE, 768))],
        spec((1024, SIDE)),
        out((1024, SIDE)),
        flops=2 * 10**9, nbytes=3 * MIB, **kw,
    )(spectra, spectrum, twiddle, second_inv, first_inv)


def run_backward(features, hidden, mine, other, sums, filter_mid, filter_out, place=seq_place, **kw):
    held = pl.BlockSpec(memory_space=pltpu.VMEM)
    return call(
        functools.partial(backward_kernel, place),
        1,
        [pl.BlockSpec(memory_space=pl.ANY)] + [held] * 5 + [spec((ORDER, ORDER)), spec((ORDER, SIDE))],
        spec((112, SIDE)),
        out((112, SIDE)),
        scratch=[pltpu.VMEM((SIDE, HALF), BF16)] * 2 + [pltpu.VMEM((16, HALF), BF16), pltpu.VMEM((32, HALF), BF16),
                                                        pltpu.SemaphoreType.DMA],
        flops=4 * 10**9, nbytes=10 * MIB, **kw,
    )(in_hbm(features), *hidden, mine, other, sums, in_hbm(filter_mid), in_hbm(filter_out))


def run_receive(query, key, value, grad, skip, field, **kw):
    block = spec((ROWS, SIDE))
    return call(receive_kernel, 1, [block] * 4 + [spec((1, SIDE)), spec((1024, SIDE))], [block] * 4,
                [out((ROWS, SIDE), BF16)] * 4, **kw)(query, key, value, grad, skip, field)


def run_finish(total, **kw):
    shapes = [(16, ORDER), (ORDER, ORDER), (ORDER, SIDE), (1, SIDE), (1, SIDE)]
    return call(finish_kernel, 1, [spec((112, SIDE))], [spec(s) for s in shapes], [out(s) for s in shapes], **kw)(
        total
    )


def exchanged(x, axis, distance):
    return lax.ppermute(x, axis, [(i, i ^ distance) for i in range(lax.axis_size(axis))])


def group_sum(x, axis, distances):
    values = [x] + [exchanged(x, axis, d) for d in distances]
    while len(values) > 1:
        values = [a + b for a, b in zip(values[::2], values[1::2])]
    return values[0]


def body(query, key, value, grad, filter_in, filter_mid, filter_out, decay_rate, skip_gain):
    decay = decay_rate.reshape(1, SIDE)
    skip = skip_gain.reshape(1, SIDE)
    features = jnp.asarray(feature_table())
    sent = run_send(query, key, value, grad)
    field = lax.all_to_all(sent.reshape(SEQ, SEQ, SIDE), SEQ_AXES, 0, 0, tiled=True).reshape(1024, SIDE)
    *hidden, mine, theirs = run_filter(features, filter_in, filter_mid, filter_out)
    other = exchanged(theirs, "core", 1)
    spectrum = run_spectrum(mine, other, decay)
    spectra, mine, theirs, sums = run_correlate(field, mine, other, decay)
    mine, spectrum = lax.optimization_barrier((mine, spectrum))
    grads = run_backward(features, hidden, mine, exchanged(theirs, "core", 1), sums, filter_mid, filter_out)
    grads, spectra = lax.optimization_barrier((grads, spectra))
    sent = run_convolve(spectra, spectrum)
    other = exchanged(grads, "core", 1)
    other, sent = lax.optimization_barrier((other, sent))
    grads = grads + other
    field = lax.all_to_all(sent.reshape(SEQ, SEQ, SIDE), SEQ_AXES, 0, 0, tiled=True).reshape(1024, SIDE)
    shared = group_sum(grads[:40], "chan", (1, 2, 3))
    shared = group_sum(shared, "chan", (6,))
    grads = jnp.concatenate([shared, grads[40:]])
    grads = group_sum(grads, "x", (1, 2, 3))
    grads, field = lax.optimization_barrier((grads, field))
    grads = group_sum(grads, "y", (1, 2, 3))
    output, grad_query, grad_key, grad_value = run_receive(query, key, value, grad, skip, field)
    grads, output = lax.optimization_barrier((grads, output))
    first, second, third, rates, gains = run_finish(grads)
    return (output, grad_query, grad_key, grad_value, first, second, third, rates.reshape(SIDE), gains.reshape(SIDE))


def solution(mesh):
    parts = Mesh(mesh.devices.reshape(4, 4, 2, 8), SEQ_AXES + ("chan",))
    wide = P(SEQ_AXES, "chan")
    return jax.shard_map(
        body,
        mesh=parts,
        in_specs=(wide, wide, wide, wide, P(), P(), P(None, "chan"), P("chan"), P("chan")),
        out_specs=(wide, wide, wide, wide, P(), P(), P(None, "chan"), P("chan"), P("chan")),
        check_vma=False,
    )
```
